32 devices in a mesh: inst: 8 (over y, x, core), tp: 4 (over z).
Axes of the slice: x: 2, y: 2, z: 4, core: 2. Of those that a mesh axis runs over, the one named last changes fastest.
Arguments:
- fresh_segment_probes: bfloat16 [2048, 64, 128], P('inst', 'tp'), may hold values from -10 to 10
- fresh_segment_pairs: bfloat16 [2048, 2, 8, 128], P('inst', None, 'tp'), may hold values from -5 to 5
- earlier_stored_pairs: bfloat16 [8192, 2, 8, 128], P('inst', None, 'tp'), may hold values from -5 to 5
- emitted_token_probe: bfloat16 [64, 128], P('tp'), may hold values from -10 to 10
- emitted_token_pair: bfloat16 [2, 8, 128], P(None, 'tp'), may hold values from -5 to 5
- final_projection_weights: bfloat16 [8192, 8192], P('tp', 'inst'), may hold values from -0.0625 to 0.0625
- remaining_instance_ids: int32 [4], replicated, may hold values from 0 to 7, as said below
- segment_destination_member: int32 [16, 1], replicated, may hold values from 0 to 3; in each aligned block of 16 rows (0 to 15, 16 to 31, ...) at most 8 rows name the same one
Outputs:
- span_hidden: bfloat16 [2048, 8192], P('inst', 'tp')
- migrated_cache: bfloat16 [8, 1024, 2, 8, 128], P('inst', None, None, 'tp')
- decode_attention: bfloat16 [64, 128], P('tp')
The draws below stay inside these ranges and needn't reach their ends.
Inputs may be any that keep to these rules, and one draw needn't show every extreme that they name: `segment_destination_member`: at most 8 blocks name one survivor, a bound that some block reaches. `remaining_instance_ids`: 4 distinct instance indices; instances 0 and 7 always survive.
All inputs are finite; a program needn't handle non-finite values.
Results may differ from the reference program's by a relative error of at most 0.024.
Values may be sent and summed in bfloat16 or wider, within the bound.
No kernel may reach another device: no remote copies, remote signals or barrier semaphores. Data moves between devices by JAX's collectives and lax.ppermute only.
A program may use at most 128 MiB of HBM per device.

```python
import math
import jax
import jax.numpy as jnp
import numpy as np
from jax import lax

D = 8192
HQ = 64
KVH = 8
HD = 128
BLK = 128
INSTANCES = 8
KVS = 8
SURV = 4
SPAN = 2048
PREFIX = 8192
NBLK = 16
CAP = 8
N_TP = 4


def drawn_parts(key):
    first = jax.random.randint(jax.random.fold_in(key, 102), (KVH,), 0, PREFIX)
    offset = jax.random.randint(jax.random.fold_in(key, 103), (KVH,), 1, PREFIX)
    second = (first + offset) % PREFIX
    chosen_rows = jax.random.randint(jax.random.fold_in(key, 104), (4,), 0, SPAN)
    return (first, second, chosen_rows)


def shared_direction(key):
    return jnp.clip(jax.random.normal(jax.random.fold_in(key, 201), (KVH, HD), jnp.float32), -3.0, 3.0)


def spread_slots(array, reduce_dimension):
    return jnp.repeat(array, KVS // KVH, axis=reduce_dimension)


def draw_earlier_stored_pairs(key, part):
    first, second, chosen_rows = drawn_parts(key)
    key = jax.random.fold_in(key, 1)
    base = jnp.clip(jax.random.normal(key, (PREFIX, 2, KVH, HD), jnp.float32), -5.0, 5.0)
    strength = 0.0
    positions = jnp.arange(PREFIX)[:, None]
    hit_first = (positions == first[None, :]).astype(jnp.float32)
    hit_second = (positions == second[None, :]).astype(jnp.float32)
    weight = jnp.minimum(hit_first + hit_second, 1.0)[..., None] * strength
    keys = base[:, 0] * (1.0 - weight)
    full = jnp.stack([keys, 0.5 * base[:, 1]], axis=1)
    return spread_slots(full, 2).astype(jnp.bfloat16)


def draw_fresh_segment_probes(key, part):
    first, second, chosen_rows = drawn_parts(key)
    key = jax.random.fold_in(key, 2)
    base = jnp.clip(2.5 * jax.random.normal(key, (SPAN, HQ, HD), jnp.float32), -10.0, 10.0)
    strength = 0.0
    hits = (jnp.arange(SPAN)[:, None] == chosen_rows[None, :]).astype(jnp.float32)
    weight = jnp.minimum(jnp.sum(hits, axis=1), 1.0)[:, None, None] * strength
    return (base * (1.0 - weight)).astype(jnp.bfloat16)


def draw_emitted_token_probe(key, part):
    common = shared_direction(key)
    key = jax.random.fold_in(key, 3)
    base = 2.5 * jax.random.normal(key, (HQ, HD), jnp.float32)
    strength = 0.0
    head_index = jnp.arange(HQ) * KVH // HQ
    base = jnp.clip(base + common[head_index], -10.0, 10.0)
    picks = jax.random.bernoulli(jax.random.fold_in(key, 31), 0.5, (HQ,)).astype(jnp.float32)
    weight = picks[:, None] * strength
    return (base * (1.0 - weight)).astype(jnp.bfloat16)


def draw_fresh_segment_pairs(key, part):
    key = jax.random.fold_in(key, 4)
    base = jnp.clip(jax.random.normal(key, (SPAN, 2, KVH, HD), jnp.float32), -5.0, 5.0)
    full = jnp.stack([base[:, 0], 0.5 * base[:, 1]], axis=1)
    return spread_slots(full, 2).astype(jnp.bfloat16)


def draw_emitted_token_pair(key, part):
    common = shared_direction(key)
    key = jax.random.fold_in(key, 5)
    values = jnp.clip(jax.random.normal(key, (KVH, HD), jnp.float32), -5.0, 5.0)
    base = jnp.stack([common, 0.5 * values], axis=0)
    return spread_slots(base, 1).astype(jnp.bfloat16)


def draw_remaining_instance_ids(key, part):
    key = jax.random.fold_in(key, 6)
    middle = jax.random.permutation(key, INSTANCES - 2)[:SURV - 2].astype(jnp.int32) + 1
    chosen = jnp.concatenate([jnp.array([0, INSTANCES - 1], jnp.int32), middle])
    order = jax.random.permutation(jax.random.fold_in(key, 61), SURV)
    return chosen[order].astype(jnp.int32)


def block_scale(key, dims, shards, least, top_value):
    def one(axis_at, shards_of):
        steps = jax.random.uniform(jax.random.fold_in(jax.random.fold_in(key, 6), axis_at), (shards_of,), jnp.float32, least / len(shards), top_value / len(shards))
        return jnp.repeat(jnp.exp(steps), dims[axis_at] // shards_of).reshape((-1,) + (1,) * (len(dims) - axis_at - 1))

    level = one(*shards[0])
    for cut in shards[1:]:
        level = level * one(*cut)
    return level


def routed_block(key, own, number, rows, number_of, top, bound, skew):
    order = jax.random.permutation(key, number_of)
    crowded, usual = load_shares(number_of, rows * top, bound, skew, True), load_shares(number_of, rows * top, bound, skew, False)
    places = jnp.arange(number_of)

    def named(tallies, offset_by):
        used = int((tallies > 0).sum())
        fixed = max(1, used // 4)
        passed = fixed + (places - fixed + offset_by * (used - fixed)) % max(1, number_of - fixed)
        return jnp.zeros((number_of,), jnp.int32).at[order[jnp.where(places < fixed, places, passed)]].set(jnp.asarray(tallies, jnp.int32))

    tallies = jnp.where(number % 4 == 0, named(crowded, number // 4), named(usual, number - number // 4 - 1))
    mixed = jax.random.permutation(jax.random.fold_in(own, 3), number_of)
    source_of, sink = mixed[0:number_of // 2 * 2:2], mixed[1:number_of // 2 * 2:2]
    margin = jnp.minimum(tallies[source_of] - 1, bound - tallies[sink]) // 2
    margin = jnp.where((source_of == order[0]) | (sink == order[0]) | (tallies[sink] == 0), 0, jnp.maximum(margin, 0))
    passed = jax.random.randint(jax.random.fold_in(own, 4), (number_of // 2,), 0, 1 << 20) % (margin + 1)
    tallies = tallies.at[source_of].add(-passed).at[sink].add(passed)
    members = jnp.searchsorted(jnp.cumsum(tallies), jnp.arange(rows * top), side="right").astype(jnp.int32)
    table = members.reshape(top, rows).T
    table = table[jax.random.permutation(jax.random.fold_in(own, 1), rows)]
    offset_by = jax.random.randint(jax.random.fold_in(own, 2), (rows, 1), 0, top)
    return jnp.take_along_axis(table, (jnp.arange(top)[None, :] + offset_by) % top, axis=1)


def load_shares(amount, total, bound, skew, full):
    weights = [(1 << 20) // math.isqrt(rank ** skew) + 1 for rank in range(1, amount + 1)]
    largest = bound if full else min(bound, max(-(-total // amount), total * weights[0] // sum(weights)))
    least = 1 if total - largest >= amount - 1 else 0
    counts, surplus = [largest] + [least] * (amount - 1), total - largest - least * (amount - 1)
    while surplus > 0:
        movable = [i for i in range(1, amount) if counts[i] < largest] or [i for i in range(1, amount) if counts[i] < bound]
        mass, budget = sum([weights[i] for i in movable]), surplus
        for i in movable:
            addition = min(bound - counts[i], max(1, budget * weights[i] // mass), surplus)
            counts[i] = counts[i] + addition
            surplus = surplus - addition
    return np.array(counts)


def scatter_about(own_key, shape, scale, bound, split=(), held_as=jnp.bfloat16):
    factor_of = block_scale(own_key, shape, split, -0.22, 0.18) if split else 1.0
    entries = jax.random.normal(own_key, shape, jnp.float32) * scale * factor_of
    return jnp.minimum(jnp.maximum(entries, -bound), bound).astype(held_as)


def setup_inputs(seed: int = 0) -> dict:
    splits = jax.random.split(jax.random.key(seed), 9)
    fresh_segment_probes = draw_fresh_segment_probes(jax.random.fold_in(splits[8], 71), 0)
    fresh_segment_pairs = draw_fresh_segment_pairs(jax.random.fold_in(splits[8], 71), 0)
    earlier_stored_pairs = draw_earlier_stored_pairs(jax.random.fold_in(splits[8], 71), 0)
    emitted_token_probe = draw_emitted_token_probe(jax.random.fold_in(splits[8], 71), 0)
    emitted_token_pair = draw_emitted_token_pair(jax.random.fold_in(splits[8], 71), 0)
    final_projection_weights = scatter_about(splits[5], (HQ * HD, D), (HQ * HD) ** -0.5, 0.0625, ((0, 4), (1, 8)))
    remaining_instance_ids = draw_remaining_instance_ids(jax.random.fold_in(splits[8], 71), 0)
    segment_destination_member_keys = jax.random.split(jax.random.fold_in(splits[7], 1), NBLK // NBLK)
    segment_destination_member_turns = jax.random.permutation(jax.random.fold_in(splits[7], 3), NBLK // NBLK)
    segment_destination_member = jax.vmap(lambda own, number: routed_block(jax.random.fold_in(splits[7], 2), own, number, NBLK, SURV, 1, CAP, 2))(segment_destination_member_keys, segment_destination_member_turns).reshape((NBLK, 1))
    return dict(fresh_segment_probes=fresh_segment_probes, fresh_segment_pairs=fresh_segment_pairs, earlier_stored_pairs=earlier_stored_pairs, emitted_token_probe=emitted_token_probe, emitted_token_pair=emitted_token_pair, final_projection_weights=final_projection_weights, remaining_instance_ids=remaining_instance_ids, segment_destination_member=segment_destination_member)


def rounded_weights(scores):
    highest = jnp.max(scores, axis=-1, keepdims=True)
    weights = jnp.exp(scores - highest)
    total = jnp.sum(weights, axis=-1)
    kept = lax.optimization_barrier(weights.astype(jnp.bfloat16)).astype(jnp.float32)
    return kept, total


def reference(fresh_segment_probes, fresh_segment_pairs, earlier_stored_pairs, emitted_token_probe, emitted_token_pair, final_projection_weights, remaining_instance_ids, segment_destination_member):
    scale = HD ** -0.5
    group = HQ // KVS
    keys_all = jnp.concatenate([earlier_stored_pairs, fresh_segment_pairs], axis=0)
    queries = fresh_segment_probes.reshape(SPAN, KVS, group, HD)
    rows_block = math.gcd(512, SPAN)
    block_count = SPAN // rows_block
    zero = jnp.zeros((), jnp.int32)
    key_positions = jnp.arange(PREFIX + SPAN, dtype=jnp.int32)

    def one_block(index):
        row_block = (index // KVS).astype(jnp.int32)
        slot = (index % KVS).astype(jnp.int32)
        start = (row_block * rows_block).astype(jnp.int32)
        query = lax.dynamic_slice(queries, (start, slot, zero, zero), (rows_block, 1, group, HD))[:, 0].astype(jnp.float32)
        pairs = lax.dynamic_index_in_dim(keys_all, slot, axis=2, keepdims=False)
        keys = pairs[:, 0].astype(jnp.float32)
        values = pairs[:, 1].astype(jnp.float32)
        scores = jnp.einsum("rgd,nd->rgn", query, keys) * scale
        row_positions = PREFIX + start + jnp.arange(rows_block, dtype=jnp.int32)
        visible = key_positions[None, :] <= row_positions[:, None]
        scores = jnp.where(visible[:, None, :], scores, -jnp.inf)
        kept, total = rounded_weights(scores)
        summed = jnp.einsum("rgn,nd->rgd", kept, values)
        return (summed / total[..., None]).astype(jnp.bfloat16)

    blocks = lax.map(one_block, jnp.arange(block_count * KVS, dtype=jnp.int32))
    blocks = blocks.reshape(block_count, KVS, rows_block, group, HD)
    attention = jnp.transpose(blocks, (0, 2, 1, 3, 4)).reshape(SPAN, HQ * HD)

    group_width = HQ * HD // N_TP

    def add_group(total, index):
        left = lax.dynamic_slice_in_dim(attention, (index * group_width).astype(jnp.int32), group_width, 1)
        right = lax.dynamic_slice_in_dim(final_projection_weights, (index * group_width).astype(jnp.int32), group_width, 0)
        part = jnp.dot(left, right, preferred_element_type=jnp.float32)
        part = lax.optimization_barrier(part.astype(jnp.bfloat16)).astype(jnp.float32)
        return total + part, None

    hidden_sum, unused = lax.scan(add_group, jnp.zeros((SPAN, D), jnp.float32), jnp.arange(N_TP, dtype=jnp.int32))
    span_hidden = hidden_sum.astype(jnp.bfloat16)

    destination_sequence = segment_destination_member[:, 0]
    destination_agreement = (destination_sequence[:, None] == jnp.arange(SURV, dtype=jnp.int32)[None, :]).astype(jnp.int32)
    slots = (jnp.sum(jnp.cumsum(destination_agreement, axis=0) * destination_agreement, axis=1) - 1).astype(jnp.int32)
    destination_members = remaining_instance_ids[destination_sequence].astype(jnp.int32)
    pieces = fresh_segment_pairs.reshape(NBLK, BLK, 2, KVS, HD)
    cache = jnp.zeros((INSTANCES, CAP, BLK, 2, KVS, HD), jnp.bfloat16).at[destination_members, slots].set(pieces)
    migrated_cache = cache.reshape(INSTANCES, CAP * BLK, 2, KVS, HD)

    every_key = jnp.concatenate([keys_all, emitted_token_pair[None]], axis=0).astype(jnp.float32)
    single = emitted_token_probe.reshape(KVS, group, HD).astype(jnp.float32)
    decode_scores = jnp.einsum("sgd,nsd->sgn", single, every_key[:, 0]) * scale
    kept, total = rounded_weights(decode_scores)
    summed = jnp.einsum("sgn,nsd->sgd", kept, every_key[:, 1])
    decode_attention = (summed / total[..., None]).astype(jnp.bfloat16).reshape(HQ, HD)
    return span_hidden, migrated_cache, decode_attention
```

```python
import functools

import jax
import jax.numpy as jnp
from jax import lax
from jax.experimental import pallas as pl
from jax.experimental.pallas import tpu as pltpu
from jax.sharding import PartitionSpec as P

BLK = 128
CAP = 8
NEG_FILL = -1e30
LOG2E = 1.4426950408889634
CHUNKS = 4
KEY_TILE = 1024


def from_behind(block, axis, distance):
    devices = range(lax.axis_size(axis))
    route = [((i - distance) % len(devices), i) for i in devices]
    return lax.ppermute(block, axis, route)


def combined_all(value, axis, combine):
    everything = jax.tree.map(lambda part: lax.all_gather(part, axis), value)
    initial = jax.tree.map(lambda part: part[0], everything)

    def turn(k, so_far):
        return combine(so_far, jax.tree.map(lambda part: part[k], everything))

    return lax.fori_loop(1, lax.axis_size(axis), turn, initial)


def attend(state, queries, key_value, visible):
    width = queries.shape[-1]
    scores = jnp.einsum(
        "rkgd,nkd->rkgn", queries, key_value[:, 0], preferred_element_type=jnp.float32
    ) * width ** (-0.5)
    if visible is not None:
        scores = jnp.where(visible[:, None, None, :], scores, NEG_FILL)
    running, total, weighted = state
    highest = jnp.maximum(running, jnp.max(scores, axis=-1))
    factor = jnp.exp(running - highest)
    weights = jnp.exp(scores - highest[..., None])
    total = total * factor + jnp.sum(weights, axis=-1)
    update = jnp.einsum(
        "rkgn,nkd->rkgd",
        weights.astype(jnp.bfloat16),
        key_value[:, 1],
        preferred_element_type=jnp.float32,
    )
    weighted = weighted * factor[..., None] + update
    return (highest, total, weighted)


def empty_state(rows, slots_local, group, width):
    return (
        jnp.full((rows, slots_local, group), -jnp.inf, jnp.float32),
        jnp.zeros((rows, slots_local, group), jnp.float32),
        jnp.zeros((rows, slots_local, group, width), jnp.float32),
    )


def combine(first, second):
    highest = jnp.maximum(first[0], second[0])
    left = jnp.exp(first[0] - highest)
    right = jnp.exp(second[0] - highest)
    return (
        highest,
        first[1] * left + second[1] * right,
        first[2] * left[..., None] + second[2] * right[..., None],
    )


def place_blocks(cache, rows_in, destination_members, slots, own_index):
    count = rows_in.shape[0] // BLK

    def put(index, current):
        spot = slots[index] * BLK
        incoming = lax.dynamic_slice_in_dim(rows_in, index * BLK, BLK, 0)
        present = lax.dynamic_slice_in_dim(current, spot, BLK, 0)
        chosen = jnp.where(destination_members[index] == own_index, incoming, present)
        return lax.dynamic_update_slice_in_dim(current, chosen, spot, 0)

    return lax.fori_loop(0, count, put, cache)


def destinations(segment_destination_member, remaining_instance_ids):
    sequence = segment_destination_member[:, 0]
    agreement = (
        sequence[:, None]
        == jnp.arange(remaining_instance_ids.shape[0], dtype=jnp.int32)[None, :]
    ).astype(jnp.int32)
    slots = jnp.sum(jnp.cumsum(agreement, axis=0) * agreement, axis=1) - 1
    members = jnp.sum(agreement * remaining_instance_ids[None, :], axis=1)
    return slots, members


def on_device_ring(
    fresh_segment_probes,
    fresh_segment_pairs,
    earlier_stored_pairs,
    emitted_token_probe,
    emitted_token_pair,
    final_projection_weights,
    remaining_instance_ids,
    segment_destination_member,
):
    own_index = lax.axis_index("inst")
    instances = lax.axis_size("inst")
    rows, heads, width = fresh_segment_probes.shape
    slots_local = fresh_segment_pairs.shape[2]
    group = heads // slots_local
    queries = fresh_segment_probes.reshape(rows, slots_local, group, width)
    slots, destination_members = destinations(segment_destination_member, remaining_instance_ids)
    held_blocks = jnp.sum((destination_members == own_index).astype(jnp.int32))
    cache = jnp.zeros((CAP * BLK, 2, slots_local, width), jnp.bfloat16)
    causal = jnp.arange(rows)[:, None] >= jnp.arange(rows)[None, :]
    state = attend(
        empty_state(rows, slots_local, group, width), queries, earlier_stored_pairs, None
    )
    state = attend(state, queries, fresh_segment_pairs, causal)
    moving = jnp.concatenate([fresh_segment_pairs, earlier_stored_pairs], axis=0)

    def turn_both(step, carry):
        moving, state, current = carry
        moving = from_behind(moving, "inst", 1)
        source = (own_index - step) % instances
        state = attend(state, queries, moving[rows:], None)
        visible = jnp.broadcast_to(source < own_index, (rows, rows))
        state = attend(state, queries, moving[:rows], visible)
        return (moving, state, current)

    moving, state, cache = lax.fori_loop(1, instances, turn_both, (moving, state, cache))
    cache = place_blocks(
        cache,
        lax.all_gather(fresh_segment_pairs, "inst", axis=0, tiled=True),
        destination_members,
        slots,
        own_index,
    )
    attention = (state[2] / state[1][..., None]).astype(jnp.bfloat16).reshape(rows, heads * width)
    terms = jnp.dot(
        attention,
        lax.all_gather(final_projection_weights, "inst", axis=1, tiled=True),
        preferred_element_type=jnp.float32,
    )
    span_hidden = lax.psum_scatter(
        terms.astype(jnp.bfloat16), "tp", scatter_dimension=1, tiled=True
    )
    single = emitted_token_probe.reshape(1, slots_local, group, width)
    decode_state = attend(
        empty_state(1, slots_local, group, width), single, earlier_stored_pairs, None
    )
    live = (jnp.arange(CAP * BLK) < held_blocks * BLK)[None, :]
    decode_state = attend(decode_state, single, cache, live)
    merged = combined_all((decode_state[0], decode_state[1], decode_state[2]), "inst", combine)
    own_scores = jnp.einsum(
        "rkgd,kd->rkg", single, emitted_token_pair[0], preferred_element_type=jnp.float32
    ) * width ** (-0.5)
    highest = jnp.maximum(merged[0], own_scores)
    left = jnp.exp(merged[0] - highest)
    right = jnp.exp(own_scores - highest)
    total = merged[1] * left + right
    own_weight = lax.optimization_barrier(right.astype(jnp.bfloat16)).astype(jnp.float32)
    own_value = emitted_token_pair[1].astype(jnp.float32)
    weighted = merged[2] * left[..., None] + own_weight[..., None] * own_value[None, :, None, :]
    decode_attention = (weighted / total[..., None]).astype(jnp.bfloat16).reshape(heads, width)
    return (span_hidden, cache[None], decode_attention)


def swapped(value, axis, distance):
    size = lax.axis_size(axis)
    return lax.ppermute(value, axis, [(i, i ^ distance) for i in range(size)])


def attention_kernel(
    chunk, chunk_rows, rows, group, scale, ids, q_ref, *refs
):
    pieces = refs[:8]
    out_ref = refs[8]
    keys, values, fresh_keys, fresh_values, sems = refs[9:]
    width = q_ref.shape[-1]
    prefix_rows = pieces[0].shape[0] - rows
    copies = []
    for p in range(8):
        block = pl.multiple_of(ids[p] * rows, rows)
        at = p * prefix_rows
        copies.append([
            pltpu.make_async_copy(
                pieces[p].at[pl.ds(rows, prefix_rows), pl.ds(0, width)],
                keys.at[pl.ds(at, prefix_rows)],
                sems.at[p, 0],
            ),
            pltpu.make_async_copy(
                pieces[p].at[pl.ds(rows, prefix_rows), pl.ds(width, width)],
                values.at[pl.ds(at, prefix_rows), pl.ds(0, width)],
                sems.at[p, 1],
            ),
            pltpu.make_async_copy(
                pieces[p].at[pl.ds(0, rows), pl.ds(0, width)],
                fresh_keys.at[pl.ds(block, rows)],
                sems.at[p, 2],
            ),
            pltpu.make_async_copy(
                pieces[p].at[pl.ds(0, rows), pl.ds(width, width)],
                fresh_values.at[pl.ds(block, rows), pl.ds(0, width)],
                sems.at[p, 3],
            ),
        ])
        for copy in copies[-1]:
            copy.start()
    values[:, width:] = jnp.ones((8 * prefix_rows, width), jnp.bfloat16)
    fresh_values[:, width:] = jnp.ones((8 * rows, width), jnp.bfloat16)
    for p in range(8):
        for copy in copies[p]:
            copy.wait()

    tile_rows = q_ref.shape[1]

    def step(q, k, v, visible, state):
        running, weighted = state
        scores = lax.dot_general(
            q, k, (((1,), (1,)), ((), ())), preferred_element_type=jnp.float32
        )
        if visible is not None:
            scores = jnp.where(visible, scores, NEG_FILL)
        highest = jnp.maximum(running, jnp.max(scores, axis=1, keepdims=True))
        weights = jnp.exp2((scores - highest) * scale).astype(jnp.bfloat16)
        factor = jnp.exp2((running - highest) * scale)
        update = jnp.dot(weights, v, preferred_element_type=jnp.float32)
        return (highest, weighted * factor + update)

    queries = [q_ref[0], q_ref[1]]
    empty = (
        jnp.full((tile_rows, 1), -jnp.inf, jnp.float32),
        jnp.zeros((tile_rows, 2 * width), jnp.float32),
    )

    def prefix_step(t, states):
        at = pl.multiple_of(t * KEY_TILE, KEY_TILE)
        k = keys[pl.ds(at, KEY_TILE), :]
        v = values[pl.ds(at, KEY_TILE), :]
        return tuple(step(queries[h], k, v, None, states[h]) for h in range(2))

    states = lax.fori_loop(0, 8 * prefix_rows // KEY_TILE, prefix_step, (empty, empty))
    token = lax.broadcasted_iota(jnp.int32, (tile_rows, rows), 0) % chunk_rows + chunk * chunk_rows
    visible = lax.broadcasted_iota(jnp.int32, (tile_rows, rows), 1) <= token
    for h in range(2):
        block = ids[8 + h]

        def fresh_step(t, state):
            at = pl.multiple_of(t * rows, rows)
            k = fresh_keys[pl.ds(at, rows), :]
            v = fresh_values[pl.ds(at, rows), :]
            return step(queries[h], k, v, None, state)

        state = lax.fori_loop(0, block, fresh_step, states[h])
        at = pl.multiple_of(block * rows, rows)
        _, weighted = step(
            queries[h], fresh_keys[pl.ds(at, rows), :], fresh_values[pl.ds(at, rows), :], visible, state
        )
        result = (weighted[:, :width] / weighted[:, width:]).astype(jnp.bfloat16)
        for g in range(group):
            out_ref[h, :, g * width : (g + 1) * width] = result[
                g * chunk_rows : (g + 1) * chunk_rows
            ]


def chunk_attention(chunk, ids, queries, pieces, rows, group):
    _, tile_rows, width = queries.shape
    chunk_rows = tile_rows // group
    held = pieces[0].shape[0]
    prefix_rows = held - rows
    return pl.pallas_call(
        functools.partial(
            attention_kernel, chunk, chunk_rows, rows, group, width ** (-0.5) * LOG2E
        ),
        out_shape=jax.ShapeDtypeStruct((2, chunk_rows, group * width), jnp.bfloat16),
        in_specs=[pl.BlockSpec(memory_space=pltpu.SMEM), pl.BlockSpec(memory_space=pltpu.VMEM)]
        + [pl.BlockSpec(memory_space=pl.ANY)] * 8,
        out_specs=pl.BlockSpec(memory_space=pltpu.VMEM),
        scratch_shapes=[
            pltpu.VMEM((8 * prefix_rows, width), jnp.bfloat16),
            pltpu.VMEM((8 * prefix_rows, 2 * width), jnp.bfloat16),
            pltpu.VMEM((8 * rows, width), jnp.bfloat16),
            pltpu.VMEM((8 * rows, 2 * width), jnp.bfloat16),
            pltpu.SemaphoreType.DMA((8, 4)),
        ],
        compiler_params=pltpu.CompilerParams(vmem_limit_bytes=48 * 1024 * 1024),
        cost_estimate=pl.CostEstimate(
            flops=2 * 2 * 2 * tile_rows * 8 * held * width * 2,
            bytes_accessed=8 * held * width * 4,
            transcendentals=2 * tile_rows * 8 * held,
        ),
        name="chunk_attention",
    )(ids, queries, *pieces)


def decode_kernel(scale, q_ref, last_ref, *refs):
    pieces, out_ref = refs[:8], refs[8]
    width = q_ref.shape[-1]
    q = q_ref[...]
    last = last_ref[...].astype(jnp.float32)
    running = jnp.sum(q.astype(jnp.float32) * last[0:1], axis=1, keepdims=True)
    total = jnp.ones_like(running)
    weighted = jnp.broadcast_to(last[1:2], (q.shape[0], width))
    for piece in pieces:
        scores = lax.dot_general(
            q, piece[:, :width], (((1,), (1,)), ((), ())), preferred_element_type=jnp.float32
        )
        highest = jnp.maximum(running, jnp.max(scores, axis=1, keepdims=True))
        weights = jnp.exp2((scores - highest) * scale)
        factor = jnp.exp2((running - highest) * scale)
        total = total * factor + jnp.sum(weights, axis=1, keepdims=True)
        weighted = weighted * factor + jnp.dot(
            weights.astype(jnp.bfloat16), piece[:, width:], preferred_element_type=jnp.float32
        )
        running = highest
    out_ref[...] = (weighted / total).astype(jnp.bfloat16)


def decode(query, last, pieces):
    group, width = query.shape
    padded = jnp.pad(query, ((0, -group % 16), (0, 0)))
    out = pl.pallas_call(
        functools.partial(decode_kernel, width ** (-0.5) * LOG2E),
        out_shape=jax.ShapeDtypeStruct(padded.shape, jnp.bfloat16),
        compiler_params=pltpu.CompilerParams(vmem_limit_bytes=32 * 1024 * 1024),
        cost_estimate=pl.CostEstimate(
            flops=4 * padded.shape[0] * width * 8 * pieces[0].shape[0],
            bytes_accessed=8 * pieces[0].shape[0] * width * 4,
            transcendentals=padded.shape[0] * 8 * pieces[0].shape[0],
        ),
        name="decode",
    )(padded, last, *pieces)
    return out[:group]


def pick_kernel(places, held, block_ref, out_ref):
    keep = held[pl.program_id(0)] > 0
    out_ref[...] = jnp.where(keep, block_ref[...], jnp.zeros_like(block_ref))


def pick_blocks(places, held, blocks):
    _, rows, width = blocks.shape
    count = places.shape[0]
    return pl.pallas_call(
        pick_kernel,
        grid_spec=pltpu.PrefetchScalarGridSpec(
            num_scalar_prefetch=2,
            grid=(count,),
            in_specs=[pl.BlockSpec((1, rows, width), lambda s, places, held: (places[s], 0, 0))],
            out_specs=pl.BlockSpec((1, rows, width), lambda s, places, held: (s, 0, 0)),
        ),
        out_shape=jax.ShapeDtypeStruct((count, rows, width), blocks.dtype),
        name="pick_blocks",
    )(places, held, blocks)


def project_kernel(slot, own, beside, across, corner, *refs):
    weights, outs = refs[:4], refs[4:]
    same = jnp.concatenate([own[0], own[1], across[0], across[1]], axis=0)
    other = jnp.concatenate([beside[1], beside[0], corner[1], corner[0]], axis=0)
    rows = own.shape[1]
    for half in range(2):
        total = jnp.dot(same, weights[2 * half][...], preferred_element_type=jnp.float32)
        total += jnp.dot(other, weights[2 * half + 1][...], preferred_element_type=jnp.float32)
        total = total.astype(jnp.bfloat16)
        for r in range(4):
            outs[r][half] = total[r * rows : (r + 1) * rows]


def project(slot, parts, own_weights, sibling_weights):
    _, rows, depth = parts[0].shape
    columns = own_weights.shape[1]
    tile = min(512, columns)
    whole = pl.BlockSpec((2, rows, depth), lambda j, slot: (0, 0, 0))
    same = pl.BlockSpec((depth, tile), lambda j, slot: (slot[0], j))
    other = pl.BlockSpec((depth, tile), lambda j, slot: (1 - slot[0], j))
    out = pl.BlockSpec((2, rows, tile), lambda j, slot: (0, 0, j))
    return pl.pallas_call(
        project_kernel,
        grid_spec=pltpu.PrefetchScalarGridSpec(
            num_scalar_prefetch=1,
            grid=(columns // tile,),
            in_specs=[whole] * 4 + [same, other] * 2,
            out_specs=[out] * 4,
        ),
        out_shape=[jax.ShapeDtypeStruct((2, rows, columns), jnp.bfloat16)] * 4,
        compiler_params=pltpu.CompilerParams(vmem_limit_bytes=48 * 1024 * 1024),
        cost_estimate=pl.CostEstimate(
            flops=2 * 4 * rows * 2 * depth * 2 * columns,
            bytes_accessed=2 * depth * 2 * columns * 2,
            transcendentals=0,
        ),
        name="project",
    )(slot, *parts, own_weights, own_weights, sibling_weights, sibling_weights)


def on_device_planes(
    fresh_segment_probes,
    fresh_segment_pairs,
    earlier_stored_pairs,
    emitted_token_probe,
    emitted_token_pair,
    final_projection_weights,
    remaining_instance_ids,
    segment_destination_member,
):
    me = lax.axis_index("inst")
    plane = lax.axis_index("tp")
    slot = me // 4
    core = me % 2
    rows, heads, width = fresh_segment_probes.shape
    group = heads // 2
    chunk_rows = rows // CHUNKS

    def one_slot(s):
        return jnp.concatenate(
            [
                lax.dynamic_index_in_dim(part, s, axis=2, keepdims=False).reshape(-1, 2 * width)
                for part in (fresh_segment_pairs, earlier_stored_pairs)
            ],
            axis=0,
        )

    def one_slot_queries(s):
        mine = lax.dynamic_slice_in_dim(fresh_segment_probes, s * group, group, 1)
        mine = mine.reshape(CHUNKS, chunk_rows, group, width)
        return mine.transpose(0, 2, 1, 3).reshape(CHUNKS, group * chunk_rows, width)

    piece = {0: one_slot(slot)}
    piece[4] = swapped(one_slot(1 - slot), "inst", 4)
    piece[2] = swapped(piece[0], "inst", 2)
    queries_own = one_slot_queries(slot)
    queries_beside = swapped(one_slot_queries(1 - slot), "inst", 4)
    piece[6] = swapped(piece[4], "inst", 2)
    for d in (0, 4, 2, 6):
        piece[d + 1] = swapped(piece[d], "inst", 1)
    pieces = [piece[d] for d in range(8)]
    sibling_weights = swapped(final_projection_weights, "inst", 1)
    ids = jnp.stack([me ^ d for d in range(8)] + [me, me ^ 4]).astype(jnp.int32)
    slot_array = jnp.reshape(slot, (1,)).astype(jnp.int32)

    offset = plane ^ (me // 2)
    low, high = offset % 2 == 0, offset // 2 % 2 == 0
    hidden = []
    for chunk in range(CHUNKS):
        queries = jnp.stack([queries_own[chunk], queries_beside[chunk]])
        own = chunk_attention(chunk, ids, queries, pieces, rows, group)
        parts = [own] + [swapped(own, "inst", d) for d in (4, 2, 6)]
        here, beside, across, corner = project(
            slot_array, parts, final_projection_weights, sibling_weights
        )
        beside, across, corner = (
            swapped(value, "inst", d) for value, d in ((beside, 4), (across, 2), (corner, 6))
        )
        keep = jnp.stack([jnp.where(low, here, across), jnp.where(low, beside, corner)])
        send = jnp.stack([jnp.where(low, across, here), jnp.where(low, corner, beside)])
        total = keep.astype(jnp.float32) + swapped(send, "tp", 1).astype(jnp.float32)
        keep = jnp.where(high, total[0], total[1])
        send = jnp.where(high, total[1], total[0]).astype(jnp.bfloat16)
        final = (keep + swapped(send, "tp", 2).astype(jnp.float32)).astype(jnp.bfloat16)
        first = jnp.where(core == 0, final[0], final[1])
        second = jnp.where(core == 0, final[1], final[0])
        hidden.append(jnp.concatenate([first, second], axis=1))
    span_hidden = jnp.concatenate(hidden, axis=0)

    slots, members = destinations(segment_destination_member, remaining_instance_ids)
    per_piece = rows // BLK

    def wanted(owner):
        match = (members[:, None] == owner) & (
            slots[:, None] == jnp.arange(CAP, dtype=jnp.int32)[None, :]
        )
        numbers = jnp.arange(members.shape[0], dtype=jnp.int32)[:, None]
        block = jnp.sum(jnp.where(match, numbers, 0), axis=0)
        place = ((block // per_piece) ^ me) * per_piece + block % per_piece
        return place.astype(jnp.int32), jnp.any(match, axis=0).astype(jnp.int32)

    blocks = jnp.concatenate([p[:rows] for p in pieces], axis=0).reshape(-1, BLK, 2 * width)
    picked_own = pick_blocks(*wanted(me), blocks)
    picked_beside = swapped(pick_blocks(*wanted(me ^ 4), blocks), "inst", 4)
    picked_own = picked_own.reshape(CAP * BLK, 2, width)
    picked_beside = picked_beside.reshape(CAP * BLK, 2, width)
    cache = jnp.stack(
        [
            jnp.where(slot == 0, picked_own, picked_beside),
            jnp.where(slot == 0, picked_beside, picked_own),
        ],
        axis=2,
    )

    single = lax.dynamic_slice_in_dim(emitted_token_probe, slot * group, group, 0)
    last = lax.dynamic_index_in_dim(emitted_token_pair, slot, axis=1, keepdims=False)
    decoded = decode(single, last, pieces)
    decoded_beside = swapped(decoded, "inst", 4)
    decode_attention = jnp.concatenate(
        [
            jnp.where(slot == 0, decoded, decoded_beside),
            jnp.where(slot == 0, decoded_beside, decoded),
        ],
        axis=0,
    )
    return (span_hidden, cache[None], decode_attention)


def solution(mesh):
    instances, groups = mesh.shape["inst"], mesh.shape["tp"]

    def on_device(*arguments):
        slots_local = arguments[1].shape[2]
        if instances == 8 and groups == 4 and slots_local == 2:
            return on_device_planes(*arguments)
        return on_device_ring(*arguments)

    return jax.shard_map(
        on_device,
        mesh=mesh,
        in_specs=(
            P("inst", "tp", None),
            P("inst", None, "tp", None),
            P("inst", None, "tp", None),
            P("tp", None),
            P(None, "tp", None),
            P("tp", "inst"),
            P(),
            P(),
        ),
        out_specs=(P("inst", "tp"), P("inst", None, None, "tp", None), P("tp", None)),
        check_vma=False,
    )
```

```python
import functools

import jax
import jax.numpy as jnp
from jax import lax
from jax.experimental import pallas as pl
from jax.experimental.pallas import tpu as pltpu
from jax.sharding import PartitionSpec as P

BLK = 128
CAP = 8
NEG_FILL = -1e30
LOG2E = 1.4426950408889634
CHUNKS = 4


def from_behind(block, axis, distance):
    devices = range(lax.axis_size(axis))
    route = [((i - distance) % len(devices), i) for i in devices]
    return lax.ppermute(block, axis, route)


def combined_all(value, axis, combine):
    everything = jax.tree.map(lambda part: lax.all_gather(part, axis), value)
    initial = jax.tree.map(lambda part: part[0], everything)

    def turn(k, so_far):
        return combine(so_far, jax.tree.map(lambda part: part[k], everything))

    return lax.fori_loop(1, lax.axis_size(axis), turn, initial)


def attend(state, queries, key_value, visible):
    width = queries.shape[-1]
    scores = jnp.einsum(
        "rkgd,nkd->rkgn", queries, key_value[:, 0], preferred_element_type=jnp.float32
    ) * width ** (-0.5)
    if visible is not None:
        scores = jnp.where(visible[:, None, None, :], scores, NEG_FILL)
    running, total, weighted = state
    highest = jnp.maximum(running, jnp.max(scores, axis=-1))
    factor = jnp.exp(running - highest)
    weights = jnp.exp(scores - highest[..., None])
    total = total * factor + jnp.sum(weights, axis=-1)
    update = jnp.einsum(
        "rkgn,nkd->rkgd",
        weights.astype(jnp.bfloat16),
        key_value[:, 1],
        preferred_element_type=jnp.float32,
    )
    weighted = weighted * factor[..., None] + update
    return (highest, total, weighted)


def empty_state(rows, slots_local, group, width):
    return (
        jnp.full((rows, slots_local, group), -jnp.inf, jnp.float32),
        jnp.zeros((rows, slots_local, group), jnp.float32),
        jnp.zeros((rows, slots_local, group, width), jnp.float32),
    )


def combine(first, second):
    highest = jnp.maximum(first[0], second[0])
    left = jnp.exp(first[0] - highest)
    right = jnp.exp(second[0] - highest)
    return (
        highest,
        first[1] * left + second[1] * right,
        first[2] * left[..., None] + second[2] * right[..., None],
    )


def place_blocks(cache, rows_in, destination_members, slots, own_index):
    count = rows_in.shape[0] // BLK

    def put(index, current):
        spot = slots[index] * BLK
        incoming = lax.dynamic_slice_in_dim(rows_in, index * BLK, BLK, 0)
        present = lax.dynamic_slice_in_dim(current, spot, BLK, 0)
        chosen = jnp.where(destination_members[index] == own_index, incoming, present)
        return lax.dynamic_update_slice_in_dim(current, chosen, spot, 0)

    return lax.fori_loop(0, count, put, cache)


def destinations(segment_destination_member, remaining_instance_ids):
    sequence = segment_destination_member[:, 0]
    agreement = (
        sequence[:, None]
        == jnp.arange(remaining_instance_ids.shape[0], dtype=jnp.int32)[None, :]
    ).astype(jnp.int32)
    slots = jnp.sum(jnp.cumsum(agreement, axis=0) * agreement, axis=1) - 1
    members = jnp.sum(agreement * remaining_instance_ids[None, :], axis=1)
    return slots, members


def on_device_ring(
    fresh_segment_probes,
    fresh_segment_pairs,
    earlier_stored_pairs,
    emitted_token_probe,
    emitted_token_pair,
    final_projection_weights,
    remaining_instance_ids,
    segment_destination_member,
):
    own_index = lax.axis_index("inst")
    instances = lax.axis_size("inst")
    rows, heads, width = fresh_segment_probes.shape
    slots_local = fresh_segment_pairs.shape[2]
    group = heads // slots_local
    queries = fresh_segment_probes.reshape(rows, slots_local, group, width)
    slots, destination_members = destinations(segment_destination_member, remaining_instance_ids)
    held_blocks = jnp.sum((destination_members == own_index).astype(jnp.int32))
    cache = jnp.zeros((CAP * BLK, 2, slots_local, width), jnp.bfloat16)
    causal = jnp.arange(rows)[:, None] >= jnp.arange(rows)[None, :]
    state = attend(
        empty_state(rows, slots_local, group, width), queries, earlier_stored_pairs, None
    )
    state = attend(state, queries, fresh_segment_pairs, causal)
    moving = jnp.concatenate([fresh_segment_pairs, earlier_stored_pairs], axis=0)

    def turn_both(step, carry):
        moving, state, current = carry
        moving = from_behind(moving, "inst", 1)
        source = (own_index - step) % instances
        state = attend(state, queries, moving[rows:], None)
        visible = jnp.broadcast_to(source < own_index, (rows, rows))
        state = attend(state, queries, moving[:rows], visible)
        return (moving, state, current)

    moving, state, cache = lax.fori_loop(1, instances, turn_both, (moving, state, cache))
    cache = place_blocks(
        cache,
        lax.all_gather(fresh_segment_pairs, "inst", axis=0, tiled=True),
        destination_members,
        slots,
        own_index,
    )
    attention = (state[2] / state[1][..., None]).astype(jnp.bfloat16).reshape(rows, heads * width)
    terms = jnp.dot(
        attention,
        lax.all_gather(final_projection_weights, "inst", axis=1, tiled=True),
        preferred_element_type=jnp.float32,
    )
    span_hidden = lax.psum_scatter(
        terms.astype(jnp.bfloat16), "tp", scatter_dimension=1, tiled=True
    )
    single = emitted_token_probe.reshape(1, slots_local, group, width)
    decode_state = attend(
        empty_state(1, slots_local, group, width), single, earlier_stored_pairs, None
    )
    live = (jnp.arange(CAP * BLK) < held_blocks * BLK)[None, :]
    decode_state = attend(decode_state, single, cache, live)
    merged = combined_all((decode_state[0], decode_state[1], decode_state[2]), "inst", combine)
    own_scores = jnp.einsum(
        "rkgd,kd->rkg", single, emitted_token_pair[0], preferred_element_type=jnp.float32
    ) * width ** (-0.5)
    highest = jnp.maximum(merged[0], own_scores)
    left = jnp.exp(merged[0] - highest)
    right = jnp.exp(own_scores - highest)
    total = merged[1] * left + right
    own_weight = lax.optimization_barrier(right.astype(jnp.bfloat16)).astype(jnp.float32)
    own_value = emitted_token_pair[1].astype(jnp.float32)
    weighted = merged[2] * left[..., None] + own_weight[..., None] * own_value[None, :, None, :]
    decode_attention = (weighted / total[..., None]).astype(jnp.bfloat16).reshape(heads, width)
    return (span_hidden, cache[None], decode_attention)


def swapped(value, axis, distance):
    size = lax.axis_size(axis)
    return lax.ppermute(value, axis, [(i, i ^ distance) for i in range(size)])


def vmem(count=1):
    return [pl.BlockSpec(memory_space=pltpu.VMEM)] * count


def smem(count=1):
    return [pl.BlockSpec(memory_space=pltpu.SMEM)] * count


def anywhere(count=1):
    return [pl.BlockSpec(memory_space=pl.ANY)] * count


def split_pairs_kernel(me, fresh, prefix, own_ref, send_ref):
    rows = fresh.shape[0]

    def place(out, s):
        for j in range(2):
            out[j, :rows] = fresh[:, j, s, :]
            out[j, rows:] = prefix[:, j, s, :]

    @pl.when(me[0] < 4)
    def _():
        place(own_ref, 0)
        place(send_ref, 1)

    @pl.when(me[0] >= 4)
    def _():
        place(own_ref, 1)
        place(send_ref, 0)


def split_pairs(me, fresh, prefix):
    held = fresh.shape[0] + prefix.shape[0]
    shape = jax.ShapeDtypeStruct((2, held, fresh.shape[3]), jnp.bfloat16)
    return pl.pallas_call(
        split_pairs_kernel,
        out_shape=[shape, shape],
        in_specs=smem() + vmem(2),
        out_specs=vmem(2),
        compiler_params=pltpu.CompilerParams(vmem_limit_bytes=32 * 1024 * 1024),
        name="split_pairs",
    )(me, fresh, prefix)


def split_queries_kernel(chunk_rows, group, me, queries, own_ref, send_ref):
    def place(out, s):
        for k in range(CHUNKS):
            for g in range(group):
                out[k, g * chunk_rows : (g + 1) * chunk_rows] = queries[
                    k * chunk_rows : (k + 1) * chunk_rows, s * group + g, :
                ]

    @pl.when(me[0] < 4)
    def _():
        place(own_ref, 0)
        place(send_ref, 1)

    @pl.when(me[0] >= 4)
    def _():
        place(own_ref, 1)
        place(send_ref, 0)


def split_queries(me, queries):
    rows, heads, width = queries.shape
    group = heads // 2
    shape = jax.ShapeDtypeStruct((CHUNKS, group * rows // CHUNKS, width), jnp.bfloat16)
    return pl.pallas_call(
        functools.partial(split_queries_kernel, rows // CHUNKS, group),
        out_shape=[shape, shape],
        in_specs=smem() + vmem(),
        out_specs=vmem(2),
        compiler_params=pltpu.CompilerParams(vmem_limit_bytes=32 * 1024 * 1024),
        name="split_queries",
    )(me, queries)


def attention_kernel(waits, chunk_start, chunk_rows, rows, group, scale, me, *refs):
    q_refs = refs[:2]
    pieces = refs[2:10]
    out_ref = refs[10 + waits]
    keys, values, fresh_keys, fresh_values, scores, weights, peaks, running, weighted, sems = refs[
        11 + waits :
    ]
    _, tile_rows, width = q_refs[0].shape
    held = pieces[0].shape[1]
    prefix_rows = held - rows
    part = min(256, prefix_rows)
    blocks = (me[0], me[0] ^ 4)

    def prefix_copies(p, piece):
        at = pl.multiple_of(p * prefix_rows, prefix_rows)
        return [
            pltpu.make_async_copy(
                piece.at[0, pl.ds(rows, prefix_rows)],
                keys.at[pl.ds(at, prefix_rows)],
                sems.at[p, 0],
            ),
            pltpu.make_async_copy(
                piece.at[1, pl.ds(rows, prefix_rows)],
                values.at[pl.ds(at, prefix_rows), pl.ds(0, width)],
                sems.at[p, 1],
            ),
        ]

    def fresh_copies(p, piece):
        at = pl.multiple_of((me[0] ^ p) * rows, rows)
        return [
            pltpu.make_async_copy(
                piece.at[0, pl.ds(0, rows)], fresh_keys.at[pl.ds(at, rows)], sems.at[p, 2]
            ),
            pltpu.make_async_copy(
                piece.at[1, pl.ds(0, rows)],
                fresh_values.at[pl.ds(at, rows), pl.ds(0, width)],
                sems.at[p, 3],
            ),
        ]

    for p in range(8):
        for copy in prefix_copies(p, pieces[p]):
            copy.start()
    for p in range(8):
        for copy in fresh_copies(p, pieces[p]):
            copy.start()
    values[:, width:] = jnp.ones((8 * prefix_rows, width), jnp.bfloat16)
    fresh_values[:, width:] = jnp.ones((8 * rows, width), jnp.bfloat16)
    running[...] = jnp.full(running.shape, -jnp.inf, jnp.float32)
    weighted[...] = jnp.zeros(weighted.shape, jnp.float32)

    def dotted(q, k):
        return lax.dot_general(q, k, (((1,), (1,)), ((), ())), preferred_element_type=jnp.float32)

    def wait_for(p):
        for copy in prefix_copies(p, pieces[0]):
            copy.wait()

    def score_part(slot, t, h, j, peak):
        at = pl.multiple_of(t * prefix_rows + j * part, part)
        value = dotted(q_refs[h][0], keys[pl.ds(at, part), :])
        scores[slot, h, :, j * part : (j + 1) * part] = value
        for l in range(0, part, width):
            block = value[:, l : l + width]
            peak = block if peak is None else jnp.maximum(peak, block)
        return peak

    def prefix_step(t, slot, following):
        for h in range(2):
            before = running[h]
            now = jnp.maximum(before, jnp.max(peaks[slot, h], axis=1, keepdims=True))
            running[h] = now
            peak = None
            for j in range(prefix_rows // part):
                if following:
                    peak = score_part(1 - slot, t + 1, h, j, peak)
                for l in range(j * part, (j + 1) * part, width):
                    weights[h, :, l : l + width] = jnp.exp2(
                        (scores[slot, h, :, l : l + width] - now) * scale
                    ).astype(jnp.bfloat16)
            if following:
                peaks[1 - slot, h] = peak
            factor = jnp.exp2((before - now) * scale)
            at = pl.multiple_of(t * prefix_rows, prefix_rows)
            update = jnp.dot(
                weights[h], values[pl.ds(at, prefix_rows), :], preferred_element_type=jnp.float32
            )
            weighted[h, :, :width] = weighted[h, :, :width] * factor + update[:, :width]
            weighted[h, :, width:] = weighted[h, :, width:] * factor + update[:, width:]

    wait_for(0)
    for h in range(2):
        peak = None
        for j in range(prefix_rows // part):
            peak = score_part(0, 0, h, j, peak)
        peaks[0, h] = peak

    def pair(u, carry):
        for s in range(2):
            t = 2 * u + s
            wait_for(t + 1)
            prefix_step(t, s, True)
        return carry

    lax.fori_loop(0, 3, pair, 0)
    wait_for(7)
    prefix_step(6, 0, True)
    prefix_step(7, 1, False)

    for p in range(8):
        for copy in fresh_copies(p, pieces[p]):
            copy.wait()

    def fresh_step(h, block, visible):
        at = pl.multiple_of(block * rows, rows)
        value = dotted(q_refs[h][0], fresh_keys[pl.ds(at, rows), :])
        if visible is not None:
            value = jnp.where(visible, value, NEG_FILL)
        before = running[h]
        now = jnp.maximum(before, jnp.max(value, axis=1, keepdims=True))
        running[h] = now
        factor = jnp.exp2((before - now) * scale)
        kept = jnp.concatenate(
            [
                jnp.exp2((value[:, l : l + width] - now) * scale).astype(jnp.bfloat16)
                for l in range(0, rows, width)
            ],
            axis=1,
        )
        update = jnp.dot(
            kept, fresh_values[pl.ds(at, rows), :], preferred_element_type=jnp.float32
        )
        weighted[h, :, :width] = weighted[h, :, :width] * factor + update[:, :width]
        weighted[h, :, width:] = weighted[h, :, width:] * factor + update[:, width:]

    fewer = me[0] & 3

    def both(block, carry):
        fresh_step(0, block, None)
        fresh_step(1, block, None)
        return carry

    lax.fori_loop(0, fewer, both, 0)
    for h in range(2):

        @pl.when(blocks[h] >= 4)
        def _():
            def one(block, carry):
                fresh_step(h, block, None)
                return carry

            lax.fori_loop(fewer, fewer + 4, one, 0)

    token = lax.broadcasted_iota(jnp.int32, (tile_rows, rows), 0) % chunk_rows + chunk_start
    visible = lax.broadcasted_iota(jnp.int32, (tile_rows, rows), 1) <= token
    for h in range(2):
        fresh_step(h, blocks[h], visible)
    for h in range(2):
        result = (weighted[h, :, :width] / weighted[h, :, width:]).astype(jnp.bfloat16)
        for g in range(group):
            out_ref[h, :, g * width : (g + 1) * width] = result[
                g * chunk_rows : (g + 1) * chunk_rows
            ]


def chunk_attention(chunk, me, queries, pieces, rows, group, after):
    _, tile_rows, width = queries[0].shape
    chunk_rows = tile_rows // group
    held = pieces[0].shape[1]
    prefix_rows = held - rows
    query = pl.BlockSpec((1, tile_rows, width), lambda i: (chunk, 0, 0))
    shape = (2, chunk_rows, group * width)
    return pl.pallas_call(
        functools.partial(
            attention_kernel,
            len(after),
            chunk * chunk_rows,
            chunk_rows,
            rows,
            group,
            width ** (-0.5) * LOG2E,
        ),
        grid=(1,),
        out_shape=jax.ShapeDtypeStruct(shape, jnp.bfloat16),
        in_specs=smem() + [query] * 2 + anywhere(8 + len(after)),
        out_specs=pl.BlockSpec(shape, lambda i: (0, 0, 0)),
        scratch_shapes=[
            pltpu.VMEM((8 * prefix_rows, width), jnp.bfloat16),
            pltpu.VMEM((8 * prefix_rows, 2 * width), jnp.bfloat16),
            pltpu.VMEM((8 * rows, width), jnp.bfloat16),
            pltpu.VMEM((8 * rows, 2 * width), jnp.bfloat16),
            pltpu.VMEM((2, 2, tile_rows, prefix_rows), jnp.float32),
            pltpu.VMEM((2, tile_rows, prefix_rows), jnp.bfloat16),
            pltpu.VMEM((2, 2, tile_rows, width), jnp.float32),
            pltpu.VMEM((2, tile_rows, width), jnp.float32),
            pltpu.VMEM((2, tile_rows, 2 * width), jnp.float32),
            pltpu.SemaphoreType.DMA((8, 4)),
        ],
        compiler_params=pltpu.CompilerParams(vmem_limit_bytes=36 * 1024 * 1024),
        cost_estimate=pl.CostEstimate(
            flops=2 * 2 * 2 * tile_rows * 8 * held * width * 2,
            bytes_accessed=8 * held * width * 4,
            transcendentals=2 * tile_rows * 8 * held,
        ),
        name="chunk_attention",
    )(me, *queries, *pieces, *after)


def decode_kernel(scale, me, q_ref, last_ref, *refs):
    pieces, out_ref = refs[:8], refs[8]
    q = q_ref[...]
    width = q.shape[1]
    low = me[0] < 4
    last = [jnp.where(low, last_ref[j, 0:1, :], last_ref[j, 1:2, :]) for j in range(2)]
    last = [value.astype(jnp.float32) for value in last]
    running = jnp.sum(q.astype(jnp.float32) * last[0], axis=1, keepdims=True)
    total = jnp.ones_like(running)
    weighted = jnp.broadcast_to(last[1], (q.shape[0], width))
    for piece in pieces:
        scores = lax.dot_general(
            q, piece[0], (((1,), (1,)), ((), ())), preferred_element_type=jnp.float32
        )
        highest = jnp.maximum(running, jnp.max(scores, axis=1, keepdims=True))
        weights = jnp.exp2((scores - highest) * scale)
        factor = jnp.exp2((running - highest) * scale)
        total = total * factor + jnp.sum(weights, axis=1, keepdims=True)
        weighted = weighted * factor + jnp.dot(
            weights.astype(jnp.bfloat16), piece[1], preferred_element_type=jnp.float32
        )
        running = highest
    out_ref[...] = (weighted / total).astype(jnp.bfloat16)


def decode(me, query, last, pieces, after):
    width = query.shape[1]
    held = pieces[0].shape[1]

    def kernel(me, q_ref, last_ref, *refs):
        decode_kernel(width ** (-0.5) * LOG2E, me, q_ref, last_ref, *refs[:8], refs[-1])

    return pl.pallas_call(
        kernel,
        out_shape=jax.ShapeDtypeStruct(query.shape, jnp.bfloat16),
        in_specs=smem() + vmem(10) + anywhere(len(after)),
        out_specs=vmem()[0],
        compiler_params=pltpu.CompilerParams(vmem_limit_bytes=32 * 1024 * 1024),
        cost_estimate=pl.CostEstimate(
            flops=4 * query.shape[0] * width * 8 * held,
            bytes_accessed=8 * held * width * 4,
            transcendentals=query.shape[0] * 8 * held,
        ),
        name="decode",
    )(me, query, last, *pieces, *after)


def pick_kernel(rows, me, member, remaining, *refs):
    pieces, outs, held, sems = refs[:8], refs[8:10], refs[10], refs[11]
    count = member.shape[0]
    copies = []
    for p in range(8):
        at = pl.multiple_of((me[0] ^ p) * rows, rows)
        copies.append(
            pltpu.make_async_copy(
                pieces[p].at[:, pl.ds(0, rows)], held.at[:, pl.ds(at, rows)], sems.at[p]
            )
        )
        copies[p].start()
    for out in outs:
        out[...] = jnp.zeros(out.shape, out.dtype)
    for copy in copies:
        copy.wait()
    for b in range(count):
        target = member[b, 0]
        owner = remaining[target]
        spot = jnp.int32(0)
        for before in range(b):
            spot += (member[before, 0] == target).astype(jnp.int32)
        at = pl.multiple_of(spot * BLK, BLK)
        for out, instance in zip(outs, (me[0], me[0] ^ 4)):

            @pl.when(owner == instance)
            def _():
                out[:, pl.ds(at, BLK), :] = held[:, b * BLK : (b + 1) * BLK, :]


def pick_blocks(me, member, remaining, pieces, rows):
    width = pieces[0].shape[2]
    shape = jax.ShapeDtypeStruct((2, CAP * BLK, width), jnp.bfloat16)
    return pl.pallas_call(
        functools.partial(pick_kernel, rows),
        out_shape=[shape, shape],
        in_specs=smem(3) + anywhere(8),
        out_specs=vmem(2),
        scratch_shapes=[
            pltpu.VMEM((2, 8 * rows, width), jnp.bfloat16),
            pltpu.SemaphoreType.DMA((8,)),
        ],
        compiler_params=pltpu.CompilerParams(vmem_limit_bytes=32 * 1024 * 1024),
        name="pick_blocks",
    )(me, member, remaining, *pieces)


def project_kernel(waits, slot, own, beside, across, corner, *refs):
    weights, outs = refs[:4], refs[4 + waits :]
    same = jnp.concatenate([own[0], own[1], across[0], across[1]], axis=0)
    other = jnp.concatenate([beside[1], beside[0], corner[1], corner[0]], axis=0)
    rows = own.shape[1]
    for half in range(2):
        total = jnp.dot(same, weights[2 * half][...], preferred_element_type=jnp.float32)
        total += jnp.dot(other, weights[2 * half + 1][...], preferred_element_type=jnp.float32)
        total = total.astype(jnp.bfloat16)
        for r in range(4):
            outs[r][half] = total[r * rows : (r + 1) * rows]


def project(slot, parts, own_weights, sibling_weights, after):
    _, rows, depth = parts[0].shape
    columns = own_weights.shape[1]
    tile = min(256, columns)
    whole = pl.BlockSpec((2, rows, depth), lambda j, slot: (0, 0, 0))
    same = pl.BlockSpec((depth, tile), lambda j, slot: (slot[0], j))
    other = pl.BlockSpec((depth, tile), lambda j, slot: (1 - slot[0], j))
    out = pl.BlockSpec((2, rows, tile), lambda j, slot: (0, 0, j))
    return pl.pallas_call(
        functools.partial(project_kernel, len(after)),
        grid_spec=pltpu.PrefetchScalarGridSpec(
            num_scalar_prefetch=1,
            grid=(columns // tile,),
            in_specs=[whole] * 4 + [same, other] * 2 + anywhere(len(after)),
            out_specs=[out] * 4,
        ),
        out_shape=[jax.ShapeDtypeStruct((2, rows, columns), jnp.bfloat16)] * 4,
        compiler_params=pltpu.CompilerParams(vmem_limit_bytes=32 * 1024 * 1024),
        cost_estimate=pl.CostEstimate(
            flops=2 * 4 * rows * 2 * depth * 2 * columns,
            bytes_accessed=2 * depth * 2 * columns * 2,
            transcendentals=0,
        ),
        name="project",
    )(slot, *parts, own_weights, own_weights, sibling_weights, sibling_weights, *after)


def away_kernel(offset, here, beside, across, corner, send_ref):
    @pl.when(offset[0] % 2 == 0)
    def _():
        send_ref[0] = across[...]
        send_ref[1] = corner[...]

    @pl.when(offset[0] % 2 == 1)
    def _():
        send_ref[0] = here[...]
        send_ref[1] = beside[...]


def away(offset, parts):
    return pl.pallas_call(
        away_kernel,
        out_shape=jax.ShapeDtypeStruct((2, *parts[0].shape), jnp.bfloat16),
        in_specs=smem() + vmem(4),
        out_specs=vmem()[0],
        name="away",
    )(offset, *parts)


def merge_kernel(offset, here, beside, across, corner, came, keep_ref, send_ref):
    def total(r):
        mine = ((here, across), (beside, corner))[r]

        def go(source):
            return source[...].astype(jnp.float32) + came[r].astype(jnp.float32)

        return [go(source) for source in mine]

    for low in range(2):
        for high in range(2):

            @pl.when(offset[0] == low + 2 * high)
            def _():
                keep_ref[...] = total(high)[low].astype(keep_ref.dtype)
                send_ref[...] = total(1 - high)[low].astype(send_ref.dtype)


def merge(offset, parts, came):
    return pl.pallas_call(
        merge_kernel,
        out_shape=[
            jax.ShapeDtypeStruct(parts[0].shape, jnp.float32),
            jax.ShapeDtypeStruct(parts[0].shape, jnp.bfloat16),
        ],
        in_specs=smem() + vmem(5),
        out_specs=vmem(2),
        name="merge",
    )(offset, *parts, came)


def on_device_planes(
    fresh_segment_probes,
    fresh_segment_pairs,
    earlier_stored_pairs,
    emitted_token_probe,
    emitted_token_pair,
    final_projection_weights,
    remaining_instance_ids,
    segment_destination_member,
):
    index = lax.axis_index("inst")
    slot = index // 4
    core = index % 2
    rows, heads, width = fresh_segment_probes.shape
    group = heads // 2
    me = jnp.reshape(index, (1,)).astype(jnp.int32)
    slot_array = jnp.reshape(slot, (1,)).astype(jnp.int32)
    offset = jnp.reshape(lax.axis_index("tp") ^ (index // 2), (1,)).astype(jnp.int32)

    piece = {}
    piece[0], to_beside = split_pairs(me, fresh_segment_pairs, earlier_stored_pairs)
    piece[4] = swapped(to_beside, "inst", 4)
    piece[2] = swapped(piece[0], "inst", 2)
    queries_own, queries_send = split_queries(me, fresh_segment_probes)
    queries = [queries_own, swapped(queries_send, "inst", 4)]
    piece[6] = swapped(piece[4], "inst", 2)
    for d in (0, 4, 2, 6):
        piece[d + 1] = swapped(piece[d], "inst", 1)
    pieces = [piece[d] for d in range(8)]
    sibling_weights = swapped(final_projection_weights, "inst", 1)

    picked_own, picked_send = pick_blocks(
        me, segment_destination_member, remaining_instance_ids, pieces, rows
    )
    picked_beside = swapped(picked_send, "inst", 4)
    first = jnp.where(slot == 0, picked_own, picked_beside)
    second = jnp.where(slot == 0, picked_beside, picked_own)
    cache = jnp.stack([first, second]).transpose(2, 1, 0, 3)

    def attention(chunk, after):
        own = chunk_attention(chunk, me, queries, pieces, rows, group, after)
        return [own] + [swapped(own, "inst", d) for d in (4, 2, 6)]

    def projected(parts, after):
        outs = project(slot_array, parts, final_projection_weights, sibling_weights, after)
        return [outs[0]] + [swapped(outs[i], "inst", d) for i, d in ((1, 4), (2, 2), (3, 6))]

    def first_step(parts):
        send = away(offset, parts)
        return send, swapped(send, "tp", 1)

    def second_step(parts, came):
        keep, send = merge(offset, parts, came)
        return keep, send, swapped(send, "tp", 2)

    def finished(keep, came):
        final = (keep + came.astype(jnp.float32)).astype(jnp.bfloat16)
        left = jnp.where(core == 0, final[0], final[1])
        right = jnp.where(core == 0, final[1], final[0])
        return jnp.concatenate([left, right], axis=1)

    gathered, partial, stepped, halves = {}, {}, {}, {}
    for turn in range(CHUNKS + 4):
        now = []
        k = turn - 4
        if 0 <= k < CHUNKS:
            halves[k] = second_step(partial[k], stepped[k][1])
            now.append(halves[k][1])
        k = turn - 3
        if 0 <= k < CHUNKS:
            stepped[k] = first_step(partial[k])
            now.append(stepped[k][0])
        k = turn - 2
        if 0 <= k < CHUNKS:
            partial[k] = projected(gathered[k], [gathered[turn - 1][0]] if turn - 1 in gathered else [])
            now.append(partial[k][0])
        if turn < CHUNKS:
            gathered[turn] = attention(turn, now)
    span_hidden = jnp.concatenate(
        [finished(halves[k][0], halves[k][2]) for k in range(CHUNKS)], axis=0
    )

    decoded = decode(me, emitted_token_probe, emitted_token_pair, pieces, [partial[CHUNKS - 1][0]])
    decoded_beside = swapped(decoded, "inst", 4)
    mine = (jnp.arange(heads) // group == slot)[:, None]
    decode_attention = jnp.where(mine, decoded, decoded_beside)
    return (span_hidden, cache[None], decode_attention)


def solution(mesh):
    instances, groups = mesh.shape["inst"], mesh.shape["tp"]

    def on_device(*arguments):
        slots_local = arguments[1].shape[2]
        if instances == 8 and groups == 4 and slots_local == 2:
            return on_device_planes(*arguments)
        return on_device_ring(*arguments)

    return jax.shard_map(
        on_device,
        mesh=mesh,
        in_specs=(
            P("inst", "tp", None),
            P("inst", None, "tp", None),
            P("inst", None, "tp", None),
            P("tp", None),
            P(None, "tp", None),
            P("tp", "inst"),
            P(),
            P(),
        ),
        out_specs=(P("inst", "tp"), P("inst", None, None, "tp", None), P("tp", None)),
        check_vma=False,
    )
```

```python
import functools

import jax
import jax.numpy as jnp
from jax import lax
from jax.experimental import pallas as pl
from jax.experimental.pallas import tpu as pltpu
from jax.sharding import PartitionSpec as P

BLK = 128
CAP = 8
NEG_FILL = -1e30
LOG2E = 1.4426950408889634
GROWTH = 60.0
CHUNKS = 4


def from_behind(block, axis, distance):
    devices = range(lax.axis_size(axis))
    route = [((i - distance) % len(devices), i) for i in devices]
    return lax.ppermute(block, axis, route)


def combined_all(value, axis, combine):
    everything = jax.tree.map(lambda part: lax.all_gather(part, axis), value)
    initial = jax.tree.map(lambda part: part[0], everything)

    def turn(k, so_far):
        return combine(so_far, jax.tree.map(lambda part: part[k], everything))

    return lax.fori_loop(1, lax.axis_size(axis), turn, initial)


def attend(state, queries, key_value, visible):
    width = queries.shape[-1]
    scores = jnp.einsum(
        "rkgd,nkd->rkgn", queries, key_value[:, 0], preferred_element_type=jnp.float32
    ) * width ** (-0.5)
    if visible is not None:
        scores = jnp.where(visible[:, None, None, :], scores, NEG_FILL)
    running, total, weighted = state
    highest = jnp.maximum(running, jnp.max(scores, axis=-1))
    factor = jnp.exp(running - highest)
    weights = jnp.exp(scores - highest[..., None])
    total = total * factor + jnp.sum(weights, axis=-1)
    update = jnp.einsum(
        "rkgn,nkd->rkgd",
        weights.astype(jnp.bfloat16),
        key_value[:, 1],
        preferred_element_type=jnp.float32,
    )
    weighted = weighted * factor[..., None] + update
    return (highest, total, weighted)


def empty_state(rows, slots_local, group, width):
    return (
        jnp.full((rows, slots_local, group), -jnp.inf, jnp.float32),
        jnp.zeros((rows, slots_local, group), jnp.float32),
        jnp.zeros((rows, slots_local, group, width), jnp.float32),
    )


def combine(first, second):
    highest = jnp.maximum(first[0], second[0])
    left = jnp.exp(first[0] - highest)
    right = jnp.exp(second[0] - highest)
    return (
        highest,
        first[1] * left + second[1] * right,
        first[2] * left[..., None] + second[2] * right[..., None],
    )


def place_blocks(cache, rows_in, destination_members, slots, own_index):
    count = rows_in.shape[0] // BLK

    def put(index, current):
        spot = slots[index] * BLK
        incoming = lax.dynamic_slice_in_dim(rows_in, index * BLK, BLK, 0)
        present = lax.dynamic_slice_in_dim(current, spot, BLK, 0)
        chosen = jnp.where(destination_members[index] == own_index, incoming, present)
        return lax.dynamic_update_slice_in_dim(current, chosen, spot, 0)

    return lax.fori_loop(0, count, put, cache)


def destinations(segment_destination_member, remaining_instance_ids):
    sequence = segment_destination_member[:, 0]
    agreement = (
        sequence[:, None]
        == jnp.arange(remaining_instance_ids.shape[0], dtype=jnp.int32)[None, :]
    ).astype(jnp.int32)
    slots = jnp.sum(jnp.cumsum(agreement, axis=0) * agreement, axis=1) - 1
    members = jnp.sum(agreement * remaining_instance_ids[None, :], axis=1)
    return slots, members


def on_device_ring(
    fresh_segment_probes,
    fresh_segment_pairs,
    earlier_stored_pairs,
    emitted_token_probe,
    emitted_token_pair,
    final_projection_weights,
    remaining_instance_ids,
    segment_destination_member,
):
    own_index = lax.axis_index("inst")
    instances = lax.axis_size("inst")
    rows, heads, width = fresh_segment_probes.shape
    slots_local = fresh_segment_pairs.shape[2]
    group = heads // slots_local
    queries = fresh_segment_probes.reshape(rows, slots_local, group, width)
    slots, destination_members = destinations(segment_destination_member, remaining_instance_ids)
    held_blocks = jnp.sum((destination_members == own_index).astype(jnp.int32))
    cache = jnp.zeros((CAP * BLK, 2, slots_local, width), jnp.bfloat16)
    causal = jnp.arange(rows)[:, None] >= jnp.arange(rows)[None, :]
    state = attend(
        empty_state(rows, slots_local, group, width), queries, earlier_stored_pairs, None
    )
    state = attend(state, queries, fresh_segment_pairs, causal)
    moving = jnp.concatenate([fresh_segment_pairs, earlier_stored_pairs], axis=0)

    def turn_both(step, carry):
        moving, state, current = carry
        moving = from_behind(moving, "inst", 1)
        source = (own_index - step) % instances
        state = attend(state, queries, moving[rows:], None)
        visible = jnp.broadcast_to(source < own_index, (rows, rows))
        state = attend(state, queries, moving[:rows], visible)
        return (moving, state, current)

    moving, state, cache = lax.fori_loop(1, instances, turn_both, (moving, state, cache))
    cache = place_blocks(
        cache,
        lax.all_gather(fresh_segment_pairs, "inst", axis=0, tiled=True),
        destination_members,
        slots,
        own_index,
    )
    attention = (state[2] / state[1][..., None]).astype(jnp.bfloat16).reshape(rows, heads * width)
    terms = jnp.dot(
        attention,
        lax.all_gather(final_projection_weights, "inst", axis=1, tiled=True),
        preferred_element_type=jnp.float32,
    )
    span_hidden = lax.psum_scatter(
        terms.astype(jnp.bfloat16), "tp", scatter_dimension=1, tiled=True
    )
    single = emitted_token_probe.reshape(1, slots_local, group, width)
    decode_state = attend(
        empty_state(1, slots_local, group, width), single, earlier_stored_pairs, None
    )
    live = (jnp.arange(CAP * BLK) < held_blocks * BLK)[None, :]
    decode_state = attend(decode_state, single, cache, live)
    merged = combined_all((decode_state[0], decode_state[1], decode_state[2]), "inst", combine)
    own_scores = jnp.einsum(
        "rkgd,kd->rkg", single, emitted_token_pair[0], preferred_element_type=jnp.float32
    ) * width ** (-0.5)
    highest = jnp.maximum(merged[0], own_scores)
    left = jnp.exp(merged[0] - highest)
    right = jnp.exp(own_scores - highest)
    total = merged[1] * left + right
    own_weight = lax.optimization_barrier(right.astype(jnp.bfloat16)).astype(jnp.float32)
    own_value = emitted_token_pair[1].astype(jnp.float32)
    weighted = merged[2] * left[..., None] + own_weight[..., None] * own_value[None, :, None, :]
    decode_attention = (weighted / total[..., None]).astype(jnp.bfloat16).reshape(heads, width)
    return (span_hidden, cache[None], decode_attention)


def swapped(value, axis, distance):
    size = lax.axis_size(axis)
    return lax.ppermute(value, axis, [(i, i ^ distance) for i in range(size)])


def vmem(count=1):
    return [pl.BlockSpec(memory_space=pltpu.VMEM)] * count


def smem(count=1):
    return [pl.BlockSpec(memory_space=pltpu.SMEM)] * count


def anywhere(count=1):
    return [pl.BlockSpec(memory_space=pl.ANY)] * count


def split_kernel(group, me, fresh, prefix, queries, own_ref, send_ref, q_own_ref, q_send_ref):
    rows = fresh.shape[0]
    chunk_rows = rows // CHUNKS

    def place(out, q_out, s):
        for j in range(2):
            out[j, :rows] = fresh[:, j, s, :]
            out[j, rows:] = prefix[:, j, s, :]
        for k in range(CHUNKS):
            for g in range(group):
                q_out[k, g * chunk_rows : (g + 1) * chunk_rows] = queries[
                    k * chunk_rows : (k + 1) * chunk_rows, s * group + g, :
                ]

    @pl.when(me[0] < 4)
    def _():
        place(own_ref, q_own_ref, 0)
        place(send_ref, q_send_ref, 1)

    @pl.when(me[0] >= 4)
    def _():
        place(own_ref, q_own_ref, 1)
        place(send_ref, q_send_ref, 0)


def split(me, fresh, prefix, queries):
    rows, heads, width = queries.shape
    group = heads // 2
    pairs = jax.ShapeDtypeStruct((2, rows + prefix.shape[0], width), jnp.bfloat16)
    probes = jax.ShapeDtypeStruct((CHUNKS, group * rows // CHUNKS, width), jnp.bfloat16)
    return pl.pallas_call(
        functools.partial(split_kernel, group),
        out_shape=[pairs, pairs, probes, probes],
        in_specs=smem() + vmem(3),
        out_specs=vmem(4),
        compiler_params=pltpu.CompilerParams(vmem_limit_bytes=32 * 1024 * 1024),
        name="split",
    )(me, fresh, prefix, queries)


def attention_kernel(waits, chunk_start, chunk_rows, rows, group, scale, me, own, beside, *refs):
    pieces = refs[:8]
    out_ref = refs[8 + waits]
    queries, keys, values, weights, shift, weighted, sems = refs[9 + waits :]
    _, tile_rows, width = own.shape
    held = pieces[0].shape[1]
    tile = held - rows
    part = 256

    def prefix_copies(p, piece):
        at = pl.multiple_of(p * tile, tile)
        return [
            pltpu.make_async_copy(
                piece.at[0, pl.ds(rows, tile)], keys.at[pl.ds(at, tile)], sems.at[p, 0]
            ),
            pltpu.make_async_copy(
                piece.at[1, pl.ds(rows, tile)],
                values.at[pl.ds(at, tile), pl.ds(0, width)],
                sems.at[p, 1],
            ),
        ]

    def fresh_copies(p, piece):
        at = pl.multiple_of(8 * tile + (me[0] ^ p) * rows, rows)
        return [
            pltpu.make_async_copy(
                piece.at[0, pl.ds(0, rows)], keys.at[pl.ds(at, rows)], sems.at[p, 2]
            ),
            pltpu.make_async_copy(
                piece.at[1, pl.ds(0, rows)],
                values.at[pl.ds(at, rows), pl.ds(0, width)],
                sems.at[p, 3],
            ),
        ]

    for p in range(8):
        for copy in prefix_copies(p, pieces[p]):
            copy.start()
    for p in range(8):
        for copy in fresh_copies(p, pieces[p]):
            copy.start()
    values[:, width:] = jnp.ones((values.shape[0], width), jnp.bfloat16)
    weighted[...] = jnp.zeros(weighted.shape, jnp.float32)

    @pl.when(me[0] < 4)
    def _():
        queries[0] = own[0]
        queries[1] = beside[0]

    @pl.when(me[0] >= 4)
    def _():
        queries[0] = beside[0]
        queries[1] = own[0]

    def wait_for(p):
        for copy in prefix_copies(p, pieces[0]):
            copy.wait()

    def scores(t, h, j):
        at = pl.multiple_of(t * tile + j * part, part)
        return lax.dot_general(
            queries[h],
            keys[pl.ds(at, part), :],
            (((1,), (1,)), ((), ())),
            preferred_element_type=jnp.float32,
        )

    def highest(peak, value):
        return value if peak is None else jnp.maximum(peak, value)

    def weigh(t, slot, h, masked):
        peak = None
        if masked:
            shape = (tile_rows, width)
            token = lax.broadcasted_iota(jnp.int32, shape, 0) % chunk_rows
            ahead = lax.broadcasted_iota(jnp.int32, shape, 1) - token
            allowed = (me[0] & 3) * rows + chunk_start
        for j in range(tile // part):
            value = scores(t, h, j)
            for l in range(0, part, width):
                at = j * part + l
                above = value[:, l : l + width] - shift[h]
                if masked:
                    above = jnp.where(ahead <= allowed - at, above, NEG_FILL)
                peak = highest(peak, above)
                weights[slot, h, :, at : at + width] = jnp.exp2(above * scale).astype(jnp.bfloat16)
        return peak

    def add(t, slot, h):
        at = pl.multiple_of(t * tile, tile)
        weighted[h] += jnp.dot(
            weights[slot, h], values[pl.ds(at, tile), :], preferred_element_type=jnp.float32
        )

    def turn(t, slot, halves, masked, before):
        peaks = []
        for h in range(2):
            if h in halves:
                peaks.append(weigh(t, slot, h, h in masked))
            if h in before:
                add(t - 1, 1 - slot, h)
        growth = functools.reduce(jnp.maximum, peaks)

        @pl.when(jnp.max(growth) * scale > GROWTH)
        def _():
            for h, peak in zip(halves, peaks):
                up = jnp.maximum(jnp.max(peak, axis=1, keepdims=True), 0.0)
                weighted[h] *= jnp.exp2(-up * scale)
                shift[h] += up
                weigh(t, slot, h, h in masked)

    wait_for(0)
    for h in range(2):
        peak = None
        for j in range(tile // part):
            value = scores(0, h, j)
            for l in range(0, part, width):
                peak = highest(peak, value[:, l : l + width])
        shift[h] = jnp.broadcast_to(jnp.max(peak, axis=1, keepdims=True), peak.shape)
    for h in range(2):
        weigh(0, 0, h, False)

    def pair(u, carry):
        for s in range(2):
            t = 2 * u + s + 1
            wait_for(t)
            turn(t, 1 - s, (0, 1), (), (0, 1))
        return carry

    lax.fori_loop(0, 3, pair, 0)
    wait_for(7)
    turn(7, 1, (0, 1), (), (0, 1))
    for p in range(8):
        for copy in fresh_copies(p, pieces[p]):
            copy.wait()
    turn(8, 0, (0, 1), (0,), (0, 1))
    turn(9, 1, (1,), (1,), (0, 1))
    add(9, 1, 1)
    for h in range(2):
        result = (weighted[h, :, :width] / weighted[h, :, width:]).astype(jnp.bfloat16)
        to = (me[0] >> 2) ^ h
        for g in range(group):
            out_ref[to, :, g * width : (g + 1) * width] = result[
                g * chunk_rows : (g + 1) * chunk_rows
            ]


def chunk_attention(chunk, me, queries, pieces, rows, group, after):
    _, tile_rows, width = queries[0].shape
    chunk_rows = tile_rows // group
    held = pieces[0].shape[1]
    tile = held - rows
    query = pl.BlockSpec((1, tile_rows, width), lambda i: (chunk, 0, 0))
    shape = (2, chunk_rows, group * width)
    return pl.pallas_call(
        functools.partial(
            attention_kernel,
            len(after),
            chunk * chunk_rows,
            chunk_rows,
            rows,
            group,
            width ** (-0.5) * LOG2E,
        ),
        grid=(1,),
        out_shape=jax.ShapeDtypeStruct(shape, jnp.bfloat16),
        in_specs=smem() + [query] * 2 + anywhere(8 + len(after)),
        out_specs=pl.BlockSpec(shape, lambda i: (0, 0, 0)),
        scratch_shapes=[
            pltpu.VMEM((2, tile_rows, width), jnp.bfloat16),
            pltpu.VMEM((8 * held, width), jnp.bfloat16),
            pltpu.VMEM((8 * held, 2 * width), jnp.bfloat16),
            pltpu.VMEM((2, 2, tile_rows, tile), jnp.bfloat16),
            pltpu.VMEM((2, tile_rows, width), jnp.float32),
            pltpu.VMEM((2, tile_rows, 2 * width), jnp.float32),
            pltpu.SemaphoreType.DMA((8, 4)),
        ],
        compiler_params=pltpu.CompilerParams(vmem_limit_bytes=26 * 1024 * 1024),
        cost_estimate=pl.CostEstimate(
            flops=2 * 2 * 2 * tile_rows * 8 * held * width * 2,
            bytes_accessed=8 * held * width * 4,
            transcendentals=2 * tile_rows * 8 * held,
        ),
        name="chunk_attention",
    )(me, *queries, *pieces, *after)


def decode_kernel(scale, me, q_ref, last_ref, *refs):
    pieces, out_ref = refs[:8], refs[8]
    q = q_ref[...]
    width = q.shape[1]
    low = me[0] < 4
    last = [jnp.where(low, last_ref[j, 0:1, :], last_ref[j, 1:2, :]) for j in range(2)]
    last = [value.astype(jnp.float32) for value in last]
    running = jnp.sum(q.astype(jnp.float32) * last[0], axis=1, keepdims=True)
    total = jnp.ones_like(running)
    weighted = jnp.broadcast_to(last[1], (q.shape[0], width))
    for piece in pieces:
        scores = lax.dot_general(
            q, piece[0], (((1,), (1,)), ((), ())), preferred_element_type=jnp.float32
        )
        highest = jnp.maximum(running, jnp.max(scores, axis=1, keepdims=True))
        weights = jnp.exp2((scores - highest) * scale)
        factor = jnp.exp2((running - highest) * scale)
        total = total * factor + jnp.sum(weights, axis=1, keepdims=True)
        weighted = weighted * factor + jnp.dot(
            weights.astype(jnp.bfloat16), piece[1], preferred_element_type=jnp.float32
        )
        running = highest
    out_ref[...] = (weighted / total).astype(jnp.bfloat16)


def decode(me, query, last, pieces, after):
    width = query.shape[1]
    held = pieces[0].shape[1]

    def kernel(me, q_ref, last_ref, *refs):
        decode_kernel(width ** (-0.5) * LOG2E, me, q_ref, last_ref, *refs[:8], refs[-1])

    return pl.pallas_call(
        kernel,
        out_shape=jax.ShapeDtypeStruct(query.shape, jnp.bfloat16),
        in_specs=smem() + vmem(10) + anywhere(len(after)),
        out_specs=vmem()[0],
        compiler_params=pltpu.CompilerParams(vmem_limit_bytes=32 * 1024 * 1024),
        cost_estimate=pl.CostEstimate(
            flops=4 * query.shape[0] * width * 8 * held,
            bytes_accessed=8 * held * width * 4,
            transcendentals=query.shape[0] * 8 * held,
        ),
        name="decode",
    )(me, query, last, *pieces, *after)


def pick_kernel(rows, me, member, remaining, *refs):
    pieces, (*outs, held, sems) = refs[:8], refs[-4:]
    count = member.shape[0]
    copies = []
    for p in range(8):
        at = pl.multiple_of((me[0] ^ p) * rows, rows)
        copies.append(
            pltpu.make_async_copy(
                pieces[p].at[:, pl.ds(0, rows)], held.at[:, pl.ds(at, rows)], sems.at[p]
            )
        )
        copies[p].start()
    for out in outs:
        out[...] = jnp.zeros(out.shape, out.dtype)
    for copy in copies:
        copy.wait()
    for b in range(count):
        target = member[b, 0]
        owner = remaining[target]
        spot = jnp.int32(0)
        for before in range(b):
            spot += (member[before, 0] == target).astype(jnp.int32)
        at = pl.multiple_of(spot * BLK, BLK)
        for out, instance in zip(outs, (me[0], me[0] ^ 4)):

            @pl.when(owner == instance)
            def _():
                out[:, pl.ds(at, BLK), :] = held[:, b * BLK : (b + 1) * BLK, :]


def pick_blocks(me, member, remaining, pieces, rows, after):
    width = pieces[0].shape[2]
    shape = jax.ShapeDtypeStruct((2, CAP * BLK, width), jnp.bfloat16)
    return pl.pallas_call(
        functools.partial(pick_kernel, rows),
        out_shape=[shape, shape],
        in_specs=smem(3) + anywhere(8 + len(after)),
        out_specs=vmem(2),
        scratch_shapes=[
            pltpu.VMEM((2, 8 * rows, width), jnp.bfloat16),
            pltpu.SemaphoreType.DMA((8,)),
        ],
        compiler_params=pltpu.CompilerParams(vmem_limit_bytes=32 * 1024 * 1024),
        name="pick_blocks",
    )(me, member, remaining, *pieces, *after)


def project_kernel(waits, slot, own, beside, across, corner, *refs):
    weights, outs = refs[:4], refs[4 + waits :]
    same = jnp.concatenate([own[0], own[1], across[0], across[1]], axis=0)
    other = jnp.concatenate([beside[1], beside[0], corner[1], corner[0]], axis=0)
    rows = own.shape[1]
    for half in range(2):
        total = jnp.dot(same, weights[2 * half][...], preferred_element_type=jnp.float32)
        total += jnp.dot(other, weights[2 * half + 1][...], preferred_element_type=jnp.float32)
        total = total.astype(jnp.bfloat16)
        for r in range(4):
            outs[r][half] = total[r * rows : (r + 1) * rows]


def project(slot, parts, own_weights, sibling_weights, after):
    _, rows, depth = parts[0].shape
    columns = own_weights.shape[1]
    tile = min(512, columns)
    whole = pl.BlockSpec((2, rows, depth), lambda j, slot: (0, 0, 0))
    same = pl.BlockSpec((depth, tile), lambda j, slot: (slot[0], j))
    other = pl.BlockSpec((depth, tile), lambda j, slot: (1 - slot[0], j))
    out = pl.BlockSpec((2, rows, tile), lambda j, slot: (0, 0, j))
    return pl.pallas_call(
        functools.partial(project_kernel, len(after)),
        grid_spec=pltpu.PrefetchScalarGridSpec(
            num_scalar_prefetch=1,
            grid=(columns // tile,),
            in_specs=[whole] * 4 + [same, other] * 2 + anywhere(len(after)),
            out_specs=[out] * 4,
        ),
        out_shape=[jax.ShapeDtypeStruct((2, rows, columns), jnp.bfloat16)] * 4,
        compiler_params=pltpu.CompilerParams(vmem_limit_bytes=32 * 1024 * 1024),
        cost_estimate=pl.CostEstimate(
            flops=2 * 4 * rows * 2 * depth * 2 * columns,
            bytes_accessed=2 * depth * 2 * columns * 2,
            transcendentals=0,
        ),
        name="project",
    )(slot, *parts, own_weights, own_weights, sibling_weights, sibling_weights, *after)


def away_kernel(offset, *refs):
    parts, sends = refs[:4], refs[4:]
    for mine in range(4):

        @pl.when(offset[0] == mine)
        def _():
            for d in range(1, 4):
                sends[d - 1][...] = parts[mine ^ d][...]


def away(offset, parts):
    return pl.pallas_call(
        away_kernel,
        out_shape=[jax.ShapeDtypeStruct(parts[0].shape, jnp.bfloat16)] * 3,
        in_specs=smem() + vmem(4),
        out_specs=vmem(3),
        name="away",
    )(offset, *parts)


def finish_kernel(offset, me, *refs):
    parts, came, out_ref = refs[:4], refs[4:7], refs[-1]
    columns = parts[0].shape[2]
    for half in range(2):
        other = came[0][half].astype(jnp.float32)
        for value in came[1:]:
            other += value[half].astype(jnp.float32)
        at = pl.multiple_of(((me[0] & 1) ^ half) * columns, columns)
        for mine in range(4):

            @pl.when(offset[0] == mine)
            def _():
                total = parts[mine][half].astype(jnp.float32) + other
                out_ref[:, pl.ds(at, columns)] = total.astype(out_ref.dtype)


def finish(chunk, offset, me, parts, came, so_far):
    _, rows, columns = parts[0].shape
    whole = pl.BlockSpec(parts[0].shape, lambda i: (0, 0, 0))
    operands = [offset, me, *parts, *came]
    specs = smem(2) + [whole] * 7
    aliases = {}
    if so_far is not None:
        aliases = {len(operands): 0}
        operands.append(so_far)
        specs += anywhere()
    return pl.pallas_call(
        finish_kernel,
        grid=(1,),
        out_shape=jax.ShapeDtypeStruct((CHUNKS * rows, 2 * columns), jnp.bfloat16),
        in_specs=specs,
        out_specs=pl.BlockSpec((rows, 2 * columns), lambda i: (chunk, 0)),
        input_output_aliases=aliases,
        name="finish",
    )(*operands)


def on_device_planes(
    fresh_segment_probes,
    fresh_segment_pairs,
    earlier_stored_pairs,
    emitted_token_probe,
    emitted_token_pair,
    final_projection_weights,
    remaining_instance_ids,
    segment_destination_member,
):
    index = lax.axis_index("inst")
    slot = index // 4
    rows, heads, width = fresh_segment_probes.shape
    group = heads // 2
    me = jnp.reshape(index, (1,)).astype(jnp.int32)
    slot_array = jnp.reshape(slot, (1,)).astype(jnp.int32)
    offset = jnp.reshape(lax.axis_index("tp") ^ (index // 2), (1,)).astype(jnp.int32)

    piece = {}
    piece[0], to_beside, queries_own, queries_send = split(
        me, fresh_segment_pairs, earlier_stored_pairs, fresh_segment_probes
    )
    piece[4] = swapped(to_beside, "inst", 4)
    piece[2] = swapped(piece[0], "inst", 2)
    queries = [queries_own, swapped(queries_send, "inst", 4)]
    piece[6] = swapped(piece[4], "inst", 2)
    for d in (0, 4, 2, 6):
        piece[d + 1] = swapped(piece[d], "inst", 1)
    pieces = [piece[d] for d in range(8)]
    sibling_weights = swapped(final_projection_weights, "inst", 1)

    def attention(chunk, after):
        own = chunk_attention(chunk, me, queries, pieces, rows, group, after)
        return [own] + [swapped(own, "inst", d) for d in (4, 2, 6)]

    def projected(parts, after):
        outs = project(slot_array, parts, final_projection_weights, sibling_weights, after)
        return [outs[0]] + [swapped(outs[i], "inst", d) for i, d in ((1, 4), (2, 2), (3, 6))]

    def exchanged(parts):
        ordered = [parts[0], parts[2], parts[1], parts[3]]
        sends = away(offset, ordered)
        return ordered, sends, [swapped(send, "tp", d + 1) for d, send in enumerate(sends)]

    gathered, partial, stepped = {}, {}, {}
    for turn in range(CHUNKS + 3):
        now = []
        k = turn - 3
        if 0 <= k < CHUNKS:
            stepped[k] = exchanged(partial[k])
            now.append(stepped[k][1][0])
        k = turn - 2
        if 0 <= k < CHUNKS:
            before = [gathered[turn - 1][0]] if turn - 1 in gathered else []
            partial[k] = projected(gathered[k], before)
            now.append(partial[k][0])
        if turn < CHUNKS:
            gathered[turn] = attention(turn, now)
        if turn == 1:
            picked_own, picked_send = pick_blocks(
                me, segment_destination_member, remaining_instance_ids, pieces, rows,
                [gathered[1][0]],
            )
            picked_beside = swapped(picked_send, "inst", 4)
    span_hidden = None
    for k in range(CHUNKS):
        ordered, _, came = stepped[k]
        span_hidden = finish(k, offset, me, ordered, came, span_hidden)

    first = jnp.where(slot == 0, picked_own, picked_beside)
    second = jnp.where(slot == 0, picked_beside, picked_own)
    cache = jnp.stack([first, second]).transpose(2, 1, 0, 3)

    decoded = decode(me, emitted_token_probe, emitted_token_pair, pieces, [partial[CHUNKS - 1][0]])
    decoded_beside = swapped(decoded, "inst", 4)
    mine = (jnp.arange(heads) // group == slot)[:, None]
    decode_attention = jnp.where(mine, decoded, decoded_beside)
    return (span_hidden, cache[None], decode_attention)


def solution(mesh):
    instances, groups = mesh.shape["inst"], mesh.shape["tp"]

    def on_device(*arguments):
        slots_local = arguments[1].shape[2]
        tile = arguments[2].shape[0]
        rows = arguments[1].shape[0]
        if instances == 8 and groups == 4 and slots_local == 2 and tile == 4 * rows:
            return on_device_planes(*arguments)
        return on_device_ring(*arguments)

    return jax.shard_map(
        on_device,
        mesh=mesh,
        in_specs=(
            P("inst", "tp", None),
            P("inst", None, "tp", None),
            P("inst", None, "tp", None),
            P("tp", None),
            P(None, "tp", None),
            P("tp", "inst"),
            P(),
            P(),
        ),
        out_specs=(P("inst", "tp"), P("inst", None, None, "tp", None), P("tp", None)),
        check_vma=False,
    )
```

```python
import functools

import jax
import jax.numpy as jnp
from jax import lax
from jax.experimental import pallas as pl
from jax.experimental.pallas import tpu as pltpu
from jax.sharding import PartitionSpec as P

BLK = 128
CAP = 8
NEG_FILL = -1e30
LOG2E = 1.4426950408889634
LARGEST = 2.0**100
CHUNKS = 4


def from_behind(block, axis, distance):
    devices = range(lax.axis_size(axis))
    route = [((i - distance) % len(devices), i) for i in devices]
    return lax.ppermute(block, axis, route)


def combined_all(value, axis, combine):
    everything = jax.tree.map(lambda part: lax.all_gather(part, axis), value)
    initial = jax.tree.map(lambda part: part[0], everything)

    def turn(k, so_far):
        return combine(so_far, jax.tree.map(lambda part: part[k], everything))

    return lax.fori_loop(1, lax.axis_size(axis), turn, initial)


def attend(state, queries, key_value, visible):
    width = queries.shape[-1]
    scores = jnp.einsum(
        "rkgd,nkd->rkgn", queries, key_value[:, 0], preferred_element_type=jnp.float32
    ) * width ** (-0.5)
    if visible is not None:
        scores = jnp.where(visible[:, None, None, :], scores, NEG_FILL)
    running, total, weighted = state
    highest = jnp.maximum(running, jnp.max(scores, axis=-1))
    factor = jnp.exp(running - highest)
    weights = jnp.exp(scores - highest[..., None])
    total = total * factor + jnp.sum(weights, axis=-1)
    update = jnp.einsum(
        "rkgn,nkd->rkgd",
        weights.astype(jnp.bfloat16),
        key_value[:, 1],
        preferred_element_type=jnp.float32,
    )
    weighted = weighted * factor[..., None] + update
    return (highest, total, weighted)


def empty_state(rows, slots_local, group, width):
    return (
        jnp.full((rows, slots_local, group), -jnp.inf, jnp.float32),
        jnp.zeros((rows, slots_local, group), jnp.float32),
        jnp.zeros((rows, slots_local, group, width), jnp.float32),
    )


def combine(first, second):
    highest = jnp.maximum(first[0], second[0])
    left = jnp.exp(first[0] - highest)
    right = jnp.exp(second[0] - highest)
    return (
        highest,
        first[1] * left + second[1] * right,
        first[2] * left[..., None] + second[2] * right[..., None],
    )


def place_blocks(cache, rows_in, destination_members, slots, own_index):
    count = rows_in.shape[0] // BLK

    def put(index, current):
        spot = slots[index] * BLK
        incoming = lax.dynamic_slice_in_dim(rows_in, index * BLK, BLK, 0)
        present = lax.dynamic_slice_in_dim(current, spot, BLK, 0)
        chosen = jnp.where(destination_members[index] == own_index, incoming, present)
        return lax.dynamic_update_slice_in_dim(current, chosen, spot, 0)

    return lax.fori_loop(0, count, put, cache)


def destinations(segment_destination_member, remaining_instance_ids):
    sequence = segment_destination_member[:, 0]
    agreement = (
        sequence[:, None]
        == jnp.arange(remaining_instance_ids.shape[0], dtype=jnp.int32)[None, :]
    ).astype(jnp.int32)
    slots = jnp.sum(jnp.cumsum(agreement, axis=0) * agreement, axis=1) - 1
    members = jnp.sum(agreement * remaining_instance_ids[None, :], axis=1)
    return slots, members


def on_device_ring(
    fresh_segment_probes,
    fresh_segment_pairs,
    earlier_stored_pairs,
    emitted_token_probe,
    emitted_token_pair,
    final_projection_weights,
    remaining_instance_ids,
    segment_destination_member,
):
    own_index = lax.axis_index("inst")
    instances = lax.axis_size("inst")
    rows, heads, width = fresh_segment_probes.shape
    slots_local = fresh_segment_pairs.shape[2]
    group = heads // slots_local
    queries = fresh_segment_probes.reshape(rows, slots_local, group, width)
    slots, destination_members = destinations(segment_destination_member, remaining_instance_ids)
    held_blocks = jnp.sum((destination_members == own_index).astype(jnp.int32))
    cache = jnp.zeros((CAP * BLK, 2, slots_local, width), jnp.bfloat16)
    causal = jnp.arange(rows)[:, None] >= jnp.arange(rows)[None, :]
    state = attend(
        empty_state(rows, slots_local, group, width), queries, earlier_stored_pairs, None
    )
    state = attend(state, queries, fresh_segment_pairs, causal)
    moving = jnp.concatenate([fresh_segment_pairs, earlier_stored_pairs], axis=0)

    def turn_both(step, carry):
        moving, state, current = carry
        moving = from_behind(moving, "inst", 1)
        source = (own_index - step) % instances
        state = attend(state, queries, moving[rows:], None)
        visible = jnp.broadcast_to(source < own_index, (rows, rows))
        state = attend(state, queries, moving[:rows], visible)
        return (moving, state, current)

    moving, state, cache = lax.fori_loop(1, instances, turn_both, (moving, state, cache))
    cache = place_blocks(
        cache,
        lax.all_gather(fresh_segment_pairs, "inst", axis=0, tiled=True),
        destination_members,
        slots,
        own_index,
    )
    attention = (state[2] / state[1][..., None]).astype(jnp.bfloat16).reshape(rows, heads * width)
    terms = jnp.dot(
        attention,
        lax.all_gather(final_projection_weights, "inst", axis=1, tiled=True),
        preferred_element_type=jnp.float32,
    )
    span_hidden = lax.psum_scatter(
        terms.astype(jnp.bfloat16), "tp", scatter_dimension=1, tiled=True
    )
    single = emitted_token_probe.reshape(1, slots_local, group, width)
    decode_state = attend(
        empty_state(1, slots_local, group, width), single, earlier_stored_pairs, None
    )
    live = (jnp.arange(CAP * BLK) < held_blocks * BLK)[None, :]
    decode_state = attend(decode_state, single, cache, live)
    merged = combined_all((decode_state[0], decode_state[1], decode_state[2]), "inst", combine)
    own_scores = jnp.einsum(
        "rkgd,kd->rkg", single, emitted_token_pair[0], preferred_element_type=jnp.float32
    ) * width ** (-0.5)
    highest = jnp.maximum(merged[0], own_scores)
    left = jnp.exp(merged[0] - highest)
    right = jnp.exp(own_scores - highest)
    total = merged[1] * left + right
    own_weight = lax.optimization_barrier(right.astype(jnp.bfloat16)).astype(jnp.float32)
    own_value = emitted_token_pair[1].astype(jnp.float32)
    weighted = merged[2] * left[..., None] + own_weight[..., None] * own_value[None, :, None, :]
    decode_attention = (weighted / total[..., None]).astype(jnp.bfloat16).reshape(heads, width)
    return (span_hidden, cache[None], decode_attention)


def swapped(value, axis, distance):
    size = lax.axis_size(axis)
    return lax.ppermute(value, axis, [(i, i ^ distance) for i in range(size)])


def vmem(count=1):
    return [pl.BlockSpec(memory_space=pltpu.VMEM)] * count


def smem(count=1):
    return [pl.BlockSpec(memory_space=pltpu.SMEM)] * count


def hbm(count=1):
    return [pl.BlockSpec(memory_space=pltpu.HBM)] * count


def anywhere(count=1):
    return [pl.BlockSpec(memory_space=pl.ANY)] * count


def split_kernel(group, me, fresh_in, prefix_in, queries_in, *refs):
    own_ref, send_ref, q_own_ref, q_send_ref, fresh, prefix, queries, sems = refs
    copies = [
        pltpu.make_async_copy(source, target, sems.at[n])
        for n, (source, target) in enumerate(
            ((fresh_in, fresh), (prefix_in, prefix), (queries_in, queries))
        )
    ]
    for copy in copies:
        copy.start()
    rows = fresh.shape[0]
    chunk_rows = rows // CHUNKS

    def place(out, s):
        for part, start in ((fresh, 0), (prefix, rows)):
            size = part.shape[0]
            out[1, start : start + size] = part[:, 1, s, :]
            for at in range(0, size, BLK):
                block = part[at : at + BLK, 0, s, :]
                out[0, start + at : start + at + BLK] = block.T

    def place_queries(q_out, s):
        for k in range(CHUNKS):
            for g in range(group):
                q_out[k, g * chunk_rows : (g + 1) * chunk_rows] = queries[
                    k * chunk_rows : (k + 1) * chunk_rows, s * group + g, :
                ]

    copies[0].wait()
    copies[1].wait()
    for y in range(2):

        @pl.when(me[0] >> 2 == y)
        def _():
            place(own_ref, y)
            place(send_ref, 1 - y)

    copies[2].wait()
    for y in range(2):

        @pl.when(me[0] >> 2 == y)
        def _():
            place_queries(q_own_ref, y)
            place_queries(q_send_ref, 1 - y)


def split(me, fresh, prefix, queries):
    rows, heads, width = queries.shape
    group = heads // 2
    pairs = jax.ShapeDtypeStruct((2, rows + prefix.shape[0], width), jnp.bfloat16)
    probes = jax.ShapeDtypeStruct((CHUNKS, group * rows // CHUNKS, width), jnp.bfloat16)
    return pl.pallas_call(
        functools.partial(split_kernel, group),
        out_shape=[pairs, pairs, probes, probes],
        in_specs=smem() + hbm(3),
        out_specs=vmem(4),
        scratch_shapes=[
            pltpu.VMEM(part.shape, part.dtype) for part in (fresh, prefix, queries)
        ]
        + [pltpu.SemaphoreType.DMA((3,))],
        compiler_params=pltpu.CompilerParams(vmem_limit_bytes=32 * 1024 * 1024),
        name="split",
    )(me, fresh, prefix, queries)


def attention_kernel(waits, chunk_start, chunk_rows, rows, group, scale, me, own, beside, *refs):
    pieces = refs[:8]
    out_ref = refs[8 + waits]
    queries, keys, values, weights, shift, weighted, sems = refs[9 + waits :]
    _, half, width = own.shape
    held = pieces[0].shape[1]
    tile = held - rows
    part = 2 * BLK

    def prefix_copies(p, piece):
        at = pl.multiple_of(p * tile, tile)
        return [
            pltpu.make_async_copy(
                piece.at[0, pl.ds(rows, tile)], keys.at[pl.ds(at, tile)], sems.at[p, 0]
            ),
            pltpu.make_async_copy(
                piece.at[1, pl.ds(rows, tile)],
                values.at[pl.ds(at, tile), pl.ds(0, width)],
                sems.at[p, 1],
            ),
        ]

    def fresh_copies(p, piece):
        at = pl.multiple_of(8 * tile + (me[0] ^ p) * rows, rows)
        return [
            pltpu.make_async_copy(
                piece.at[0, pl.ds(0, rows)], keys.at[pl.ds(at, rows)], sems.at[p, 2]
            ),
            pltpu.make_async_copy(
                piece.at[1, pl.ds(0, rows)],
                values.at[pl.ds(at, rows), pl.ds(0, width)],
                sems.at[p, 3],
            ),
        ]

    for p in range(8):
        for copy in prefix_copies(p, pieces[p]):
            copy.start()
    for p in range(8):
        for copy in fresh_copies(p, pieces[p]):
            copy.start()
    values[:, width:] = jnp.ones((values.shape[0], width), jnp.bfloat16)
    weighted[...] = jnp.zeros(weighted.shape, jnp.float32)

    @pl.when(me[0] < 4)
    def _():
        queries[:half] = own[0]
        queries[half:] = beside[0]

    @pl.when(me[0] >= 4)
    def _():
        queries[:half] = beside[0]
        queries[half:] = own[0]

    def wait_for(p):
        for copy in prefix_copies(p, pieces[0]):
            copy.wait()

    def scores(t, j, lo, hi):
        at = pl.multiple_of(t * tile + j * part, part)
        block = jnp.concatenate(
            [keys[pl.ds(at + l, BLK), :] for l in range(0, part, BLK)], axis=1
        )
        return jnp.dot(queries[lo:hi], block, preferred_element_type=jnp.float32)

    def above(t, j, lo, hi, masked):
        value = scores(t, j, lo, hi)
        blocks = [value[:, l : l + width] - shift[lo:hi] for l in range(0, part, width)]
        if not masked:
            return blocks
        shape = (hi - lo, width)
        row = lax.broadcasted_iota(jnp.int32, shape, 0)
        latest = (me[0] & 3) * rows + chunk_start + row % chunk_rows
        if hi - lo > half:
            latest = jnp.where(row < half, latest, tile)
        column = lax.broadcasted_iota(jnp.int32, shape, 1)
        return [
            jnp.where(column <= latest - (j * part + l * width), block, NEG_FILL)
            for l, block in enumerate(blocks)
        ]

    def weigh(t, slot, j, lo, hi, masked):
        for l, block in enumerate(above(t, j, lo, hi, masked)):
            at = j * part + l * width
            weights[slot, lo:hi, at : at + width] = jnp.exp2(block * scale).astype(jnp.bfloat16)

    def add(t, slot, lo, hi):
        at = pl.multiple_of(t * tile, tile)
        weighted[lo:hi] += jnp.dot(
            weights[slot, lo:hi], values[pl.ds(at, tile), :], preferred_element_type=jnp.float32
        )

    def turn(t, slot, lo, masked):
        for j in range(tile // part):
            weigh(t, slot, j, lo, 2 * half, masked)
            if j % 2 == 0:
                side = j // 2 * half
                add(t - 1, 1 - slot, side, side + half)

    wait_for(0)
    peak = None
    for j in range(tile // part):
        value = scores(0, j, 0, 2 * half)
        for l in range(0, part, width):
            block = value[:, l : l + width]
            peak = block if peak is None else jnp.maximum(peak, block)
    shift[...] = jnp.broadcast_to(jnp.max(peak, axis=1, keepdims=True), peak.shape)
    for j in range(tile // part):
        weigh(0, 0, j, 0, 2 * half, False)

    def prefix_turn(t, carry):
        wait_for(t)
        turn(t, t & 1, 0, False)
        return carry

    lax.fori_loop(1, 8, prefix_turn, 0)
    for p in range(8):
        for copy in fresh_copies(p, pieces[p]):
            copy.wait()
    turn(8, 0, 0, True)
    turn(9, 1, half, True)
    add(9, 1, half, 2 * half)

    def careful(t, lo, masked):
        peak = None
        for j in range(tile // part):
            for block in above(t, j, lo, 2 * half, masked):
                peak = block if peak is None else jnp.maximum(peak, block)
        up = jnp.maximum(jnp.max(peak, axis=1, keepdims=True), 0.0)
        weighted[lo:] *= jnp.exp2(-up * scale)
        shift[lo:] += up
        for j in range(tile // part):
            weigh(t, 0, j, lo, 2 * half, masked)
        add(t, 0, lo, 2 * half)

    @pl.when(jnp.logical_not(jnp.max(weighted[:, width:]) < LARGEST))
    def _():
        weighted[...] = jnp.zeros(weighted.shape, jnp.float32)

        def prefix_tile(t, carry):
            careful(t, 0, False)
            return carry

        lax.fori_loop(0, 8, prefix_tile, 0)
        careful(8, 0, True)
        careful(9, half, True)

    for h in range(2):
        block = weighted[h * half : (h + 1) * half]
        result = (block[:, :width] / block[:, width:]).astype(jnp.bfloat16)
        to = (me[0] >> 2) ^ h
        for g in range(group):
            out_ref[to, :, g * width : (g + 1) * width] = result[
                g * chunk_rows : (g + 1) * chunk_rows
            ]


def chunk_attention(chunk, me, queries, pieces, rows, group, after):
    _, tile_rows, width = queries[0].shape
    chunk_rows = tile_rows // group
    held = pieces[0].shape[1]
    tile = held - rows
    query = pl.BlockSpec((1, tile_rows, width), lambda i: (chunk, 0, 0))
    shape = (2, chunk_rows, group * width)
    return pl.pallas_call(
        functools.partial(
            attention_kernel,
            len(after),
            chunk * chunk_rows,
            chunk_rows,
            rows,
            group,
            width ** (-0.5) * LOG2E,
        ),
        grid=(1,),
        out_shape=jax.ShapeDtypeStruct(shape, jnp.bfloat16),
        in_specs=smem() + [query] * 2 + hbm(8) + anywhere(len(after)),
        out_specs=pl.BlockSpec(shape, lambda i: (0, 0, 0)),
        scratch_shapes=[
            pltpu.VMEM((2 * tile_rows, width), jnp.bfloat16),
            pltpu.VMEM((8 * held, width), jnp.bfloat16),
            pltpu.VMEM((8 * held, 2 * width), jnp.bfloat16),
            pltpu.VMEM((2, 2 * tile_rows, tile), jnp.bfloat16),
            pltpu.VMEM((2 * tile_rows, width), jnp.float32),
            pltpu.VMEM((2 * tile_rows, 2 * width), jnp.float32),
            pltpu.SemaphoreType.DMA((8, 4)),
        ],
        compiler_params=pltpu.CompilerParams(vmem_limit_bytes=26 * 1024 * 1024),
        cost_estimate=pl.CostEstimate(
            flops=2 * 2 * 2 * tile_rows * 8 * held * width * 2,
            bytes_accessed=8 * held * width * 4,
            transcendentals=2 * tile_rows * 8 * held,
        ),
        name="chunk_attention",
    )(me, *queries, *pieces, *after)


def decode_kernel(scale, me, q_ref, last_ref, *refs):
    pieces, out_ref = refs[:8], refs[8]
    q = q_ref[...]
    width = q.shape[1]
    low = me[0] < 4
    last = [jnp.where(low, last_ref[j, 0:1, :], last_ref[j, 1:2, :]) for j in range(2)]
    last = [value.astype(jnp.float32) for value in last]
    running = jnp.sum(q.astype(jnp.float32) * last[0], axis=1, keepdims=True)
    total = jnp.ones_like(running)
    weighted = jnp.broadcast_to(last[1], (q.shape[0], width))
    for piece in pieces:
        scores = jnp.concatenate(
            [
                jnp.dot(q, piece[0, at : at + BLK], preferred_element_type=jnp.float32)
                for at in range(0, piece.shape[1], BLK)
            ],
            axis=1,
        )
        highest = jnp.maximum(running, jnp.max(scores, axis=1, keepdims=True))
        weights = jnp.exp2((scores - highest) * scale)
        factor = jnp.exp2((running - highest) * scale)
        total = total * factor + jnp.sum(weights, axis=1, keepdims=True)
        weighted = weighted * factor + jnp.dot(
            weights.astype(jnp.bfloat16), piece[1], preferred_element_type=jnp.float32
        )
        running = highest
    out_ref[...] = (weighted / total).astype(jnp.bfloat16)


def decode(me, query, last, pieces, after):
    width = query.shape[1]
    held = pieces[0].shape[1]

    def kernel(me, q_ref, last_ref, *refs):
        decode_kernel(width ** (-0.5) * LOG2E, me, q_ref, last_ref, *refs[:8], refs[-1])

    return pl.pallas_call(
        kernel,
        out_shape=jax.ShapeDtypeStruct(query.shape, jnp.bfloat16),
        in_specs=smem() + vmem(10) + anywhere(len(after)),
        out_specs=vmem()[0],
        compiler_params=pltpu.CompilerParams(vmem_limit_bytes=32 * 1024 * 1024),
        cost_estimate=pl.CostEstimate(
            flops=4 * query.shape[0] * width * 8 * held,
            bytes_accessed=8 * held * width * 4,
            transcendentals=query.shape[0] * 8 * held,
        ),
        name="decode",
    )(me, query, last, *pieces, *after)


def pick_kernel(rows, me, member, remaining, *refs):
    pieces, (*outs, held, sems) = refs[:8], refs[-4:]
    count = member.shape[0]
    copies = []
    for p in range(8):
        at = pl.multiple_of((me[0] ^ p) * rows, rows)
        copies.append(
            pltpu.make_async_copy(
                pieces[p].at[:, pl.ds(0, rows)], held.at[:, pl.ds(at, rows)], sems.at[p]
            )
        )
        copies[p].start()
    for out in outs:
        out[...] = jnp.zeros(out.shape, out.dtype)
    for copy in copies:
        copy.wait()
    for b in range(count):
        target = member[b, 0]
        owner = remaining[target]
        spot = jnp.int32(0)
        for before in range(b):
            spot += (member[before, 0] == target).astype(jnp.int32)
        at = pl.multiple_of(spot * BLK, BLK)
        for out, instance in zip(outs, (me[0], me[0] ^ 4)):

            @pl.when(owner == instance)
            def _():
                out[0, pl.ds(at, BLK), :] = held[0, b * BLK : (b + 1) * BLK, :].T
                out[1, pl.ds(at, BLK), :] = held[1, b * BLK : (b + 1) * BLK, :]


def pick_blocks(me, member, remaining, pieces, rows, after):
    width = pieces[0].shape[2]
    shape = jax.ShapeDtypeStruct((2, CAP * BLK, width), jnp.bfloat16)
    return pl.pallas_call(
        functools.partial(pick_kernel, rows),
        out_shape=[shape, shape],
        in_specs=smem(3) + hbm(8) + anywhere(len(after)),
        out_specs=vmem(2),
        scratch_shapes=[
            pltpu.VMEM((2, 8 * rows, width), jnp.bfloat16),
            pltpu.SemaphoreType.DMA((8,)),
        ],
        compiler_params=pltpu.CompilerParams(vmem_limit_bytes=32 * 1024 * 1024),
        name="pick_blocks",
    )(me, member, remaining, *pieces, *after)


def project_kernel(waits, slot, own, beside, across, corner, *refs):
    weights, outs, held, sems = refs[:2], refs[2 + waits : -2], refs[-2], refs[-1]
    depth = held.shape[2]
    tile = held.shape[3]
    tiles = weights[0].shape[1] // tile
    copies = []
    for step in range(2 * tiles):
        half, j = step // tiles, step % tiles
        for other in range(2):
            at = pl.multiple_of((slot[0] ^ other) * depth, depth)
            copies.append(
                pltpu.make_async_copy(
                    weights[half].at[pl.ds(at, depth), pl.ds(j * tile, tile)],
                    held.at[step, other],
                    sems.at[step, other],
                )
            )
            copies[-1].start()
    same = jnp.concatenate([own[0], own[1], across[0], across[1]], axis=0)
    other = jnp.concatenate([beside[1], beside[0], corner[1], corner[0]], axis=0)
    rows = own.shape[1]
    for step in range(2 * tiles):
        half, j = step // tiles, step % tiles
        copies[2 * step].wait()
        copies[2 * step + 1].wait()
        total = jnp.dot(same, held[step, 0], preferred_element_type=jnp.float32)
        total += jnp.dot(other, held[step, 1], preferred_element_type=jnp.float32)
        total = total.astype(jnp.bfloat16)
        for r in range(4):
            outs[r][half, :, j * tile : (j + 1) * tile] = total[r * rows : (r + 1) * rows]


def project(slot, parts, own_weights, sibling_weights, after):
    _, rows, depth = parts[0].shape
    columns = own_weights.shape[1]
    tile = min(256, columns)
    tiles = columns // tile
    return pl.pallas_call(
        functools.partial(project_kernel, len(after)),
        out_shape=[jax.ShapeDtypeStruct((2, rows, columns), jnp.bfloat16)] * 4,
        in_specs=smem() + vmem(4) + hbm(2) + anywhere(len(after)),
        out_specs=vmem(4),
        scratch_shapes=[
            pltpu.VMEM((2 * tiles, 2, depth, tile), jnp.bfloat16),
            pltpu.SemaphoreType.DMA((2 * tiles, 2)),
        ],
        compiler_params=pltpu.CompilerParams(vmem_limit_bytes=26 * 1024 * 1024),
        cost_estimate=pl.CostEstimate(
            flops=2 * 4 * rows * 2 * depth * 2 * columns,
            bytes_accessed=2 * depth * 2 * columns * 2,
            transcendentals=0,
        ),
        name="project",
    )(slot, *parts, own_weights, sibling_weights, *after)


def away_kernel(offset, *refs):
    parts, sends = refs[:4], refs[-3:]
    for mine in range(4):

        @pl.when(offset[0] == mine)
        def _():
            for d in range(1, 4):
                sends[d - 1][...] = parts[mine ^ d][...]


def away(offset, parts, after):
    return pl.pallas_call(
        away_kernel,
        out_shape=[jax.ShapeDtypeStruct(parts[0].shape, jnp.bfloat16)] * 3,
        in_specs=smem() + vmem(4) + anywhere(len(after)),
        out_specs=vmem(3),
        name="away",
    )(offset, *parts, *after)


def finish_kernel(offset, me, *refs):
    parts, came, out_ref = refs[:4], refs[4:7], refs[-1]
    columns = parts[0].shape[2]
    for half in range(2):
        other = came[0][half].astype(jnp.float32)
        for value in came[1:]:
            other += value[half].astype(jnp.float32)
        at = pl.multiple_of(((me[0] & 1) ^ half) * columns, columns)
        for mine in range(4):

            @pl.when(offset[0] == mine)
            def _():
                total = parts[mine][half].astype(jnp.float32) + other
                out_ref[:, pl.ds(at, columns)] = total.astype(out_ref.dtype)


def finish(chunk, offset, me, parts, came, so_far):
    _, rows, columns = parts[0].shape
    whole = pl.BlockSpec(parts[0].shape, lambda i: (0, 0, 0))
    operands = [offset, me, *parts, *came]
    specs = smem(2) + [whole] * 7
    aliases = {}
    if so_far is not None:
        aliases = {len(operands): 0}
        operands.append(so_far)
        specs += anywhere()
    return pl.pallas_call(
        finish_kernel,
        grid=(1,),
        out_shape=jax.ShapeDtypeStruct((CHUNKS * rows, 2 * columns), jnp.bfloat16),
        in_specs=specs,
        out_specs=pl.BlockSpec((rows, 2 * columns), lambda i: (chunk, 0)),
        input_output_aliases=aliases,
        name="finish",
    )(*operands)


def on_device_planes(
    fresh_segment_probes,
    fresh_segment_pairs,
    earlier_stored_pairs,
    emitted_token_probe,
    emitted_token_pair,
    final_projection_weights,
    remaining_instance_ids,
    segment_destination_member,
):
    index = lax.axis_index("inst")
    slot = index // 4
    rows, heads, width = fresh_segment_probes.shape
    group = heads // 2
    me = jnp.reshape(index, (1,)).astype(jnp.int32)
    slot_array = jnp.reshape(slot, (1,)).astype(jnp.int32)
    offset = jnp.reshape(lax.axis_index("tp") ^ (index // 2), (1,)).astype(jnp.int32)

    piece = {}
    piece[0], to_beside, queries_own, queries_send = split(
        me, fresh_segment_pairs, earlier_stored_pairs, fresh_segment_probes
    )
    piece[4] = swapped(to_beside, "inst", 4)
    piece[2] = swapped(piece[0], "inst", 2)
    queries = [queries_own, swapped(queries_send, "inst", 4)]
    piece[6] = swapped(piece[4], "inst", 2)
    for d in (0, 4, 2, 6):
        piece[d + 1] = swapped(piece[d], "inst", 1)
    pieces = [piece[d] for d in range(8)]
    sibling_weights = swapped(final_projection_weights, "inst", 1)

    def attention(chunk, after):
        own = chunk_attention(chunk, me, queries, pieces, rows, group, after)
        return [own] + [swapped(own, "inst", d) for d in (4, 2, 6)]

    def projected(parts, after):
        outs = project(slot_array, parts, final_projection_weights, sibling_weights, after)
        return [outs[0]] + [swapped(outs[i], "inst", d) for i, d in ((1, 4), (2, 2), (3, 6))]

    def exchanged(parts, after):
        ordered = [parts[0], parts[2], parts[1], parts[3]]
        sends = away(offset, ordered, after)
        return ordered, sends, [swapped(send, "tp", d + 1) for d, send in enumerate(sends)]

    gathered, partial, stepped = {}, {}, {}
    gathered[0] = attention(0, [])
    gathered[1] = attention(1, [])
    picked_own, picked_send = pick_blocks(
        me, segment_destination_member, remaining_instance_ids, pieces, rows, [gathered[1][0]]
    )
    picked_beside = swapped(picked_send, "inst", 4)
    for k in range(CHUNKS):
        last = k + 1 >= CHUNKS
        after = [] if last else [gathered[k + 1][0]]
        if 0 < k < CHUNKS - 1:
            stepped[k - 1] = exchanged(partial[k - 1], after)
            after = after + [stepped[k - 1][1][0]]
        partial[k] = projected(gathered[k], after)
        if k + 2 < CHUNKS:
            gathered[k + 2] = attention(k + 2, [partial[k][0]])
    for k in range(CHUNKS - 2, CHUNKS):
        stepped[k] = exchanged(partial[k], [partial[CHUNKS - 1][0]])
    span_hidden = None
    for k in range(CHUNKS):
        ordered, _, came = stepped[k]
        span_hidden = finish(k, offset, me, ordered, came, span_hidden)

    first = jnp.where(slot == 0, picked_own, picked_beside)
    second = jnp.where(slot == 0, picked_beside, picked_own)
    cache = jnp.stack([first, second]).transpose(2, 1, 0, 3)

    decoded = decode(me, emitted_token_probe, emitted_token_pair, pieces, [partial[CHUNKS - 1][0]])
    decoded_beside = swapped(decoded, "inst", 4)
    mine = (jnp.arange(heads) // group == slot)[:, None]
    decode_attention = jnp.where(mine, decoded, decoded_beside)
    return (span_hidden, cache[None], decode_attention)


def solution(mesh):
    instances, groups = mesh.shape["inst"], mesh.shape["tp"]

    def on_device(*arguments):
        slots_local = arguments[1].shape[2]
        tile = arguments[2].shape[0]
        rows = arguments[1].shape[0]
        if instances == 8 and groups == 4 and slots_local == 2 and tile == 4 * rows:
            return on_device_planes(*arguments)
        return on_device_ring(*arguments)

    return jax.shard_map(
        on_device,
        mesh=mesh,
        in_specs=(
            P("inst", "tp", None),
            P("inst", None, "tp", None),
            P("inst", None, "tp", None),
            P("tp", None),
            P(None, "tp", None),
            P("tp", "inst"),
            P(),
            P(),
        ),
        out_specs=(P("inst", "tp"), P("inst", None, None, "tp", None), P("tp", None)),
        check_vma=False,
    )
```

```python
import functools

import jax
import jax.numpy as jnp
from jax import lax
from jax.experimental import pallas as pl
from jax.experimental.pallas import tpu as pltpu
from jax.sharding import PartitionSpec as P

BLK = 128
CAP = 8
NEG_FILL = -1e30
LOG2E = 1.4426950408889634
LARGEST = 2.0**100
CHUNKS = 4


def from_behind(block, axis, distance):
    devices = range(lax.axis_size(axis))
    route = [((i - distance) % len(devices), i) for i in devices]
    return lax.ppermute(block, axis, route)


def combined_all(value, axis, combine):
    everything = jax.tree.map(lambda part: lax.all_gather(part, axis), value)
    initial = jax.tree.map(lambda part: part[0], everything)

    def turn(k, so_far):
        return combine(so_far, jax.tree.map(lambda part: part[k], everything))

    return lax.fori_loop(1, lax.axis_size(axis), turn, initial)


def attend(state, queries, key_value, visible):
    width = queries.shape[-1]
    scores = jnp.einsum(
        "rkgd,nkd->rkgn", queries, key_value[:, 0], preferred_element_type=jnp.float32
    ) * width ** (-0.5)
    if visible is not None:
        scores = jnp.where(visible[:, None, None, :], scores, NEG_FILL)
    running, total, weighted = state
    highest = jnp.maximum(running, jnp.max(scores, axis=-1))
    factor = jnp.exp(running - highest)
    weights = jnp.exp(scores - highest[..., None])
    total = total * factor + jnp.sum(weights, axis=-1)
    update = jnp.einsum(
        "rkgn,nkd->rkgd",
        weights.astype(jnp.bfloat16),
        key_value[:, 1],
        preferred_element_type=jnp.float32,
    )
    weighted = weighted * factor[..., None] + update
    return (highest, total, weighted)


def empty_state(rows, slots_local, group, width):
    return (
        jnp.full((rows, slots_local, group), -jnp.inf, jnp.float32),
        jnp.zeros((rows, slots_local, group), jnp.float32),
        jnp.zeros((rows, slots_local, group, width), jnp.float32),
    )


def combine(first, second):
    highest = jnp.maximum(first[0], second[0])
    left = jnp.exp(first[0] - highest)
    right = jnp.exp(second[0] - highest)
    return (
        highest,
        first[1] * left + second[1] * right,
        first[2] * left[..., None] + second[2] * right[..., None],
    )


def place_blocks(cache, rows_in, destination_members, slots, own_index):
    count = rows_in.shape[0] // BLK

    def put(index, current):
        spot = slots[index] * BLK
        incoming = lax.dynamic_slice_in_dim(rows_in, index * BLK, BLK, 0)
        present = lax.dynamic_slice_in_dim(current, spot, BLK, 0)
        chosen = jnp.where(destination_members[index] == own_index, incoming, present)
        return lax.dynamic_update_slice_in_dim(current, chosen, spot, 0)

    return lax.fori_loop(0, count, put, cache)


def destinations(segment_destination_member, remaining_instance_ids):
    sequence = segment_destination_member[:, 0]
    agreement = (
        sequence[:, None]
        == jnp.arange(remaining_instance_ids.shape[0], dtype=jnp.int32)[None, :]
    ).astype(jnp.int32)
    slots = jnp.sum(jnp.cumsum(agreement, axis=0) * agreement, axis=1) - 1
    members = jnp.sum(agreement * remaining_instance_ids[None, :], axis=1)
    return slots, members


def on_device_ring(
    fresh_segment_probes,
    fresh_segment_pairs,
    earlier_stored_pairs,
    emitted_token_probe,
    emitted_token_pair,
    final_projection_weights,
    remaining_instance_ids,
    segment_destination_member,
):
    own_index = lax.axis_index("inst")
    instances = lax.axis_size("inst")
    rows, heads, width = fresh_segment_probes.shape
    slots_local = fresh_segment_pairs.shape[2]
    group = heads // slots_local
    queries = fresh_segment_probes.reshape(rows, slots_local, group, width)
    slots, destination_members = destinations(segment_destination_member, remaining_instance_ids)
    held_blocks = jnp.sum((destination_members == own_index).astype(jnp.int32))
    cache = jnp.zeros((CAP * BLK, 2, slots_local, width), jnp.bfloat16)
    causal = jnp.arange(rows)[:, None] >= jnp.arange(rows)[None, :]
    state = attend(
        empty_state(rows, slots_local, group, width), queries, earlier_stored_pairs, None
    )
    state = attend(state, queries, fresh_segment_pairs, causal)
    moving = jnp.concatenate([fresh_segment_pairs, earlier_stored_pairs], axis=0)

    def turn_both(step, carry):
        moving, state, current = carry
        moving = from_behind(moving, "inst", 1)
        source = (own_index - step) % instances
        state = attend(state, queries, moving[rows:], None)
        visible = jnp.broadcast_to(source < own_index, (rows, rows))
        state = attend(state, queries, moving[:rows], visible)
        return (moving, state, current)

    moving, state, cache = lax.fori_loop(1, instances, turn_both, (moving, state, cache))
    cache = place_blocks(
        cache,
        lax.all_gather(fresh_segment_pairs, "inst", axis=0, tiled=True),
        destination_members,
        slots,
        own_index,
    )
    attention = (state[2] / state[1][..., None]).astype(jnp.bfloat16).reshape(rows, heads * width)
    terms = jnp.dot(
        attention,
        lax.all_gather(final_projection_weights, "inst", axis=1, tiled=True),
        preferred_element_type=jnp.float32,
    )
    span_hidden = lax.psum_scatter(
        terms.astype(jnp.bfloat16), "tp", scatter_dimension=1, tiled=True
    )
    single = emitted_token_probe.reshape(1, slots_local, group, width)
    decode_state = attend(
        empty_state(1, slots_local, group, width), single, earlier_stored_pairs, None
    )
    live = (jnp.arange(CAP * BLK) < held_blocks * BLK)[None, :]
    decode_state = attend(decode_state, single, cache, live)
    merged = combined_all((decode_state[0], decode_state[1], decode_state[2]), "inst", combine)
    own_scores = jnp.einsum(
        "rkgd,kd->rkg", single, emitted_token_pair[0], preferred_element_type=jnp.float32
    ) * width ** (-0.5)
    highest = jnp.maximum(merged[0], own_scores)
    left = jnp.exp(merged[0] - highest)
    right = jnp.exp(own_scores - highest)
    total = merged[1] * left + right
    own_weight = lax.optimization_barrier(right.astype(jnp.bfloat16)).astype(jnp.float32)
    own_value = emitted_token_pair[1].astype(jnp.float32)
    weighted = merged[2] * left[..., None] + own_weight[..., None] * own_value[None, :, None, :]
    decode_attention = (weighted / total[..., None]).astype(jnp.bfloat16).reshape(heads, width)
    return (span_hidden, cache[None], decode_attention)


def swapped(value, axis, distance):
    size = lax.axis_size(axis)
    return lax.ppermute(value, axis, [(i, i ^ distance) for i in range(size)])


def vmem(count=1):
    return [pl.BlockSpec(memory_space=pltpu.VMEM)] * count


def smem(count=1):
    return [pl.BlockSpec(memory_space=pltpu.SMEM)] * count


def hbm(count=1):
    return [pl.BlockSpec(memory_space=pltpu.HBM)] * count


def anywhere(count=1):
    return [pl.BlockSpec(memory_space=pl.ANY)] * count


def split_kernel(group, me, fresh_in, prefix_in, queries_in, *refs):
    own_ref, send_ref, q_own_ref, q_send_ref, fresh, prefix, queries, sems = refs
    copies = [
        pltpu.make_async_copy(source, target, sems.at[n])
        for n, (source, target) in enumerate(
            ((fresh_in, fresh), (prefix_in, prefix), (queries_in, queries))
        )
    ]
    for copy in copies:
        copy.start()
    rows = fresh.shape[0]
    chunk_rows = rows // CHUNKS

    def place(out, s):
        for part, start in ((fresh, 0), (prefix, rows)):
            size = part.shape[0]
            out[1, start : start + size] = part[:, 1, s, :]
            for at in range(0, size, BLK):
                block = part[at : at + BLK, 0, s, :]
                out[0, start + at : start + at + BLK] = block.T

    def place_queries(q_out, s):
        for k in range(CHUNKS):
            for g in range(group):
                q_out[k, g * chunk_rows : (g + 1) * chunk_rows] = queries[
                    k * chunk_rows : (k + 1) * chunk_rows, s * group + g, :
                ]

    copies[0].wait()
    copies[1].wait()
    for y in range(2):

        @pl.when(me[0] >> 2 == y)
        def _():
            place(own_ref, y)
            place(send_ref, 1 - y)

    copies[2].wait()
    for y in range(2):

        @pl.when(me[0] >> 2 == y)
        def _():
            place_queries(q_own_ref, y)
            place_queries(q_send_ref, 1 - y)


def split(me, fresh, prefix, queries):
    rows, heads, width = queries.shape
    group = heads // 2
    pairs = jax.ShapeDtypeStruct((2, rows + prefix.shape[0], width), jnp.bfloat16)
    probes = jax.ShapeDtypeStruct((CHUNKS, group * rows // CHUNKS, width), jnp.bfloat16)
    return pl.pallas_call(
        functools.partial(split_kernel, group),
        out_shape=[pairs, pairs, probes, probes],
        in_specs=smem() + hbm(3),
        out_specs=vmem(4),
        scratch_shapes=[
            pltpu.VMEM(part.shape, part.dtype) for part in (fresh, prefix, queries)
        ]
        + [pltpu.SemaphoreType.DMA((3,))],
        compiler_params=pltpu.CompilerParams(vmem_limit_bytes=32 * 1024 * 1024),
        name="split",
    )(me, fresh, prefix, queries)


def attention_kernel(waits, chunk_start, chunk_rows, rows, group, scale, me, own, beside, *refs):
    pieces = refs[:8]
    out_ref = refs[8 + waits]
    queries, keys, values, even, odd, shift, sums, weighted, sems = refs[9 + waits :]
    weights = (even, odd)
    _, half, width = own.shape
    held = pieces[0].shape[1]
    tile = held - rows
    part = 2 * BLK

    def prefix_copies(p, piece):
        at = pl.multiple_of(p * tile, tile)
        return [
            pltpu.make_async_copy(
                piece.at[0, pl.ds(rows, tile)], keys.at[pl.ds(at, tile)], sems.at[p, 0]
            ),
            pltpu.make_async_copy(
                piece.at[1, pl.ds(rows, tile)],
                values.at[pl.ds(at, tile)],
                sems.at[p, 1],
            ),
        ]

    def fresh_copies(p, piece):
        at = pl.multiple_of(8 * tile + (me[0] ^ p) * rows, rows)
        return [
            pltpu.make_async_copy(
                piece.at[0, pl.ds(0, rows)], keys.at[pl.ds(at, rows)], sems.at[p, 2]
            ),
            pltpu.make_async_copy(
                piece.at[1, pl.ds(0, rows)],
                values.at[pl.ds(at, rows)],
                sems.at[p, 3],
            ),
        ]

    for p in range(8):
        for copy in prefix_copies(p, pieces[p]):
            copy.start()
    for p in range(8):
        for copy in fresh_copies(p, pieces[p]):
            copy.start()
    weighted[...] = jnp.zeros(weighted.shape, jnp.float32)
    sums[...] = jnp.zeros(sums.shape, jnp.float32)

    @pl.when(me[0] < 4)
    def _():
        queries[:half] = own[0]
        queries[half:] = beside[0]

    @pl.when(me[0] >= 4)
    def _():
        queries[:half] = beside[0]
        queries[half:] = own[0]

    def wait_for(p):
        for copy in prefix_copies(p, pieces[0]):
            copy.wait()

    def scores(t, j, lo, hi):
        at = pl.multiple_of(t * tile + j * part, part)
        block = jnp.concatenate(
            [keys[pl.ds(at + l, BLK), :] for l in range(0, part, BLK)], axis=1
        )
        return jnp.dot(queries[lo:hi], block, preferred_element_type=jnp.float32)

    def above(t, j, lo, hi, masked):
        value = scores(t, j, lo, hi)
        blocks = [value[:, l : l + width] - shift[lo:hi] for l in range(0, part, width)]
        if not masked:
            return blocks
        shape = (hi - lo, width)
        row = lax.broadcasted_iota(jnp.int32, shape, 0)
        latest = (me[0] & 3) * rows + chunk_start + row % chunk_rows
        if hi - lo > half:
            latest = jnp.where(row < half, latest, tile)
        column = lax.broadcasted_iota(jnp.int32, shape, 1)
        return [
            jnp.where(column <= latest - (j * part + l * width), block, NEG_FILL)
            for l, block in enumerate(blocks)
        ]

    def weigh(t, slot, j, lo, hi, masked):
        total = sums[lo:hi]
        for l, block in enumerate(above(t, j, lo, hi, masked)):
            at = j * part + l * width
            weight = jnp.exp2(block * scale)
            total += weight
            weights[slot][lo:hi, at : at + width] = weight.astype(jnp.bfloat16)
        sums[lo:hi] = total

    def add(t, slot, lo, hi):
        at = pl.multiple_of(t * tile, tile)
        weighted[lo:hi] += jnp.dot(
            weights[slot][lo:hi], values[pl.ds(at, tile), :], preferred_element_type=jnp.float32
        )

    def turn(t, slot, lo, masked):
        for j in range(tile // part):
            weigh(t, slot, j, lo, 2 * half, masked)
            if j % 2 == 0:
                side = j // 2 * half
                add(t - 1, 1 - slot, side, side + half)

    wait_for(0)
    peak = None
    for j in range(tile // part):
        value = scores(0, j, 0, 2 * half)
        for l in range(0, part, width):
            block = value[:, l : l + width]
            peak = block if peak is None else jnp.maximum(peak, block)
    shift[...] = jnp.broadcast_to(jnp.max(peak, axis=1, keepdims=True), peak.shape)
    for j in range(tile // part):
        weigh(0, 0, j, 0, 2 * half, False)

    def pair(u, carry):
        for s in range(2):
            t = 2 * u + s + 1
            wait_for(t)
            turn(t, 1 - s, 0, False)
        return carry

    lax.fori_loop(0, 3, pair, 0)
    wait_for(7)
    turn(7, 1, 0, False)
    for p in range(8):
        for copy in fresh_copies(p, pieces[p]):
            copy.wait()
    turn(8, 0, 0, True)
    turn(9, 1, half, True)
    add(9, 1, half, 2 * half)

    def careful(t, lo, masked):
        peak = None
        for j in range(tile // part):
            for block in above(t, j, lo, 2 * half, masked):
                peak = block if peak is None else jnp.maximum(peak, block)
        up = jnp.maximum(jnp.max(peak, axis=1, keepdims=True), 0.0)
        weighted[lo:] *= jnp.exp2(-up * scale)
        sums[lo:] *= jnp.exp2(-up * scale)
        shift[lo:] += up
        for j in range(tile // part):
            weigh(t, 0, j, lo, 2 * half, masked)
        add(t, 0, lo, 2 * half)

    @pl.when(jnp.logical_not(jnp.max(sums[...]) < LARGEST))
    def _():
        weighted[...] = jnp.zeros(weighted.shape, jnp.float32)
        sums[...] = jnp.zeros(sums.shape, jnp.float32)

        def prefix_tile(t, carry):
            careful(t, 0, False)
            return carry

        lax.fori_loop(0, 8, prefix_tile, 0)
        careful(8, 0, True)
        careful(9, half, True)

    for h in range(2):
        total = jnp.sum(sums[h * half : (h + 1) * half], axis=1, keepdims=True)
        result = (weighted[h * half : (h + 1) * half] / total).astype(jnp.bfloat16)
        to = (me[0] >> 2) ^ h
        for g in range(group):
            out_ref[to, :, g * width : (g + 1) * width] = result[
                g * chunk_rows : (g + 1) * chunk_rows
            ]


def chunk_attention(chunk, me, queries, pieces, rows, group, after):
    _, tile_rows, width = queries[0].shape
    chunk_rows = tile_rows // group
    held = pieces[0].shape[1]
    tile = held - rows
    query = pl.BlockSpec((1, tile_rows, width), lambda i: (chunk, 0, 0))
    shape = (2, chunk_rows, group * width)
    return pl.pallas_call(
        functools.partial(
            attention_kernel,
            len(after),
            chunk * chunk_rows,
            chunk_rows,
            rows,
            group,
            width ** (-0.5) * LOG2E,
        ),
        grid=(1,),
        out_shape=jax.ShapeDtypeStruct(shape, jnp.bfloat16),
        in_specs=smem() + [query] * 2 + hbm(8) + anywhere(len(after)),
        out_specs=pl.BlockSpec(shape, lambda i: (0, 0, 0)),
        scratch_shapes=[
            pltpu.VMEM((2 * tile_rows, width), jnp.bfloat16),
            pltpu.VMEM((8 * held, width), jnp.bfloat16),
            pltpu.VMEM((8 * held, width), jnp.bfloat16),
            pltpu.VMEM((2 * tile_rows, tile), jnp.bfloat16),
            pltpu.VMEM((2 * tile_rows, tile), jnp.bfloat16),
            pltpu.VMEM((2 * tile_rows, width), jnp.float32),
            pltpu.VMEM((2 * tile_rows, width), jnp.float32),
            pltpu.VMEM((2 * tile_rows, width), jnp.float32),
            pltpu.SemaphoreType.DMA((8, 4)),
        ],
        compiler_params=pltpu.CompilerParams(vmem_limit_bytes=26 * 1024 * 1024),
        cost_estimate=pl.CostEstimate(
            flops=2 * 2 * 2 * tile_rows * 8 * held * width * 2,
            bytes_accessed=8 * held * width * 4,
            transcendentals=2 * tile_rows * 8 * held,
        ),
        name="chunk_attention",
    )(me, *queries, *pieces, *after)


def decode_kernel(scale, me, q_ref, last_ref, *refs):
    pieces, out_ref = refs[:8], refs[8]
    q = q_ref[...]
    width = q.shape[1]
    low = me[0] < 4
    last = [jnp.where(low, last_ref[j, 0:1, :], last_ref[j, 1:2, :]) for j in range(2)]
    last = [value.astype(jnp.float32) for value in last]
    running = jnp.sum(q.astype(jnp.float32) * last[0], axis=1, keepdims=True)
    total = jnp.ones_like(running)
    weighted = jnp.broadcast_to(last[1], (q.shape[0], width))
    for piece in pieces:
        scores = jnp.concatenate(
            [
                jnp.dot(q, piece[0, at : at + BLK], preferred_element_type=jnp.float32)
                for at in range(0, piece.shape[1], BLK)
            ],
            axis=1,
        )
        highest = jnp.maximum(running, jnp.max(scores, axis=1, keepdims=True))
        weights = jnp.exp2((scores - highest) * scale)
        factor = jnp.exp2((running - highest) * scale)
        total = total * factor + jnp.sum(weights, axis=1, keepdims=True)
        weighted = weighted * factor + jnp.dot(
            weights.astype(jnp.bfloat16), piece[1], preferred_element_type=jnp.float32
        )
        running = highest
    out_ref[...] = (weighted / total).astype(jnp.bfloat16)


def decode(me, query, last, pieces, after):
    width = query.shape[1]
    held = pieces[0].shape[1]

    def kernel(me, q_ref, last_ref, *refs):
        decode_kernel(width ** (-0.5) * LOG2E, me, q_ref, last_ref, *refs[:8], refs[-1])

    return pl.pallas_call(
        kernel,
        out_shape=jax.ShapeDtypeStruct(query.shape, jnp.bfloat16),
        in_specs=smem() + vmem(10) + anywhere(len(after)),
        out_specs=vmem()[0],
        compiler_params=pltpu.CompilerParams(vmem_limit_bytes=32 * 1024 * 1024),
        cost_estimate=pl.CostEstimate(
            flops=4 * query.shape[0] * width * 8 * held,
            bytes_accessed=8 * held * width * 4,
            transcendentals=query.shape[0] * 8 * held,
        ),
        name="decode",
    )(me, query, last, *pieces, *after)


def pick_kernel(rows, me, member, remaining, *refs):
    pieces, (*outs, held, sems) = refs[:8], refs[-4:]
    count = member.shape[0]
    copies = []
    for p in range(8):
        at = pl.multiple_of((me[0] ^ p) * rows, rows)
        copies.append(
            pltpu.make_async_copy(
                pieces[p].at[:, pl.ds(0, rows)], held.at[:, pl.ds(at, rows)], sems.at[p]
            )
        )
        copies[p].start()
    for out in outs:
        out[...] = jnp.zeros(out.shape, out.dtype)
    for copy in copies:
        copy.wait()
    for b in range(count):
        target = member[b, 0]
        owner = remaining[target]
        spot = jnp.int32(0)
        for before in range(b):
            spot += (member[before, 0] == target).astype(jnp.int32)
        at = pl.multiple_of(spot * BLK, BLK)
        for out, instance in zip(outs, (me[0], me[0] ^ 4)):

            @pl.when(owner == instance)
            def _():
                out[0, pl.ds(at, BLK), :] = held[0, b * BLK : (b + 1) * BLK, :].T
                out[1, pl.ds(at, BLK), :] = held[1, b * BLK : (b + 1) * BLK, :]


def pick_blocks(me, member, remaining, pieces, rows, after):
    width = pieces[0].shape[2]
    shape = jax.ShapeDtypeStruct((2, CAP * BLK, width), jnp.bfloat16)
    return pl.pallas_call(
        functools.partial(pick_kernel, rows),
        out_shape=[shape, shape],
        in_specs=smem(3) + hbm(8) + anywhere(len(after)),
        out_specs=vmem(2),
        scratch_shapes=[
            pltpu.VMEM((2, 8 * rows, width), jnp.bfloat16),
            pltpu.SemaphoreType.DMA((8,)),
        ],
        compiler_params=pltpu.CompilerParams(vmem_limit_bytes=32 * 1024 * 1024),
        name="pick_blocks",
    )(me, member, remaining, *pieces, *after)


def project_kernel(waits, slot, own, beside, across, corner, *refs):
    weights, outs = refs[:4], refs[4 + waits :]
    same = jnp.concatenate([own[0], own[1], across[0], across[1]], axis=0)
    other = jnp.concatenate([beside[1], beside[0], corner[1], corner[0]], axis=0)
    rows = own.shape[1]
    for half in range(2):
        total = jnp.dot(same, weights[2 * half][...], preferred_element_type=jnp.float32)
        total += jnp.dot(other, weights[2 * half + 1][...], preferred_element_type=jnp.float32)
        total = total.astype(jnp.bfloat16)
        for r in range(4):
            outs[r][half] = total[r * rows : (r + 1) * rows]


def project(slot, parts, own_weights, sibling_weights, after):
    _, rows, depth = parts[0].shape
    columns = own_weights.shape[1]
    tile = min(512, columns)
    whole = pl.BlockSpec((2, rows, depth), lambda j, slot: (0, 0, 0))
    same = pl.BlockSpec((depth, tile), lambda j, slot: (slot[0], j))
    other = pl.BlockSpec((depth, tile), lambda j, slot: (1 - slot[0], j))
    out = pl.BlockSpec((2, rows, tile), lambda j, slot: (0, 0, j))
    return pl.pallas_call(
        functools.partial(project_kernel, len(after)),
        grid_spec=pltpu.PrefetchScalarGridSpec(
            num_scalar_prefetch=1,
            grid=(columns // tile,),
            in_specs=[whole] * 4 + [same, other] * 2 + anywhere(len(after)),
            out_specs=[out] * 4,
        ),
        out_shape=[jax.ShapeDtypeStruct((2, rows, columns), jnp.bfloat16)] * 4,
        compiler_params=pltpu.CompilerParams(vmem_limit_bytes=26 * 1024 * 1024),
        cost_estimate=pl.CostEstimate(
            flops=2 * 4 * rows * 2 * depth * 2 * columns,
            bytes_accessed=2 * depth * 2 * columns * 2,
            transcendentals=0,
        ),
        name="project",
    )(slot, *parts, own_weights, own_weights, sibling_weights, sibling_weights, *after)


def on_device_planes(
    fresh_segment_probes,
    fresh_segment_pairs,
    earlier_stored_pairs,
    emitted_token_probe,
    emitted_token_pair,
    final_projection_weights,
    remaining_instance_ids,
    segment_destination_member,
):
    index = lax.axis_index("inst")
    slot = index // 4
    rows, heads, width = fresh_segment_probes.shape
    group = heads // 2
    me = jnp.reshape(index, (1,)).astype(jnp.int32)
    slot_array = jnp.reshape(slot, (1,)).astype(jnp.int32)
    core = index % 2

    piece = {}
    piece[0], to_beside, queries_own, queries_send = split(
        me, fresh_segment_pairs, earlier_stored_pairs, fresh_segment_probes
    )
    piece[4] = swapped(to_beside, "inst", 4)
    piece[2] = swapped(piece[0], "inst", 2)
    queries = [queries_own, swapped(queries_send, "inst", 4)]
    piece[6] = swapped(piece[4], "inst", 2)
    for d in (0, 4, 2, 6):
        piece[d + 1] = swapped(piece[d], "inst", 1)
    pieces = [piece[d] for d in range(8)]
    sibling_weights = swapped(final_projection_weights, "inst", 1)

    def attention(chunk, after):
        own = chunk_attention(chunk, me, queries, pieces, rows, group, after)
        return [own] + [swapped(own, "inst", d) for d in (4, 2, 6)]

    def projected(parts, after):
        outs = project(slot_array, parts, final_projection_weights, sibling_weights, after)
        return [outs[0]] + [swapped(outs[i], "inst", d) for i, d in ((1, 4), (2, 2), (3, 6))]

    planes = lax.axis_size("tp")
    lines = [
        [i * planes + (r ^ (i // 2)) for r in range(planes)] for i in range(lax.axis_size("inst"))
    ]

    def reduced(parts):
        ordered = jnp.stack([parts[0], parts[2], parts[1], parts[3]])
        total = lax.psum_scatter(ordered, ("inst", "tp"), axis_index_groups=lines)
        left = jnp.where(core == 0, total[0], total[1])
        right = jnp.where(core == 0, total[1], total[0])
        return jnp.concatenate([left, right], axis=1)

    gathered, partial = {}, {}
    gathered[0] = attention(0, [])
    gathered[1] = attention(1, [])
    picked_own, picked_send = pick_blocks(
        me, segment_destination_member, remaining_instance_ids, pieces, rows, [gathered[1][0]]
    )
    picked_beside = swapped(picked_send, "inst", 4)
    for k in range(CHUNKS):
        after = [gathered[k + 1][0]] if k + 1 < CHUNKS else []
        partial[k] = projected(gathered[k], after)
        if k + 2 < CHUNKS:
            gathered[k + 2] = attention(k + 2, [partial[k][0]])
    span_hidden = jnp.concatenate([reduced(partial[k]) for k in range(CHUNKS)], axis=0)

    first = jnp.where(slot == 0, picked_own, picked_beside)
    second = jnp.where(slot == 0, picked_beside, picked_own)
    cache = jnp.stack([first, second]).transpose(2, 1, 0, 3)

    decoded = decode(me, emitted_token_probe, emitted_token_pair, pieces, [partial[CHUNKS - 1][0]])
    decoded_beside = swapped(decoded, "inst", 4)
    mine = (jnp.arange(heads) // group == slot)[:, None]
    decode_attention = jnp.where(mine, decoded, decoded_beside)
    return (span_hidden, cache[None], decode_attention)


def solution(mesh):
    instances, groups = mesh.shape["inst"], mesh.shape["tp"]

    def on_device(*arguments):
        slots_local = arguments[1].shape[2]
        tile = arguments[2].shape[0]
        rows = arguments[1].shape[0]
        if instances == 8 and groups == 4 and slots_local == 2 and tile == 4 * rows:
            return on_device_planes(*arguments)
        return on_device_ring(*arguments)

    return jax.shard_map(
        on_device,
        mesh=mesh,
        in_specs=(
            P("inst", "tp", None),
            P("inst", None, "tp", None),
            P("inst", None, "tp", None),
            P("tp", None),
            P(None, "tp", None),
            P("tp", "inst"),
            P(),
            P(),
        ),
        out_specs=(P("inst", "tp"), P("inst", None, None, "tp", None), P("tp", None)),
        check_vma=False,
    )
```

```python
import functools

import jax
import jax.numpy as jnp
from jax import lax
from jax.experimental import pallas as pl
from jax.experimental.pallas import tpu as pltpu
from jax.sharding import PartitionSpec as P

BLK = 128
CAP = 8
NEG_FILL = -1e30
LOG2E = 1.4426950408889634
LARGEST = 2.0**100
CHUNKS = 4


def from_behind(block, axis, distance):
    devices = range(lax.axis_size(axis))
    route = [((i - distance) % len(devices), i) for i in devices]
    return lax.ppermute(block, axis, route)


def combined_all(value, axis, combine):
    everything = jax.tree.map(lambda part: lax.all_gather(part, axis), value)
    initial = jax.tree.map(lambda part: part[0], everything)

    def turn(k, so_far):
        return combine(so_far, jax.tree.map(lambda part: part[k], everything))

    return lax.fori_loop(1, lax.axis_size(axis), turn, initial)


def attend(state, queries, key_value, visible):
    width = queries.shape[-1]
    scores = jnp.einsum(
        "rkgd,nkd->rkgn", queries, key_value[:, 0], preferred_element_type=jnp.float32
    ) * width ** (-0.5)
    if visible is not None:
        scores = jnp.where(visible[:, None, None, :], scores, NEG_FILL)
    running, total, weighted = state
    highest = jnp.maximum(running, jnp.max(scores, axis=-1))
    factor = jnp.exp(running - highest)
    weights = jnp.exp(scores - highest[..., None])
    total = total * factor + jnp.sum(weights, axis=-1)
    update = jnp.einsum(
        "rkgn,nkd->rkgd",
        weights.astype(jnp.bfloat16),
        key_value[:, 1],
        preferred_element_type=jnp.float32,
    )
    weighted = weighted * factor[..., None] + update
    return (highest, total, weighted)


def empty_state(rows, slots_local, group, width):
    return (
        jnp.full((rows, slots_local, group), -jnp.inf, jnp.float32),
        jnp.zeros((rows, slots_local, group), jnp.float32),
        jnp.zeros((rows, slots_local, group, width), jnp.float32),
    )


def combine(first, second):
    highest = jnp.maximum(first[0], second[0])
    left = jnp.exp(first[0] - highest)
    right = jnp.exp(second[0] - highest)
    return (
        highest,
        first[1] * left + second[1] * right,
        first[2] * left[..., None] + second[2] * right[..., None],
    )


def place_blocks(cache, rows_in, destination_members, slots, own_index):
    count = rows_in.shape[0] // BLK

    def put(index, current):
        spot = slots[index] * BLK
        incoming = lax.dynamic_slice_in_dim(rows_in, index * BLK, BLK, 0)
        present = lax.dynamic_slice_in_dim(current, spot, BLK, 0)
        chosen = jnp.where(destination_members[index] == own_index, incoming, present)
        return lax.dynamic_update_slice_in_dim(current, chosen, spot, 0)

    return lax.fori_loop(0, count, put, cache)


def destinations(segment_destination_member, remaining_instance_ids):
    sequence = segment_destination_member[:, 0]
    agreement = (
        sequence[:, None]
        == jnp.arange(remaining_instance_ids.shape[0], dtype=jnp.int32)[None, :]
    ).astype(jnp.int32)
    slots = jnp.sum(jnp.cumsum(agreement, axis=0) * agreement, axis=1) - 1
    members = jnp.sum(agreement * remaining_instance_ids[None, :], axis=1)
    return slots, members


def on_device_ring(
    fresh_segment_probes,
    fresh_segment_pairs,
    earlier_stored_pairs,
    emitted_token_probe,
    emitted_token_pair,
    final_projection_weights,
    remaining_instance_ids,
    segment_destination_member,
):
    own_index = lax.axis_index("inst")
    instances = lax.axis_size("inst")
    rows, heads, width = fresh_segment_probes.shape
    slots_local = fresh_segment_pairs.shape[2]
    group = heads // slots_local
    queries = fresh_segment_probes.reshape(rows, slots_local, group, width)
    slots, destination_members = destinations(segment_destination_member, remaining_instance_ids)
    held_blocks = jnp.sum((destination_members == own_index).astype(jnp.int32))
    cache = jnp.zeros((CAP * BLK, 2, slots_local, width), jnp.bfloat16)
    causal = jnp.arange(rows)[:, None] >= jnp.arange(rows)[None, :]
    state = attend(
        empty_state(rows, slots_local, group, width), queries, earlier_stored_pairs, None
    )
    state = attend(state, queries, fresh_segment_pairs, causal)
    moving = jnp.concatenate([fresh_segment_pairs, earlier_stored_pairs], axis=0)

    def turn_both(step, carry):
        moving, state, current = carry
        moving = from_behind(moving, "inst", 1)
        source = (own_index - step) % instances
        state = attend(state, queries, moving[rows:], None)
        visible = jnp.broadcast_to(source < own_index, (rows, rows))
        state = attend(state, queries, moving[:rows], visible)
        return (moving, state, current)

    moving, state, cache = lax.fori_loop(1, instances, turn_both, (moving, state, cache))
    cache = place_blocks(
        cache,
        lax.all_gather(fresh_segment_pairs, "inst", axis=0, tiled=True),
        destination_members,
        slots,
        own_index,
    )
    attention = (state[2] / state[1][..., None]).astype(jnp.bfloat16).reshape(rows, heads * width)
    terms = jnp.dot(
        attention,
        lax.all_gather(final_projection_weights, "inst", axis=1, tiled=True),
        preferred_element_type=jnp.float32,
    )
    span_hidden = lax.psum_scatter(
        terms.astype(jnp.bfloat16), "tp", scatter_dimension=1, tiled=True
    )
    single = emitted_token_probe.reshape(1, slots_local, group, width)
    decode_state = attend(
        empty_state(1, slots_local, group, width), single, earlier_stored_pairs, None
    )
    live = (jnp.arange(CAP * BLK) < held_blocks * BLK)[None, :]
    decode_state = attend(decode_state, single, cache, live)
    merged = combined_all((decode_state[0], decode_state[1], decode_state[2]), "inst", combine)
    own_scores = jnp.einsum(
        "rkgd,kd->rkg", single, emitted_token_pair[0], preferred_element_type=jnp.float32
    ) * width ** (-0.5)
    highest = jnp.maximum(merged[0], own_scores)
    left = jnp.exp(merged[0] - highest)
    right = jnp.exp(own_scores - highest)
    total = merged[1] * left + right
    own_weight = lax.optimization_barrier(right.astype(jnp.bfloat16)).astype(jnp.float32)
    own_value = emitted_token_pair[1].astype(jnp.float32)
    weighted = merged[2] * left[..., None] + own_weight[..., None] * own_value[None, :, None, :]
    decode_attention = (weighted / total[..., None]).astype(jnp.bfloat16).reshape(heads, width)
    return (span_hidden, cache[None], decode_attention)


def swapped(value, axis, distance):
    size = lax.axis_size(axis)
    return lax.ppermute(value, axis, [(i, i ^ distance) for i in range(size)])


def vmem(count=1):
    return [pl.BlockSpec(memory_space=pltpu.VMEM)] * count


def smem(count=1):
    return [pl.BlockSpec(memory_space=pltpu.SMEM)] * count


def hbm(count=1):
    return [pl.BlockSpec(memory_space=pltpu.HBM)] * count


def anywhere(count=1):
    return [pl.BlockSpec(memory_space=pl.ANY)] * count


def split_pairs_kernel(away, me, fresh, prefix, out):
    rows = fresh.shape[0]
    for y in range(2):

        @pl.when(me[0] >> 2 == y)
        def _():
            s = y ^ away
            for part, start in ((fresh, 0), (prefix, rows)):
                size = part.shape[0]
                out[1, start : start + size] = part[:, 1, s, :]
                for at in range(0, size, BLK):
                    block = part[at : at + BLK, 0, s, :]
                    out[0, start + at : start + at + BLK] = block.T


def split_pairs(away, me, fresh, prefix, after):
    def kernel(me, fresh, prefix, *refs):
        split_pairs_kernel(away, me, fresh, prefix, refs[-1])

    held, width = fresh.shape[0] + prefix.shape[0], fresh.shape[3]
    return pl.pallas_call(
        kernel,
        out_shape=jax.ShapeDtypeStruct((2, held, width), jnp.bfloat16),
        in_specs=smem() + vmem(2) + anywhere(len(after)),
        out_specs=vmem()[0],
        compiler_params=pltpu.CompilerParams(vmem_limit_bytes=24 * 1024 * 1024),
        name="split_pairs",
    )(me, fresh, prefix, *after)


def split_queries_kernel(group, me, queries, own_ref, send_ref):
    chunk_rows = queries.shape[0] // CHUNKS

    def place(out, s):
        for k in range(CHUNKS):
            for g in range(group):
                out[k, g * chunk_rows : (g + 1) * chunk_rows] = queries[
                    k * chunk_rows : (k + 1) * chunk_rows, s * group + g, :
                ]

    for y in range(2):

        @pl.when(me[0] >> 2 == y)
        def _():
            place(own_ref, y)
            place(send_ref, 1 - y)


def split_queries(me, queries, after):
    rows, heads, width = queries.shape
    group = heads // 2
    probes = jax.ShapeDtypeStruct((CHUNKS, group * rows // CHUNKS, width), jnp.bfloat16)

    def kernel(me, queries, *refs):
        split_queries_kernel(group, me, queries, *refs[-2:])

    return pl.pallas_call(
        kernel,
        out_shape=[probes, probes],
        in_specs=smem() + vmem() + anywhere(len(after)),
        out_specs=vmem(2),
        compiler_params=pltpu.CompilerParams(vmem_limit_bytes=24 * 1024 * 1024),
        name="split_queries",
    )(me, queries, *after)


EARLY = (0, 1, 4, 5, 2, 3)
LATE = (6, 7)


def prefix_copies(n, piece, rows, keys, values, sems):
    tile = piece.shape[1] - rows
    at = pl.multiple_of(n * tile, tile)
    return [
        pltpu.make_async_copy(
            piece.at[j, pl.ds(rows, tile)], target.at[pl.ds(at, tile)], sems.at[n, j]
        )
        for j, target in enumerate((keys, values))
    ]


class Tiles:
    def __init__(self, tile, scale, queries, keys, values, weights, shift, sums, weighted):
        self.tile, self.part, self.scale = tile, 2 * BLK, scale
        self.queries, self.keys, self.values = queries, keys, values
        self.weights, self.shift, self.sums, self.weighted = weights, shift, sums, weighted

    def scores(self, t, j, rows):
        at = pl.multiple_of(t * self.tile + j * self.part, self.part)
        block = jnp.concatenate(
            [self.keys[pl.ds(at + l, BLK), :] for l in range(0, self.part, BLK)], axis=1
        )
        return jnp.dot(self.queries[pl.ds(*rows)], block, preferred_element_type=jnp.float32)

    def above(self, t, j, rows, latest):
        width = self.shift.shape[1]
        value, shift = self.scores(t, j, rows), self.shift[pl.ds(*rows)]
        blocks = [value[:, l : l + width] - shift for l in range(0, self.part, width)]
        if latest is None:
            return blocks
        column = lax.broadcasted_iota(jnp.int32, blocks[0].shape, 1)
        return [
            jnp.where(column <= latest - (j * self.part + l * width), block, NEG_FILL)
            for l, block in enumerate(blocks)
        ]

    def weigh(self, t, slot, j, rows, latest):
        width = self.shift.shape[1]
        total = self.sums[pl.ds(*rows)]
        for l, block in enumerate(self.above(t, j, rows, latest)):
            weight = jnp.exp2(block * self.scale)
            total += weight
            at = j * self.part + l * width
            self.weights[slot][pl.ds(*rows), at : at + width] = weight.astype(jnp.bfloat16)
        self.sums[pl.ds(*rows)] = total

    def add(self, t, slot, rows):
        at = pl.multiple_of(t * self.tile, self.tile)
        self.weighted[pl.ds(*rows)] += jnp.dot(
            self.weights[slot][pl.ds(*rows)],
            self.values[pl.ds(at, self.tile), :],
            preferred_element_type=jnp.float32,
        )

    def peak(self, t, rows, latest=None, shifted=True):
        width = self.shift.shape[1]
        peak = None
        for j in range(self.tile // self.part):
            if shifted:
                blocks = self.above(t, j, rows, latest)
            else:
                value = self.scores(t, j, rows)
                blocks = [value[:, l : l + width] for l in range(0, self.part, width)]
            for block in blocks:
                peak = block if peak is None else jnp.maximum(peak, block)
        return jnp.max(peak, axis=1, keepdims=True)

    def first(self, rows):
        top = self.peak(0, rows, shifted=False)
        self.shift[pl.ds(*rows)] = jnp.broadcast_to(top, (rows[1], self.shift.shape[1]))
        for name in (self.sums, self.weighted):
            name[pl.ds(*rows)] = jnp.zeros((rows[1], name.shape[1]), jnp.float32)
        for j in range(self.tile // self.part):
            self.weigh(0, 0, j, rows, None)

    def turn(self, t, slot, rows, latest, before):
        parts = self.tile // self.part
        for j in range(parts):
            self.weigh(t, slot, j, rows, latest)
            for n, side in enumerate(before):
                if n * parts // len(before) == j:
                    self.add(t - 1, 1 - slot, side)

    def careful(self, t, rows, latest):
        up = jnp.maximum(self.peak(t, rows, latest), 0.0)
        factor = jnp.exp2(-up * self.scale)
        self.weighted[pl.ds(*rows)] *= factor
        self.sums[pl.ds(*rows)] *= factor
        self.shift[pl.ds(*rows)] += up
        for j in range(self.tile // self.part):
            self.weigh(t, 0, j, rows, latest)
        self.add(t, 0, rows)


def early_kernel(rows, scale, q_ref, *refs):
    pieces = refs[: len(EARLY)]
    shift, sums, weighted, queries, keys, values, even, odd, sems = refs[len(EARLY) :]
    count, half, _ = q_ref.shape
    tile = pieces[0].shape[1] - rows
    copies = [
        prefix_copies(n, piece, rows, keys, values, sems) for n, piece in enumerate(pieces)
    ]

    @pl.when(pl.program_id(0) == 0)
    def _():
        for pair in copies:
            for copy in pair:
                copy.start()

    for n in range(count):
        queries[n * half : (n + 1) * half] = q_ref[n]

    @pl.when(pl.program_id(0) == 0)
    def _():
        for pair in copies:
            for copy in pair:
                copy.wait()

    tiles = Tiles(tile, scale, queries, keys, values, (even, odd), shift, sums, weighted)
    everything = (0, count * half)
    halves = [(n * half, half) for n in range(count)]
    tiles.first(everything)

    def pair(u, carry):
        tiles.turn(2 * u + 1, 1, everything, None, halves)
        tiles.turn(2 * u + 2, 0, everything, None, halves)
        return carry

    lax.fori_loop(0, 2, pair, 0)
    tiles.turn(5, 1, everything, None, halves)
    for side in halves:
        tiles.add(5, 1, side)


def early_attention(queries, pieces, rows):
    chunks, half, width = queries.shape
    held = pieces[0].shape[1]
    tile = held - rows
    step = 2
    state = jax.ShapeDtypeStruct((chunks * half, width), jnp.float32)
    size = step * half
    keys = len(EARLY) * tile
    return pl.pallas_call(
        functools.partial(early_kernel, rows, width ** (-0.5) * LOG2E),
        grid=(chunks // step,),
        out_shape=[state] * 3,
        in_specs=[pl.BlockSpec((step, half, width), lambda i: (i, 0, 0))] + hbm(len(EARLY)),
        out_specs=[pl.BlockSpec((size, width), lambda i: (i, 0))] * 3,
        scratch_shapes=[
            pltpu.VMEM((size, width), jnp.bfloat16),
            pltpu.VMEM((keys, width), jnp.bfloat16),
            pltpu.VMEM((keys, width), jnp.bfloat16),
            pltpu.VMEM((size, tile), jnp.bfloat16),
            pltpu.VMEM((size, tile), jnp.bfloat16),
            pltpu.SemaphoreType.DMA((len(EARLY), 2)),
        ],
        compiler_params=pltpu.CompilerParams(vmem_limit_bytes=24 * 1024 * 1024),
        cost_estimate=pl.CostEstimate(
            flops=2 * 2 * chunks * half * keys * width * 2,
            bytes_accessed=keys * width * 4 + 3 * chunks * half * width * 4,
            transcendentals=chunks * half * keys,
        ),
        name="early_attention",
    )(queries, *[pieces[p] for p in EARLY])


def attention_kernel(waits, chunk, chunk_rows, rows, group, scale, me, own, beside, *refs):
    states, pieces = refs[:3], refs[3:11]
    out_ref = refs[11 + waits]
    queries, keys, values, even, odd, shift, sums, weighted, sems, late_sems = refs[12 + waits :]
    half = own.shape[1]
    held, width = pieces[0].shape[1:]
    tile = held - rows
    y = me[0] >> 2
    own_rows = (pl.multiple_of(y * half, half), half)
    beside_rows = (pl.multiple_of((1 - y) * half, half), half)
    low, high, everything = (0, half), (half, half), (0, 2 * half)
    order = EARLY + LATE

    def fresh_copies(p):
        at = pl.multiple_of(8 * tile + (me[0] ^ p) * rows, rows)
        return [
            pltpu.make_async_copy(
                pieces[p].at[j, pl.ds(0, rows)], target.at[pl.ds(at, rows)], sems.at[p, 2 + j]
            )
            for j, target in enumerate((keys, values))
        ]

    query_copies = [
        pltpu.make_async_copy(source.at[chunk], queries.at[pl.ds(*place)], late_sems.at[n])
        for n, (source, place) in enumerate(((own, own_rows), (beside, beside_rows)))
    ]
    state_copies = [
        pltpu.make_async_copy(
            source.at[pl.ds(chunk * half, half)], target.at[pl.ds(*own_rows)], late_sems.at[2 + n]
        )
        for n, (source, target) in enumerate(zip(states, (shift, sums, weighted)))
    ]
    copies = [prefix_copies(n, pieces[p], rows, keys, values, sems) for n, p in enumerate(order)]
    for copy in query_copies + copies[0] + state_copies:
        copy.start()
    for pair in copies[1:]:
        for copy in pair:
            copy.start()
    for p in range(8):
        for copy in fresh_copies(p):
            copy.start()

    def wait_for(n):
        for copy in prefix_copies(n, pieces[0], rows, keys, values, sems):
            copy.wait()

    tiles = Tiles(tile, scale, queries, keys, values, (even, odd), shift, sums, weighted)
    for copy in query_copies + copies[0]:
        copy.wait()
    tiles.first(beside_rows)

    def pair(u, carry):
        wait_for(2 * u + 1)
        tiles.turn(2 * u + 1, 1, beside_rows, None, [beside_rows])
        wait_for(2 * u + 2)
        tiles.turn(2 * u + 2, 0, beside_rows, None, [beside_rows])
        return carry

    lax.fori_loop(0, 2, pair, 0)
    wait_for(5)
    tiles.turn(5, 1, beside_rows, None, [beside_rows])
    wait_for(6)
    wait_for(7)
    for copy in state_copies:
        copy.wait()
    tiles.turn(6, 0, everything, None, [beside_rows])
    tiles.turn(7, 1, everything, None, [low, high])
    for p in range(8):
        for copy in fresh_copies(p):
            copy.wait()

    def latest(count):
        row = lax.broadcasted_iota(jnp.int32, (count, width), 0)
        last = (me[0] & 3) * rows + chunk * chunk_rows + row % chunk_rows
        return last if count == half else jnp.where(row < half, last, tile)

    tiles.turn(8, 0, everything, latest(2 * half), [low, high])
    tiles.turn(9, 1, high, latest(half), [low, high])
    tiles.add(9, 1, high)

    @pl.when(jnp.logical_not(jnp.max(sums[...]) < LARGEST))
    def _():
        weighted[...] = jnp.zeros(weighted.shape, jnp.float32)
        sums[...] = jnp.zeros(sums.shape, jnp.float32)

        def prefix_tile(t, carry):
            tiles.careful(t, everything, None)
            return carry

        lax.fori_loop(0, 8, prefix_tile, 0)
        tiles.careful(8, everything, latest(2 * half))
        tiles.careful(9, high, latest(half))

    for h in range(2):
        block = slice(h * half, (h + 1) * half)
        total = jnp.sum(sums[block], axis=1, keepdims=True)
        result = (weighted[block] / total).astype(jnp.bfloat16)
        for g in range(group):
            out_ref[y ^ h, :, g * width : (g + 1) * width] = result[
                g * chunk_rows : (g + 1) * chunk_rows
            ]


def chunk_attention(chunk, me, queries, states, pieces, rows, group, after):
    _, half, width = queries[0].shape
    chunk_rows = half // group
    held = pieces[0].shape[1]
    tile = held - rows
    return pl.pallas_call(
        functools.partial(
            attention_kernel,
            len(after),
            chunk,
            chunk_rows,
            rows,
            group,
            width ** (-0.5) * LOG2E,
        ),
        out_shape=jax.ShapeDtypeStruct((2, chunk_rows, group * width), jnp.bfloat16),
        in_specs=smem() + hbm(13) + anywhere(len(after)),
        out_specs=vmem()[0],
        scratch_shapes=[
            pltpu.VMEM((2 * half, width), jnp.bfloat16),
            pltpu.VMEM((8 * held, width), jnp.bfloat16),
            pltpu.VMEM((8 * held, width), jnp.bfloat16),
            pltpu.VMEM((2 * half, tile), jnp.bfloat16),
            pltpu.VMEM((2 * half, tile), jnp.bfloat16),
            pltpu.VMEM((2 * half, width), jnp.float32),
            pltpu.VMEM((2 * half, width), jnp.float32),
            pltpu.VMEM((2 * half, width), jnp.float32),
            pltpu.SemaphoreType.DMA((8, 4)),
            pltpu.SemaphoreType.DMA((5,)),
        ],
        compiler_params=pltpu.CompilerParams(vmem_limit_bytes=24 * 1024 * 1024),
        cost_estimate=pl.CostEstimate(
            flops=2 * 2 * 2 * half * 8 * held * width * 2 * 2 // 3,
            bytes_accessed=8 * held * width * 4,
            transcendentals=2 * half * 8 * held * 2 // 3,
        ),
        name="chunk_attention",
    )(me, *queries, *states, *pieces, *after)


def stack_kernel(*refs):
    parts, out, sems = refs[:4], refs[-2], refs[-1]
    copies = [
        pltpu.make_async_copy(part, out.at[r], sems.at[r]) for r, part in enumerate(parts)
    ]
    for copy in copies:
        copy.start()
    for copy in copies:
        copy.wait()


def stack(parts, after):
    return pl.pallas_call(
        stack_kernel,
        out_shape=jax.ShapeDtypeStruct((4, *parts[0].shape), jnp.bfloat16),
        in_specs=anywhere(4 + len(after)),
        out_specs=anywhere()[0],
        scratch_shapes=[pltpu.SemaphoreType.DMA((4,))],
        name="stack",
    )(*parts, *after)


def decode_kernel(scale, me, q_ref, last_ref, *refs):
    pieces, out_ref = refs[:8], refs[8]
    q = q_ref[...]
    width = q.shape[1]
    low = me[0] < 4
    last = [jnp.where(low, last_ref[j, 0:1, :], last_ref[j, 1:2, :]) for j in range(2)]
    last = [value.astype(jnp.float32) for value in last]
    running = jnp.sum(q.astype(jnp.float32) * last[0], axis=1, keepdims=True)
    total = jnp.ones_like(running)
    weighted = jnp.broadcast_to(last[1], (q.shape[0], width))
    for piece in pieces:
        scores = jnp.concatenate(
            [
                jnp.dot(q, piece[0, at : at + BLK], preferred_element_type=jnp.float32)
                for at in range(0, piece.shape[1], BLK)
            ],
            axis=1,
        )
        highest = jnp.maximum(running, jnp.max(scores, axis=1, keepdims=True))
        weights = jnp.exp2((scores - highest) * scale)
        factor = jnp.exp2((running - highest) * scale)
        total = total * factor + jnp.sum(weights, axis=1, keepdims=True)
        weighted = weighted * factor + jnp.dot(
            weights.astype(jnp.bfloat16), piece[1], preferred_element_type=jnp.float32
        )
        running = highest
    out_ref[...] = (weighted / total).astype(jnp.bfloat16)


def decode(me, query, last, pieces, after):
    width = query.shape[1]
    held = pieces[0].shape[1]

    def kernel(me, q_ref, last_ref, *refs):
        decode_kernel(width ** (-0.5) * LOG2E, me, q_ref, last_ref, *refs[:8], refs[-1])

    return pl.pallas_call(
        kernel,
        out_shape=jax.ShapeDtypeStruct(query.shape, jnp.bfloat16),
        in_specs=smem() + vmem(10) + anywhere(len(after)),
        out_specs=vmem()[0],
        compiler_params=pltpu.CompilerParams(vmem_limit_bytes=32 * 1024 * 1024),
        cost_estimate=pl.CostEstimate(
            flops=4 * query.shape[0] * width * 8 * held,
            bytes_accessed=8 * held * width * 4,
            transcendentals=query.shape[0] * 8 * held,
        ),
        name="decode",
    )(me, query, last, *pieces, *after)


def pick_kernel(rows, me, member, remaining, *refs):
    pieces, (*outs, held, sems) = refs[:8], refs[-4:]
    count = member.shape[0]
    copies = []
    for p in range(8):
        at = pl.multiple_of((me[0] ^ p) * rows, rows)
        copies.append(
            pltpu.make_async_copy(
                pieces[p].at[:, pl.ds(0, rows)], held.at[:, pl.ds(at, rows)], sems.at[p]
            )
        )
        copies[p].start()
    for out in outs:
        out[...] = jnp.zeros(out.shape, out.dtype)
    for copy in copies:
        copy.wait()
    for b in range(count):
        target = member[b, 0]
        owner = remaining[target]
        spot = jnp.int32(0)
        for before in range(b):
            spot += (member[before, 0] == target).astype(jnp.int32)
        at = pl.multiple_of(spot * BLK, BLK)
        for out, instance in zip(outs, (me[0], me[0] ^ 4)):

            @pl.when(owner == instance)
            def _():
                out[0, pl.ds(at, BLK), :] = held[0, b * BLK : (b + 1) * BLK, :].T
                out[1, pl.ds(at, BLK), :] = held[1, b * BLK : (b + 1) * BLK, :]


def pick_blocks(me, member, remaining, pieces, rows, after):
    width = pieces[0].shape[2]
    shape = jax.ShapeDtypeStruct((2, CAP * BLK, width), jnp.bfloat16)
    return pl.pallas_call(
        functools.partial(pick_kernel, rows),
        out_shape=[shape, shape],
        in_specs=smem(3) + hbm(8) + anywhere(len(after)),
        out_specs=vmem(2),
        scratch_shapes=[
            pltpu.VMEM((2, 8 * rows, width), jnp.bfloat16),
            pltpu.SemaphoreType.DMA((8,)),
        ],
        compiler_params=pltpu.CompilerParams(vmem_limit_bytes=32 * 1024 * 1024),
        name="pick_blocks",
    )(me, member, remaining, *pieces, *after)


def project_kernel(waits, slot, own, beside, across, corner, *refs):
    weights, outs = refs[:4], refs[4 + waits :]
    same = jnp.concatenate([own[0], own[1], across[0], across[1]], axis=0)
    other = jnp.concatenate([beside[1], beside[0], corner[1], corner[0]], axis=0)
    rows = own.shape[1]
    for half in range(2):
        total = jnp.dot(same, weights[2 * half][...], preferred_element_type=jnp.float32)
        total += jnp.dot(other, weights[2 * half + 1][...], preferred_element_type=jnp.float32)
        total = total.astype(jnp.bfloat16)
        for r in range(4):
            outs[r][half] = total[r * rows : (r + 1) * rows]


def project(slot, parts, own_weights, sibling_weights, after):
    _, rows, depth = parts[0].shape
    columns = own_weights.shape[1]
    tile = min(512, columns)
    whole = pl.BlockSpec((2, rows, depth), lambda j, slot: (0, 0, 0))
    same = pl.BlockSpec((depth, tile), lambda j, slot: (slot[0], j))
    other = pl.BlockSpec((depth, tile), lambda j, slot: (1 - slot[0], j))
    out = pl.BlockSpec((2, rows, tile), lambda j, slot: (0, 0, j))
    return pl.pallas_call(
        functools.partial(project_kernel, len(after)),
        grid_spec=pltpu.PrefetchScalarGridSpec(
            num_scalar_prefetch=1,
            grid=(columns // tile,),
            in_specs=[whole] * 4 + [same, other] * 2 + anywhere(len(after)),
            out_specs=[out] * 4,
        ),
        out_shape=[jax.ShapeDtypeStruct((2, rows, columns), jnp.bfloat16)] * 4,
        compiler_params=pltpu.CompilerParams(vmem_limit_bytes=26 * 1024 * 1024),
        cost_estimate=pl.CostEstimate(
            flops=2 * 4 * rows * 2 * depth * 2 * columns,
            bytes_accessed=2 * depth * 2 * columns * 2,
            transcendentals=0,
        ),
        name="project",
    )(slot, *parts, own_weights, own_weights, sibling_weights, sibling_weights, *after)


def on_device_planes(
    fresh_segment_probes,
    fresh_segment_pairs,
    earlier_stored_pairs,
    emitted_token_probe,
    emitted_token_pair,
    final_projection_weights,
    remaining_instance_ids,
    segment_destination_member,
):
    index = lax.axis_index("inst")
    slot = index // 4
    rows, heads, width = fresh_segment_probes.shape
    group = heads // 2
    me = jnp.reshape(index, (1,)).astype(jnp.int32)
    slot_array = jnp.reshape(slot, (1,)).astype(jnp.int32)
    core = index % 2

    piece = {}
    to_beside = split_pairs(1, me, fresh_segment_pairs, earlier_stored_pairs, [])
    piece[4] = swapped(to_beside, "inst", 4)
    piece[0] = split_pairs(0, me, fresh_segment_pairs, earlier_stored_pairs, [to_beside])
    piece[2] = swapped(piece[0], "inst", 2)
    queries_own, queries_send = split_queries(me, fresh_segment_probes, [piece[0]])
    queries = [queries_own, swapped(queries_send, "inst", 4)]
    piece[6] = swapped(piece[4], "inst", 2)
    for d in (0, 4, 2, 6):
        piece[d + 1] = swapped(piece[d], "inst", 1)
    pieces = [piece[d] for d in range(8)]
    sibling_weights = swapped(final_projection_weights, "inst", 1)

    states = early_attention(queries_own, pieces, rows)

    def attention(chunk, after):
        own = chunk_attention(chunk, me, queries, states, pieces, rows, group, after)
        return [own] + [swapped(own, "inst", d) for d in (4, 2, 6)]

    def projected(parts, after):
        outs = project(slot_array, parts, final_projection_weights, sibling_weights, after)
        return [outs[0]] + [swapped(outs[i], "inst", d) for i, d in ((1, 4), (2, 2), (3, 6))]

    planes = lax.axis_size("tp")
    lines = [
        [i * planes + (r ^ (i // 2)) for r in range(planes)] for i in range(lax.axis_size("inst"))
    ]

    def reduced(parts, after):
        ordered = stack([parts[0], parts[2], parts[1], parts[3]], after)
        total = lax.psum_scatter(ordered, ("inst", "tp"), axis_index_groups=lines)
        left = jnp.where(core == 0, total[0], total[1])
        right = jnp.where(core == 0, total[1], total[0])
        return jnp.concatenate([left, right], axis=1)

    gathered, partial = {}, {}
    gathered[0] = attention(0, [])
    gathered[1] = attention(1, [])
    picked_own, picked_send = pick_blocks(
        me, segment_destination_member, remaining_instance_ids, pieces, rows, [gathered[1][0]]
    )
    picked_beside = swapped(picked_send, "inst", 4)
    hidden = []
    for k in range(CHUNKS):
        after = [gathered[k + 1][0]] if k + 1 < CHUNKS else []
        partial[k] = projected(gathered[k], after)
        if k + 2 < CHUNKS:
            gathered[k + 2] = attention(k + 2, [partial[k][0], picked_own])
    for k in range(CHUNKS):
        later = gathered[k + 2][0] if k + 2 < CHUNKS else partial[CHUNKS - 1][0]
        hidden.append(reduced(partial[k], [later] if k + 1 < CHUNKS else []))
    span_hidden = jnp.concatenate(hidden, axis=0)

    first = jnp.where(slot == 0, picked_own, picked_beside)
    second = jnp.where(slot == 0, picked_beside, picked_own)
    cache = jnp.stack([first, second]).transpose(2, 1, 0, 3)

    decoded = decode(me, emitted_token_probe, emitted_token_pair, pieces, [partial[CHUNKS - 1][0]])
    decoded_beside = swapped(decoded, "inst", 4)
    mine = (jnp.arange(heads) // group == slot)[:, None]
    decode_attention = jnp.where(mine, decoded, decoded_beside)
    return (span_hidden, cache[None], decode_attention)


def solution(mesh):
    instances, groups = mesh.shape["inst"], mesh.shape["tp"]

    def on_device(*arguments):
        slots_local = arguments[1].shape[2]
        tile = arguments[2].shape[0]
        rows = arguments[1].shape[0]
        if instances == 8 and groups == 4 and slots_local == 2 and tile == 4 * rows:
            return on_device_planes(*arguments)
        return on_device_ring(*arguments)

    return jax.shard_map(
        on_device,
        mesh=mesh,
        in_specs=(
            P("inst", "tp", None),
            P("inst", None, "tp", None),
            P("inst", None, "tp", None),
            P("tp", None),
            P(None, "tp", None),
            P("tp", "inst"),
            P(),
            P(),
        ),
        out_specs=(P("inst", "tp"), P("inst", None, None, "tp", None), P("tp", None)),
        check_vma=False,
    )
```

```python
import functools

import jax
import jax.numpy as jnp
from jax import lax
from jax.experimental import pallas as pl
from jax.experimental.pallas import tpu as pltpu
from jax.sharding import PartitionSpec as P

BLK = 128
CAP = 8
NEG_FILL = -1e30
LOG2E = 1.4426950408889634
LARGEST = 2.0**100
CHUNKS = 4


def from_behind(block, axis, distance):
    devices = range(lax.axis_size(axis))
    route = [((i - distance) % len(devices), i) for i in devices]
    return lax.ppermute(block, axis, route)


def combined_all(value, axis, combine):
    everything = jax.tree.map(lambda part: lax.all_gather(part, axis), value)
    initial = jax.tree.map(lambda part: part[0], everything)

    def turn(k, so_far):
        return combine(so_far, jax.tree.map(lambda part: part[k], everything))

    return lax.fori_loop(1, lax.axis_size(axis), turn, initial)


def attend(state, queries, key_value, visible):
    width = queries.shape[-1]
    scores = jnp.einsum(
        "rkgd,nkd->rkgn", queries, key_value[:, 0], preferred_element_type=jnp.float32
    ) * width ** (-0.5)
    if visible is not None:
        scores = jnp.where(visible[:, None, None, :], scores, NEG_FILL)
    running, total, weighted = state
    highest = jnp.maximum(running, jnp.max(scores, axis=-1))
    factor = jnp.exp(running - highest)
    weights = jnp.exp(scores - highest[..., None])
    total = total * factor + jnp.sum(weights, axis=-1)
    update = jnp.einsum(
        "rkgn,nkd->rkgd",
        weights.astype(jnp.bfloat16),
        key_value[:, 1],
        preferred_element_type=jnp.float32,
    )
    weighted = weighted * factor[..., None] + update
    return (highest, total, weighted)


def empty_state(rows, slots_local, group, width):
    return (
        jnp.full((rows, slots_local, group), -jnp.inf, jnp.float32),
        jnp.zeros((rows, slots_local, group), jnp.float32),
        jnp.zeros((rows, slots_local, group, width), jnp.float32),
    )


def combine(first, second):
    highest = jnp.maximum(first[0], second[0])
    left = jnp.exp(first[0] - highest)
    right = jnp.exp(second[0] - highest)
    return (
        highest,
        first[1] * left + second[1] * right,
        first[2] * left[..., None] + second[2] * right[..., None],
    )


def place_blocks(cache, rows_in, destination_members, slots, own_index):
    count = rows_in.shape[0] // BLK

    def put(index, current):
        spot = slots[index] * BLK
        incoming = lax.dynamic_slice_in_dim(rows_in, index * BLK, BLK, 0)
        present = lax.dynamic_slice_in_dim(current, spot, BLK, 0)
        chosen = jnp.where(destination_members[index] == own_index, incoming, present)
        return lax.dynamic_update_slice_in_dim(current, chosen, spot, 0)

    return lax.fori_loop(0, count, put, cache)


def destinations(segment_destination_member, remaining_instance_ids):
    sequence = segment_destination_member[:, 0]
    agreement = (
        sequence[:, None]
        == jnp.arange(remaining_instance_ids.shape[0], dtype=jnp.int32)[None, :]
    ).astype(jnp.int32)
    slots = jnp.sum(jnp.cumsum(agreement, axis=0) * agreement, axis=1) - 1
    members = jnp.sum(agreement * remaining_instance_ids[None, :], axis=1)
    return slots, members


def on_device_ring(
    fresh_segment_probes,
    fresh_segment_pairs,
    earlier_stored_pairs,
    emitted_token_probe,
    emitted_token_pair,
    final_projection_weights,
    remaining_instance_ids,
    segment_destination_member,
):
    own_index = lax.axis_index("inst")
    instances = lax.axis_size("inst")
    rows, heads, width = fresh_segment_probes.shape
    slots_local = fresh_segment_pairs.shape[2]
    group = heads // slots_local
    queries = fresh_segment_probes.reshape(rows, slots_local, group, width)
    slots, destination_members = destinations(segment_destination_member, remaining_instance_ids)
    held_blocks = jnp.sum((destination_members == own_index).astype(jnp.int32))
    cache = jnp.zeros((CAP * BLK, 2, slots_local, width), jnp.bfloat16)
    causal = jnp.arange(rows)[:, None] >= jnp.arange(rows)[None, :]
    state = attend(
        empty_state(rows, slots_local, group, width), queries, earlier_stored_pairs, None
    )
    state = attend(state, queries, fresh_segment_pairs, causal)
    moving = jnp.concatenate([fresh_segment_pairs, earlier_stored_pairs], axis=0)

    def turn_both(step, carry):
        moving, state, current = carry
        moving = from_behind(moving, "inst", 1)
        source = (own_index - step) % instances
        state = attend(state, queries, moving[rows:], None)
        visible = jnp.broadcast_to(source < own_index, (rows, rows))
        state = attend(state, queries, moving[:rows], visible)
        return (moving, state, current)

    moving, state, cache = lax.fori_loop(1, instances, turn_both, (moving, state, cache))
    cache = place_blocks(
        cache,
        lax.all_gather(fresh_segment_pairs, "inst", axis=0, tiled=True),
        destination_members,
        slots,
        own_index,
    )
    attention = (state[2] / state[1][..., None]).astype(jnp.bfloat16).reshape(rows, heads * width)
    terms = jnp.dot(
        attention,
        lax.all_gather(final_projection_weights, "inst", axis=1, tiled=True),
        preferred_element_type=jnp.float32,
    )
    span_hidden = lax.psum_scatter(
        terms.astype(jnp.bfloat16), "tp", scatter_dimension=1, tiled=True
    )
    single = emitted_token_probe.reshape(1, slots_local, group, width)
    decode_state = attend(
        empty_state(1, slots_local, group, width), single, earlier_stored_pairs, None
    )
    live = (jnp.arange(CAP * BLK) < held_blocks * BLK)[None, :]
    decode_state = attend(decode_state, single, cache, live)
    merged = combined_all((decode_state[0], decode_state[1], decode_state[2]), "inst", combine)
    own_scores = jnp.einsum(
        "rkgd,kd->rkg", single, emitted_token_pair[0], preferred_element_type=jnp.float32
    ) * width ** (-0.5)
    highest = jnp.maximum(merged[0], own_scores)
    left = jnp.exp(merged[0] - highest)
    right = jnp.exp(own_scores - highest)
    total = merged[1] * left + right
    own_weight = lax.optimization_barrier(right.astype(jnp.bfloat16)).astype(jnp.float32)
    own_value = emitted_token_pair[1].astype(jnp.float32)
    weighted = merged[2] * left[..., None] + own_weight[..., None] * own_value[None, :, None, :]
    decode_attention = (weighted / total[..., None]).astype(jnp.bfloat16).reshape(heads, width)
    return (span_hidden, cache[None], decode_attention)


def swapped(value, axis, distance):
    size = lax.axis_size(axis)
    return lax.ppermute(value, axis, [(i, i ^ distance) for i in range(size)])


def vmem(count=1):
    return [pl.BlockSpec(memory_space=pltpu.VMEM)] * count


def smem(count=1):
    return [pl.BlockSpec(memory_space=pltpu.SMEM)] * count


def hbm(count=1):
    return [pl.BlockSpec(memory_space=pltpu.HBM)] * count


def anywhere(count=1):
    return [pl.BlockSpec(memory_space=pl.ANY)] * count


def split_pairs_kernel(away, me, fresh, prefix, out):
    rows = fresh.shape[0]
    for y in range(2):

        @pl.when(me[0] >> 2 == y)
        def _():
            s = y ^ away
            for part, start in ((fresh, 0), (prefix, rows)):
                size = part.shape[0]
                out[1, start : start + size] = part[:, 1, s, :]
                for at in range(0, size, BLK):
                    block = part[at : at + BLK, 0, s, :]
                    out[0, start + at : start + at + BLK] = block.T


def split_pairs(away, me, fresh, prefix, after):
    def kernel(me, fresh, prefix, *refs):
        split_pairs_kernel(away, me, fresh, prefix, refs[-1])

    held, width = fresh.shape[0] + prefix.shape[0], fresh.shape[3]
    return pl.pallas_call(
        kernel,
        out_shape=jax.ShapeDtypeStruct((2, held, width), jnp.bfloat16),
        in_specs=smem() + vmem(2) + anywhere(len(after)),
        out_specs=vmem()[0],
        compiler_params=pltpu.CompilerParams(vmem_limit_bytes=24 * 1024 * 1024),
        name="split_pairs",
    )(me, fresh, prefix, *after)


def split_queries_kernel(group, me, queries, own_ref, send_ref):
    chunk_rows = queries.shape[0] // CHUNKS

    def place(out, s):
        for k in range(CHUNKS):
            for g in range(group):
                out[k, g * chunk_rows : (g + 1) * chunk_rows] = queries[
                    k * chunk_rows : (k + 1) * chunk_rows, s * group + g, :
                ]

    for y in range(2):

        @pl.when(me[0] >> 2 == y)
        def _():
            place(own_ref, y)
            place(send_ref, 1 - y)


def split_queries(me, queries, after):
    rows, heads, width = queries.shape
    group = heads // 2
    probes = jax.ShapeDtypeStruct((CHUNKS, group * rows // CHUNKS, width), jnp.bfloat16)

    def kernel(me, queries, *refs):
        split_queries_kernel(group, me, queries, *refs[-2:])

    return pl.pallas_call(
        kernel,
        out_shape=[probes, probes],
        in_specs=smem() + vmem() + anywhere(len(after)),
        out_specs=vmem(2),
        compiler_params=pltpu.CompilerParams(vmem_limit_bytes=24 * 1024 * 1024),
        name="split_queries",
    )(me, queries, *after)


EARLY = (0, 1, 4, 5, 2, 3)
LATE = (6, 7)


def prefix_copies(n, piece, rows, keys, values, sems):
    tile = piece.shape[1] - rows
    at = pl.multiple_of(n * tile, tile)
    return [
        pltpu.make_async_copy(
            piece.at[j, pl.ds(rows, tile)], target.at[pl.ds(at, tile)], sems.at[n, j]
        )
        for j, target in enumerate((keys, values))
    ]


class Tiles:
    def __init__(self, tile, scale, queries, keys, values, weights, shift, sums, weighted):
        self.tile, self.part, self.scale = tile, 2 * BLK, scale
        self.queries, self.keys, self.values = queries, keys, values
        self.weights, self.shift, self.sums, self.weighted = weights, shift, sums, weighted

    def scores(self, t, j, rows):
        at = pl.multiple_of(t * self.tile + j * self.part, self.part)
        block = jnp.concatenate(
            [self.keys[pl.ds(at + l, BLK), :] for l in range(0, self.part, BLK)], axis=1
        )
        return jnp.dot(self.queries[pl.ds(*rows)], block, preferred_element_type=jnp.float32)

    def above(self, t, j, rows, latest):
        width = self.shift.shape[1]
        value, shift = self.scores(t, j, rows), self.shift[pl.ds(*rows)]
        blocks = [value[:, l : l + width] - shift for l in range(0, self.part, width)]
        if latest is None:
            return blocks
        column = lax.broadcasted_iota(jnp.int32, blocks[0].shape, 1)
        return [
            jnp.where(column <= latest - (j * self.part + l * width), block, NEG_FILL)
            for l, block in enumerate(blocks)
        ]

    def weigh(self, t, slot, j, rows, latest):
        width = self.shift.shape[1]
        total = self.sums[pl.ds(*rows)]
        for l, block in enumerate(self.above(t, j, rows, latest)):
            weight = jnp.exp2(block * self.scale)
            total += weight
            at = j * self.part + l * width
            self.weights[slot][pl.ds(*rows), at : at + width] = weight.astype(jnp.bfloat16)
        self.sums[pl.ds(*rows)] = total

    def add(self, t, slot, rows):
        at = pl.multiple_of(t * self.tile, self.tile)
        self.weighted[pl.ds(*rows)] += jnp.dot(
            self.weights[slot][pl.ds(*rows)],
            self.values[pl.ds(at, self.tile), :],
            preferred_element_type=jnp.float32,
        )

    def peak(self, t, rows, latest=None, shifted=True):
        width = self.shift.shape[1]
        peak = None
        for j in range(self.tile // self.part):
            if shifted:
                blocks = self.above(t, j, rows, latest)
            else:
                value = self.scores(t, j, rows)
                blocks = [value[:, l : l + width] for l in range(0, self.part, width)]
            for block in blocks:
                peak = block if peak is None else jnp.maximum(peak, block)
        return jnp.max(peak, axis=1, keepdims=True)

    def first(self, rows):
        top = self.peak(0, rows, shifted=False)
        self.shift[pl.ds(*rows)] = jnp.broadcast_to(top, (rows[1], self.shift.shape[1]))
        for name in (self.sums, self.weighted):
            name[pl.ds(*rows)] = jnp.zeros((rows[1], name.shape[1]), jnp.float32)
        for j in range(self.tile // self.part):
            self.weigh(0, 0, j, rows, None)

    def turn(self, t, slot, rows, latest, before):
        parts = self.tile // self.part
        for j in range(parts):
            self.weigh(t, slot, j, rows, latest)
            for n, side in enumerate(before):
                if n * parts // len(before) == j:
                    self.add(t - 1, 1 - slot, side)

    def careful(self, t, rows, latest):
        up = jnp.maximum(self.peak(t, rows, latest), 0.0)
        factor = jnp.exp2(-up * self.scale)
        self.weighted[pl.ds(*rows)] *= factor
        self.sums[pl.ds(*rows)] *= factor
        self.shift[pl.ds(*rows)] += up
        for j in range(self.tile // self.part):
            self.weigh(t, 0, j, rows, latest)
        self.add(t, 0, rows)


def early_kernel(rows, scale, q_ref, *refs):
    pieces = refs[: len(EARLY)]
    shift, sums, weighted, queries, keys, values, even, odd, sems = refs[len(EARLY) :]
    count, half, _ = q_ref.shape
    tile = pieces[0].shape[1] - rows
    copies = [
        prefix_copies(n, piece, rows, keys, values, sems) for n, piece in enumerate(pieces)
    ]

    @pl.when(pl.program_id(0) == 0)
    def _():
        for pair in copies:
            for copy in pair:
                copy.start()

    for n in range(count):
        queries[n * half : (n + 1) * half] = q_ref[n]

    @pl.when(pl.program_id(0) == 0)
    def _():
        for pair in copies:
            for copy in pair:
                copy.wait()

    tiles = Tiles(tile, scale, queries, keys, values, (even, odd), shift, sums, weighted)
    everything = (0, count * half)
    halves = [(n * half, half) for n in range(count)]
    tiles.first(everything)

    def pair(u, carry):
        tiles.turn(2 * u + 1, 1, everything, None, halves)
        tiles.turn(2 * u + 2, 0, everything, None, halves)
        return carry

    lax.fori_loop(0, 2, pair, 0)
    tiles.turn(5, 1, everything, None, halves)
    for side in halves:
        tiles.add(5, 1, side)


def early_attention(queries, pieces, rows):
    chunks, half, width = queries.shape
    held = pieces[0].shape[1]
    tile = held - rows
    step = 2
    state = jax.ShapeDtypeStruct((chunks * half, width), jnp.float32)
    size = step * half
    keys = len(EARLY) * tile
    return pl.pallas_call(
        functools.partial(early_kernel, rows, width ** (-0.5) * LOG2E),
        grid=(chunks // step,),
        out_shape=[state] * 3,
        in_specs=[pl.BlockSpec((step, half, width), lambda i: (i, 0, 0))] + hbm(len(EARLY)),
        out_specs=[pl.BlockSpec((size, width), lambda i: (i, 0))] * 3,
        scratch_shapes=[
            pltpu.VMEM((size, width), jnp.bfloat16),
            pltpu.VMEM((keys, width), jnp.bfloat16),
            pltpu.VMEM((keys, width), jnp.bfloat16),
            pltpu.VMEM((size, tile), jnp.bfloat16),
            pltpu.VMEM((size, tile), jnp.bfloat16),
            pltpu.SemaphoreType.DMA((len(EARLY), 2)),
        ],
        compiler_params=pltpu.CompilerParams(vmem_limit_bytes=24 * 1024 * 1024),
        cost_estimate=pl.CostEstimate(
            flops=2 * 2 * chunks * half * keys * width * 2,
            bytes_accessed=keys * width * 4 + 3 * chunks * half * width * 4,
            transcendentals=chunks * half * keys,
        ),
        name="early_attention",
    )(queries, *[pieces[p] for p in EARLY])


def attention_kernel(waits, chunk, chunk_rows, rows, group, scale, me, own, beside, *refs):
    states, pieces = refs[:3], refs[3:11]
    out_ref = refs[11 + waits]
    queries, keys, values, even, odd, shift, sums, weighted, sems, late_sems = refs[12 + waits :]
    half = own.shape[1]
    held, width = pieces[0].shape[1:]
    tile = held - rows
    y = me[0] >> 2
    own_rows = (pl.multiple_of(y * half, half), half)
    beside_rows = (pl.multiple_of((1 - y) * half, half), half)
    low, high, everything = (0, half), (half, half), (0, 2 * half)
    order = EARLY + LATE

    def fresh_copies(p):
        at = pl.multiple_of(8 * tile + (me[0] ^ p) * rows, rows)
        return [
            pltpu.make_async_copy(
                pieces[p].at[j, pl.ds(0, rows)], target.at[pl.ds(at, rows)], sems.at[p, 2 + j]
            )
            for j, target in enumerate((keys, values))
        ]

    query_copies = [
        pltpu.make_async_copy(source.at[chunk], queries.at[pl.ds(*place)], late_sems.at[n])
        for n, (source, place) in enumerate(((own, own_rows), (beside, beside_rows)))
    ]
    state_copies = [
        pltpu.make_async_copy(
            source.at[pl.ds(chunk * half, half)], target.at[pl.ds(*own_rows)], late_sems.at[2 + n]
        )
        for n, (source, target) in enumerate(zip(states, (shift, sums, weighted)))
    ]
    copies = [prefix_copies(n, pieces[p], rows, keys, values, sems) for n, p in enumerate(order)]
    for copy in query_copies + copies[0] + state_copies:
        copy.start()
    for pair in copies[1:]:
        for copy in pair:
            copy.start()
    for p in range(8):
        for copy in fresh_copies(p):
            copy.start()

    def wait_for(n):
        for copy in prefix_copies(n, pieces[0], rows, keys, values, sems):
            copy.wait()

    tiles = Tiles(tile, scale, queries, keys, values, (even, odd), shift, sums, weighted)
    for copy in query_copies + copies[0]:
        copy.wait()
    tiles.first(beside_rows)

    def pair(u, carry):
        wait_for(2 * u + 1)
        tiles.turn(2 * u + 1, 1, beside_rows, None, [beside_rows])
        wait_for(2 * u + 2)
        tiles.turn(2 * u + 2, 0, beside_rows, None, [beside_rows])
        return carry

    lax.fori_loop(0, 2, pair, 0)
    wait_for(5)
    tiles.turn(5, 1, beside_rows, None, [beside_rows])
    wait_for(6)
    wait_for(7)
    for copy in state_copies:
        copy.wait()
    tiles.turn(6, 0, everything, None, [beside_rows])
    tiles.turn(7, 1, everything, None, [low, high])
    for p in range(8):
        for copy in fresh_copies(p):
            copy.wait()

    def latest(count):
        row = lax.broadcasted_iota(jnp.int32, (count, width), 0)
        last = (me[0] & 3) * rows + chunk * chunk_rows + row % chunk_rows
        return last if count == half else jnp.where(row < half, last, tile)

    tiles.turn(8, 0, everything, latest(2 * half), [low, high])
    tiles.turn(9, 1, high, latest(half), [low, high])
    tiles.add(9, 1, high)

    @pl.when(jnp.logical_not(jnp.max(sums[...]) < LARGEST))
    def _():
        weighted[...] = jnp.zeros(weighted.shape, jnp.float32)
        sums[...] = jnp.zeros(sums.shape, jnp.float32)

        def prefix_tile(t, carry):
            tiles.careful(t, everything, None)
            return carry

        lax.fori_loop(0, 8, prefix_tile, 0)
        tiles.careful(8, everything, latest(2 * half))
        tiles.careful(9, high, latest(half))

    for h in range(2):
        block = slice(h * half, (h + 1) * half)
        total = jnp.sum(sums[block], axis=1, keepdims=True)
        result = (weighted[block] / total).astype(jnp.bfloat16)
        for g in range(group):
            out_ref[y ^ h, :, g * width : (g + 1) * width] = result[
                g * chunk_rows : (g + 1) * chunk_rows
            ]


def chunk_attention(chunk, me, queries, states, pieces, rows, group, after):
    _, half, width = queries[0].shape
    chunk_rows = half // group
    held = pieces[0].shape[1]
    tile = held - rows
    return pl.pallas_call(
        functools.partial(
            attention_kernel,
            len(after),
            chunk,
            chunk_rows,
            rows,
            group,
            width ** (-0.5) * LOG2E,
        ),
        out_shape=jax.ShapeDtypeStruct((2, chunk_rows, group * width), jnp.bfloat16),
        in_specs=smem() + hbm(13) + anywhere(len(after)),
        out_specs=vmem()[0],
        scratch_shapes=[
            pltpu.VMEM((2 * half, width), jnp.bfloat16),
            pltpu.VMEM((8 * held, width), jnp.bfloat16),
            pltpu.VMEM((8 * held, width), jnp.bfloat16),
            pltpu.VMEM((2 * half, tile), jnp.bfloat16),
            pltpu.VMEM((2 * half, tile), jnp.bfloat16),
            pltpu.VMEM((2 * half, width), jnp.float32),
            pltpu.VMEM((2 * half, width), jnp.float32),
            pltpu.VMEM((2 * half, width), jnp.float32),
            pltpu.SemaphoreType.DMA((8, 4)),
            pltpu.SemaphoreType.DMA((5,)),
        ],
        compiler_params=pltpu.CompilerParams(vmem_limit_bytes=24 * 1024 * 1024),
        cost_estimate=pl.CostEstimate(
            flops=2 * 2 * 2 * half * 8 * held * width * 2 * 2 // 3,
            bytes_accessed=8 * held * width * 4,
            transcendentals=2 * half * 8 * held * 2 // 3,
        ),
        name="chunk_attention",
    )(me, *queries, *states, *pieces, *after)


def away_kernel(offset, here, across, beside, corner, *refs):
    send_ref = refs[-1]

    @pl.when(offset[0] % 2 == 0)
    def _():
        send_ref[0] = across[...]
        send_ref[1] = corner[...]

    @pl.when(offset[0] % 2 == 1)
    def _():
        send_ref[0] = here[...]
        send_ref[1] = beside[...]


def away(offset, parts, after):
    return pl.pallas_call(
        away_kernel,
        out_shape=jax.ShapeDtypeStruct((2, *parts[0].shape), jnp.bfloat16),
        in_specs=smem() + vmem(4) + anywhere(len(after)),
        out_specs=vmem()[0],
        name="away",
    )(offset, *parts, *after)


def merge_kernel(offset, here, across, beside, corner, came, *refs):
    keep_ref, send_ref = refs[-2:]
    sides = ((here, across), (beside, corner))
    for low in range(2):
        for high in range(2):

            @pl.when(offset[0] == low + 2 * high)
            def _():
                for r, target in ((high, keep_ref), (1 - high, send_ref)):
                    total = sides[r][low][...].astype(jnp.float32) + came[r].astype(jnp.float32)
                    target[...] = total.astype(target.dtype)


def merge(offset, parts, came, after):
    return pl.pallas_call(
        merge_kernel,
        out_shape=[
            jax.ShapeDtypeStruct(parts[0].shape, jnp.float32),
            jax.ShapeDtypeStruct(parts[0].shape, jnp.bfloat16),
        ],
        in_specs=smem() + vmem(5) + anywhere(len(after)),
        out_specs=vmem(2),
        name="merge",
    )(offset, *parts, came, *after)


def finish_kernel(me, keep, came, *refs):
    out_ref = refs[-1]
    columns = keep.shape[2]
    for half in range(2):
        at = pl.multiple_of(((me[0] & 1) ^ half) * columns, columns)
        total = keep[half] + came[half].astype(jnp.float32)
        out_ref[:, pl.ds(at, columns)] = total.astype(out_ref.dtype)


def finish(chunk, me, keep, came, so_far):
    _, rows, columns = keep.shape
    whole = pl.BlockSpec(keep.shape, lambda i: (0, 0, 0))
    operands = [me, keep, came]
    specs = smem() + [whole] * 2
    aliases = {}
    if so_far is not None:
        aliases = {len(operands): 0}
        operands.append(so_far)
        specs += anywhere()
    return pl.pallas_call(
        finish_kernel,
        grid=(1,),
        out_shape=jax.ShapeDtypeStruct((CHUNKS * rows, 2 * columns), jnp.bfloat16),
        in_specs=specs,
        out_specs=pl.BlockSpec((rows, 2 * columns), lambda i: (chunk, 0)),
        input_output_aliases=aliases,
        name="finish",
    )(*operands)


def decode_kernel(scale, me, q_ref, last_ref, *refs):
    pieces, out_ref = refs[:8], refs[8]
    q = q_ref[...]
    width = q.shape[1]
    low = me[0] < 4
    last = [jnp.where(low, last_ref[j, 0:1, :], last_ref[j, 1:2, :]) for j in range(2)]
    last = [value.astype(jnp.float32) for value in last]
    running = jnp.sum(q.astype(jnp.float32) * last[0], axis=1, keepdims=True)
    total = jnp.ones_like(running)
    weighted = jnp.broadcast_to(last[1], (q.shape[0], width))
    for piece in pieces:
        scores = jnp.concatenate(
            [
                jnp.dot(q, piece[0, at : at + BLK], preferred_element_type=jnp.float32)
                for at in range(0, piece.shape[1], BLK)
            ],
            axis=1,
        )
        highest = jnp.maximum(running, jnp.max(scores, axis=1, keepdims=True))
        weights = jnp.exp2((scores - highest) * scale)
        factor = jnp.exp2((running - highest) * scale)
        total = total * factor + jnp.sum(weights, axis=1, keepdims=True)
        weighted = weighted * factor + jnp.dot(
            weights.astype(jnp.bfloat16), piece[1], preferred_element_type=jnp.float32
        )
        running = highest
    out_ref[...] = (weighted / total).astype(jnp.bfloat16)


def decode(me, query, last, pieces, after):
    width = query.shape[1]
    held = pieces[0].shape[1]

    def kernel(me, q_ref, last_ref, *refs):
        decode_kernel(width ** (-0.5) * LOG2E, me, q_ref, last_ref, *refs[:8], refs[-1])

    return pl.pallas_call(
        kernel,
        out_shape=jax.ShapeDtypeStruct(query.shape, jnp.bfloat16),
        in_specs=smem() + vmem(10) + anywhere(len(after)),
        out_specs=vmem()[0],
        compiler_params=pltpu.CompilerParams(vmem_limit_bytes=32 * 1024 * 1024),
        cost_estimate=pl.CostEstimate(
            flops=4 * query.shape[0] * width * 8 * held,
            bytes_accessed=8 * held * width * 4,
            transcendentals=query.shape[0] * 8 * held,
        ),
        name="decode",
    )(me, query, last, *pieces, *after)


def pick_kernel(rows, me, member, remaining, *refs):
    pieces, (*outs, held, sems) = refs[:8], refs[-4:]
    count = member.shape[0]
    copies = []
    for p in range(8):
        at = pl.multiple_of((me[0] ^ p) * rows, rows)
        copies.append(
            pltpu.make_async_copy(
                pieces[p].at[:, pl.ds(0, rows)], held.at[:, pl.ds(at, rows)], sems.at[p]
            )
        )
        copies[p].start()
    for out in outs:
        out[...] = jnp.zeros(out.shape, out.dtype)
    for copy in copies:
        copy.wait()
    for b in range(count):
        target = member[b, 0]
        owner = remaining[target]
        spot = jnp.int32(0)
        for before in range(b):
            spot += (member[before, 0] == target).astype(jnp.int32)
        at = pl.multiple_of(spot * BLK, BLK)
        for out, instance in zip(outs, (me[0], me[0] ^ 4)):

            @pl.when(owner == instance)
            def _():
                out[0, pl.ds(at, BLK), :] = held[0, b * BLK : (b + 1) * BLK, :].T
                out[1, pl.ds(at, BLK), :] = held[1, b * BLK : (b + 1) * BLK, :]


def pick_blocks(me, member, remaining, pieces, rows, after):
    width = pieces[0].shape[2]
    shape = jax.ShapeDtypeStruct((2, CAP * BLK, width), jnp.bfloat16)
    return pl.pallas_call(
        functools.partial(pick_kernel, rows),
        out_shape=[shape, shape],
        in_specs=smem(3) + hbm(8) + anywhere(len(after)),
        out_specs=vmem(2),
        scratch_shapes=[
            pltpu.VMEM((2, 8 * rows, width), jnp.bfloat16),
            pltpu.SemaphoreType.DMA((8,)),
        ],
        compiler_params=pltpu.CompilerParams(vmem_limit_bytes=32 * 1024 * 1024),
        name="pick_blocks",
    )(me, member, remaining, *pieces, *after)


def project_kernel(waits, slot, own, beside, across, corner, *refs):
    weights, outs = refs[:4], refs[4 + waits :]
    same = jnp.concatenate([own[0], own[1], across[0], across[1]], axis=0)
    other = jnp.concatenate([beside[1], beside[0], corner[1], corner[0]], axis=0)
    rows = own.shape[1]
    for half in range(2):
        total = jnp.dot(same, weights[2 * half][...], preferred_element_type=jnp.float32)
        total += jnp.dot(other, weights[2 * half + 1][...], preferred_element_type=jnp.float32)
        total = total.astype(jnp.bfloat16)
        for r in range(4):
            outs[r][half] = total[r * rows : (r + 1) * rows]


def project(slot, parts, own_weights, sibling_weights, after):
    _, rows, depth = parts[0].shape
    columns = own_weights.shape[1]
    tile = min(512, columns)
    whole = pl.BlockSpec((2, rows, depth), lambda j, slot: (0, 0, 0))
    same = pl.BlockSpec((depth, tile), lambda j, slot: (slot[0], j))
    other = pl.BlockSpec((depth, tile), lambda j, slot: (1 - slot[0], j))
    out = pl.BlockSpec((2, rows, tile), lambda j, slot: (0, 0, j))
    return pl.pallas_call(
        functools.partial(project_kernel, len(after)),
        grid_spec=pltpu.PrefetchScalarGridSpec(
            num_scalar_prefetch=1,
            grid=(columns // tile,),
            in_specs=[whole] * 4 + [same, other] * 2 + anywhere(len(after)),
            out_specs=[out] * 4,
        ),
        out_shape=[jax.ShapeDtypeStruct((2, rows, columns), jnp.bfloat16)] * 4,
        compiler_params=pltpu.CompilerParams(vmem_limit_bytes=26 * 1024 * 1024),
        cost_estimate=pl.CostEstimate(
            flops=2 * 4 * rows * 2 * depth * 2 * columns,
            bytes_accessed=2 * depth * 2 * columns * 2,
            transcendentals=0,
        ),
        name="project",
    )(slot, *parts, own_weights, own_weights, sibling_weights, sibling_weights, *after)


def on_device_planes(
    fresh_segment_probes,
    fresh_segment_pairs,
    earlier_stored_pairs,
    emitted_token_probe,
    emitted_token_pair,
    final_projection_weights,
    remaining_instance_ids,
    segment_destination_member,
):
    index = lax.axis_index("inst")
    slot = index // 4
    rows, heads, width = fresh_segment_probes.shape
    group = heads // 2
    me = jnp.reshape(index, (1,)).astype(jnp.int32)
    slot_array = jnp.reshape(slot, (1,)).astype(jnp.int32)
    offset = jnp.reshape(lax.axis_index("tp") ^ (index // 2), (1,)).astype(jnp.int32)

    piece = {}
    to_beside = split_pairs(1, me, fresh_segment_pairs, earlier_stored_pairs, [])
    piece[4] = swapped(to_beside, "inst", 4)
    piece[0] = split_pairs(0, me, fresh_segment_pairs, earlier_stored_pairs, [to_beside])
    piece[2] = swapped(piece[0], "inst", 2)
    queries_own, queries_send = split_queries(me, fresh_segment_probes, [piece[0]])
    queries = [queries_own, swapped(queries_send, "inst", 4)]
    piece[6] = swapped(piece[4], "inst", 2)
    for d in (0, 4, 2, 6):
        piece[d + 1] = swapped(piece[d], "inst", 1)
    pieces = [piece[d] for d in range(8)]
    sibling_weights = swapped(final_projection_weights, "inst", 1)

    states = early_attention(queries_own, pieces, rows)

    def attention(chunk, after):
        own = chunk_attention(chunk, me, queries, states, pieces, rows, group, after)
        return [own] + [swapped(own, "inst", d) for d in (4, 2, 6)]

    def projected(parts, after):
        outs = project(slot_array, parts, final_projection_weights, sibling_weights, after)
        return [outs[0]] + [swapped(outs[i], "inst", d) for i, d in ((1, 4), (2, 2), (3, 6))]

    sums = {}

    def first_step(k, after):
        parts = [partial[k][0], partial[k][2], partial[k][1], partial[k][3]]
        send = away(offset, parts, after)
        sums[k] = (parts, swapped(send, "tp", 1))
        return send

    def second_step(k, after):
        keep, send = merge(offset, *sums[k], after)
        sums[k] = (keep, swapped(send, "tp", 2))
        return send

    gathered, partial = {}, {}
    gathered[0] = attention(0, [])
    gathered[1] = attention(1, [])
    picked_own, picked_send = pick_blocks(
        me, segment_destination_member, remaining_instance_ids, pieces, rows, [gathered[1][0]]
    )
    picked_beside = swapped(picked_send, "inst", 4)
    partial[0] = projected(gathered[0], [gathered[1][0], picked_own])
    for k in range(2, CHUNKS):
        gathered[k] = attention(k, [partial[k - 2][0]])
        token = gathered[k][0]
        if k >= 3:
            token = second_step(k - 3, [token])
        if k + 1 < CHUNKS:
            token = first_step(k - 2, [token])
        partial[k - 1] = projected(gathered[k - 1], [token])
    last = CHUNKS - 1
    token = first_step(last - 2, [partial[last - 1][0]])
    partial[last] = projected(gathered[last], [token])
    token = second_step(last - 2, [partial[last][0]])
    token = first_step(last - 1, [token])
    token = first_step(last, [token])
    decode_after = token
    token = second_step(last - 1, [token])
    token = second_step(last, [token])
    span_hidden = None
    for k in range(CHUNKS):
        span_hidden = finish(k, me, *sums[k], span_hidden)

    first = jnp.where(slot == 0, picked_own, picked_beside)
    second = jnp.where(slot == 0, picked_beside, picked_own)
    cache = jnp.stack([first, second]).transpose(2, 1, 0, 3)

    decoded = decode(me, emitted_token_probe, emitted_token_pair, pieces, [decode_after])
    decoded_beside = swapped(decoded, "inst", 4)
    mine = (jnp.arange(heads) // group == slot)[:, None]
    decode_attention = jnp.where(mine, decoded, decoded_beside)
    return (span_hidden, cache[None], decode_attention)


def solution(mesh):
    instances, groups = mesh.shape["inst"], mesh.shape["tp"]

    def on_device(*arguments):
        slots_local = arguments[1].shape[2]
        tile = arguments[2].shape[0]
        rows = arguments[1].shape[0]
        if instances == 8 and groups == 4 and slots_local == 2 and tile == 4 * rows:
            return on_device_planes(*arguments)
        return on_device_ring(*arguments)

    return jax.shard_map(
        on_device,
        mesh=mesh,
        in_specs=(
            P("inst", "tp", None),
            P("inst", None, "tp", None),
            P("inst", None, "tp", None),
            P("tp", None),
            P(None, "tp", None),
            P("tp", "inst"),
            P(),
            P(),
        ),
        out_specs=(P("inst", "tp"), P("inst", None, None, "tp", None), P("tp", None)),
        check_vma=False,
    )
```

```python
import functools

import jax
import jax.numpy as jnp
from jax import lax
from jax.experimental import pallas as pl
from jax.experimental.pallas import tpu as pltpu
from jax.sharding import PartitionSpec as P

BLK = 128
CAP = 8
NEG_FILL = -1e30
LOG2E = 1.4426950408889634
LARGEST = 2.0**100
CHUNKS = 4
GROUP = 2


def from_behind(block, axis, distance):
    devices = range(lax.axis_size(axis))
    route = [((i - distance) % len(devices), i) for i in devices]
    return lax.ppermute(block, axis, route)


def combined_all(value, axis, combine):
    everything = jax.tree.map(lambda part: lax.all_gather(part, axis), value)
    initial = jax.tree.map(lambda part: part[0], everything)

    def turn(k, so_far):
        return combine(so_far, jax.tree.map(lambda part: part[k], everything))

    return lax.fori_loop(1, lax.axis_size(axis), turn, initial)


def attend(state, queries, key_value, visible):
    width = queries.shape[-1]
    scores = jnp.einsum(
        "rkgd,nkd->rkgn", queries, key_value[:, 0], preferred_element_type=jnp.float32
    ) * width ** (-0.5)
    if visible is not None:
        scores = jnp.where(visible[:, None, None, :], scores, NEG_FILL)
    running, total, weighted = state
    highest = jnp.maximum(running, jnp.max(scores, axis=-1))
    factor = jnp.exp(running - highest)
    weights = jnp.exp(scores - highest[..., None])
    total = total * factor + jnp.sum(weights, axis=-1)
    update = jnp.einsum(
        "rkgn,nkd->rkgd",
        weights.astype(jnp.bfloat16),
        key_value[:, 1],
        preferred_element_type=jnp.float32,
    )
    weighted = weighted * factor[..., None] + update
    return (highest, total, weighted)


def empty_state(rows, slots_local, group, width):
    return (
        jnp.full((rows, slots_local, group), -jnp.inf, jnp.float32),
        jnp.zeros((rows, slots_local, group), jnp.float32),
        jnp.zeros((rows, slots_local, group, width), jnp.float32),
    )


def combine(first, second):
    highest = jnp.maximum(first[0], second[0])
    left = jnp.exp(first[0] - highest)
    right = jnp.exp(second[0] - highest)
    return (
        highest,
        first[1] * left + second[1] * right,
        first[2] * left[..., None] + second[2] * right[..., None],
    )


def place_blocks(cache, rows_in, destination_members, slots, own_index):
    count = rows_in.shape[0] // BLK

    def put(index, current):
        spot = slots[index] * BLK
        incoming = lax.dynamic_slice_in_dim(rows_in, index * BLK, BLK, 0)
        present = lax.dynamic_slice_in_dim(current, spot, BLK, 0)
        chosen = jnp.where(destination_members[index] == own_index, incoming, present)
        return lax.dynamic_update_slice_in_dim(current, chosen, spot, 0)

    return lax.fori_loop(0, count, put, cache)


def destinations(segment_destination_member, remaining_instance_ids):
    sequence = segment_destination_member[:, 0]
    agreement = (
        sequence[:, None]
        == jnp.arange(remaining_instance_ids.shape[0], dtype=jnp.int32)[None, :]
    ).astype(jnp.int32)
    slots = jnp.sum(jnp.cumsum(agreement, axis=0) * agreement, axis=1) - 1
    members = jnp.sum(agreement * remaining_instance_ids[None, :], axis=1)
    return slots, members


def on_device_ring(
    fresh_segment_probes,
    fresh_segment_pairs,
    earlier_stored_pairs,
    emitted_token_probe,
    emitted_token_pair,
    final_projection_weights,
    remaining_instance_ids,
    segment_destination_member,
):
    own_index = lax.axis_index("inst")
    instances = lax.axis_size("inst")
    rows, heads, width = fresh_segment_probes.shape
    slots_local = fresh_segment_pairs.shape[2]
    group = heads // slots_local
    queries = fresh_segment_probes.reshape(rows, slots_local, group, width)
    slots, destination_members = destinations(segment_destination_member, remaining_instance_ids)
    held_blocks = jnp.sum((destination_members == own_index).astype(jnp.int32))
    cache = jnp.zeros((CAP * BLK, 2, slots_local, width), jnp.bfloat16)
    causal = jnp.arange(rows)[:, None] >= jnp.arange(rows)[None, :]
    state = attend(
        empty_state(rows, slots_local, group, width), queries, earlier_stored_pairs, None
    )
    state = attend(state, queries, fresh_segment_pairs, causal)
    moving = jnp.concatenate([fresh_segment_pairs, earlier_stored_pairs], axis=0)

    def turn_both(step, carry):
        moving, state, current = carry
        moving = from_behind(moving, "inst", 1)
        source = (own_index - step) % instances
        state = attend(state, queries, moving[rows:], None)
        visible = jnp.broadcast_to(source < own_index, (rows, rows))
        state = attend(state, queries, moving[:rows], visible)
        return (moving, state, current)

    moving, state, cache = lax.fori_loop(1, instances, turn_both, (moving, state, cache))
    cache = place_blocks(
        cache,
        lax.all_gather(fresh_segment_pairs, "inst", axis=0, tiled=True),
        destination_members,
        slots,
        own_index,
    )
    attention = (state[2] / state[1][..., None]).astype(jnp.bfloat16).reshape(rows, heads * width)
    terms = jnp.dot(
        attention,
        lax.all_gather(final_projection_weights, "inst", axis=1, tiled=True),
        preferred_element_type=jnp.float32,
    )
    span_hidden = lax.psum_scatter(
        terms.astype(jnp.bfloat16), "tp", scatter_dimension=1, tiled=True
    )
    single = emitted_token_probe.reshape(1, slots_local, group, width)
    decode_state = attend(
        empty_state(1, slots_local, group, width), single, earlier_stored_pairs, None
    )
    live = (jnp.arange(CAP * BLK) < held_blocks * BLK)[None, :]
    decode_state = attend(decode_state, single, cache, live)
    merged = combined_all((decode_state[0], decode_state[1], decode_state[2]), "inst", combine)
    own_scores = jnp.einsum(
        "rkgd,kd->rkg", single, emitted_token_pair[0], preferred_element_type=jnp.float32
    ) * width ** (-0.5)
    highest = jnp.maximum(merged[0], own_scores)
    left = jnp.exp(merged[0] - highest)
    right = jnp.exp(own_scores - highest)
    total = merged[1] * left + right
    own_weight = lax.optimization_barrier(right.astype(jnp.bfloat16)).astype(jnp.float32)
    own_value = emitted_token_pair[1].astype(jnp.float32)
    weighted = merged[2] * left[..., None] + own_weight[..., None] * own_value[None, :, None, :]
    decode_attention = (weighted / total[..., None]).astype(jnp.bfloat16).reshape(heads, width)
    return (span_hidden, cache[None], decode_attention)


def swapped(value, axis, distance):
    size = lax.axis_size(axis)
    return lax.ppermute(value, axis, [(i, i ^ distance) for i in range(size)])


def vmem(count=1):
    return [pl.BlockSpec(memory_space=pltpu.VMEM)] * count


def smem(count=1):
    return [pl.BlockSpec(memory_space=pltpu.SMEM)] * count


def hbm(count=1):
    return [pl.BlockSpec(memory_space=pltpu.HBM)] * count


def anywhere(count=1):
    return [pl.BlockSpec(memory_space=pl.ANY)] * count


def split_pairs_kernel(away, me, fresh, prefix, out):
    rows = fresh.shape[0]
    for y in range(2):

        @pl.when(me[0] >> 2 == y)
        def _():
            s = y ^ away
            for part, start in ((fresh, 0), (prefix, rows)):
                size = part.shape[0]
                out[1, start : start + size] = part[:, 1, s, :]
                for at in range(0, size, BLK):
                    block = part[at : at + BLK, 0, s, :]
                    out[0, start + at : start + at + BLK] = block.T


def split_pairs(away, me, fresh, prefix, after):
    def kernel(me, fresh, prefix, *refs):
        split_pairs_kernel(away, me, fresh, prefix, refs[-1])

    held, width = fresh.shape[0] + prefix.shape[0], fresh.shape[3]
    return pl.pallas_call(
        kernel,
        out_shape=jax.ShapeDtypeStruct((2, held, width), jnp.bfloat16),
        in_specs=smem() + vmem(2) + anywhere(len(after)),
        out_specs=vmem()[0],
        compiler_params=pltpu.CompilerParams(vmem_limit_bytes=24 * 1024 * 1024),
        name="split_pairs",
    )(me, fresh, prefix, *after)


def split_queries_kernel(group, me, queries, own_ref, send_ref):
    chunk_rows = queries.shape[0] // CHUNKS

    def place(out, s):
        for k in range(CHUNKS):
            for g in range(group):
                out[k, g * chunk_rows : (g + 1) * chunk_rows] = queries[
                    k * chunk_rows : (k + 1) * chunk_rows, s * group + g, :
                ]

    for y in range(2):

        @pl.when(me[0] >> 2 == y)
        def _():
            place(own_ref, y)
            place(send_ref, 1 - y)


def split_queries(me, queries, after):
    rows, heads, width = queries.shape
    group = heads // 2
    probes = jax.ShapeDtypeStruct((CHUNKS, group * rows // CHUNKS, width), jnp.bfloat16)

    def kernel(me, queries, *refs):
        split_queries_kernel(group, me, queries, *refs[-2:])

    return pl.pallas_call(
        kernel,
        out_shape=[probes, probes],
        in_specs=smem() + vmem() + anywhere(len(after)),
        out_specs=vmem(2),
        compiler_params=pltpu.CompilerParams(vmem_limit_bytes=24 * 1024 * 1024),
        name="split_queries",
    )(me, queries, *after)


EARLY = (0, 1, 4, 5, 2, 3)
LATE = (6, 7)


def prefix_copies(n, piece, rows, keys, values, sems):
    tile = piece.shape[1] - rows
    at = pl.multiple_of(n * tile, tile)
    return [
        pltpu.make_async_copy(
            piece.at[j, pl.ds(rows, tile)], target.at[pl.ds(at, tile)], sems.at[n, j]
        )
        for j, target in enumerate((keys, values))
    ]


class Tiles:
    def __init__(self, tile, scale, queries, keys, values, weights, shift, sums, weighted):
        self.tile, self.part, self.scale = tile, 2 * BLK, scale
        self.queries, self.keys, self.values = queries, keys, values
        self.weights, self.shift, self.sums, self.weighted = weights, shift, sums, weighted

    def scores(self, t, j, rows):
        at = pl.multiple_of(t * self.tile + j * self.part, self.part)
        block = jnp.concatenate(
            [self.keys[pl.ds(at + l, BLK), :] for l in range(0, self.part, BLK)], axis=1
        )
        return jnp.dot(self.queries[pl.ds(*rows)], block, preferred_element_type=jnp.float32)

    def above(self, t, j, rows, latest):
        width = self.shift.shape[1]
        value, shift = self.scores(t, j, rows), self.shift[pl.ds(*rows)]
        blocks = [value[:, l : l + width] - shift for l in range(0, self.part, width)]
        if latest is None:
            return blocks
        column = lax.broadcasted_iota(jnp.int32, blocks[0].shape, 1)
        return [
            jnp.where(column <= latest - (j * self.part + l * width), block, NEG_FILL)
            for l, block in enumerate(blocks)
        ]

    def weigh(self, t, slot, j, rows, latest):
        width = self.shift.shape[1]
        total = self.sums[pl.ds(*rows)]
        for l, block in enumerate(self.above(t, j, rows, latest)):
            weight = jnp.exp2(block * self.scale)
            total += weight
            at = j * self.part + l * width
            self.weights[slot][pl.ds(*rows), at : at + width] = weight.astype(jnp.bfloat16)
        self.sums[pl.ds(*rows)] = total

    def add(self, t, slot, rows):
        at = pl.multiple_of(t * self.tile, self.tile)
        self.weighted[pl.ds(*rows)] += jnp.dot(
            self.weights[slot][pl.ds(*rows)],
            self.values[pl.ds(at, self.tile), :],
            preferred_element_type=jnp.float32,
        )

    def peak(self, t, rows, latest=None, shifted=True):
        width = self.shift.shape[1]
        peak = None
        for j in range(self.tile // self.part):
            if shifted:
                blocks = self.above(t, j, rows, latest)
            else:
                value = self.scores(t, j, rows)
                blocks = [value[:, l : l + width] for l in range(0, self.part, width)]
            for block in blocks:
                peak = block if peak is None else jnp.maximum(peak, block)
        return jnp.max(peak, axis=1, keepdims=True)

    def first(self, rows):
        top = self.peak(0, rows, shifted=False)
        self.shift[pl.ds(*rows)] = jnp.broadcast_to(top, (rows[1], self.shift.shape[1]))
        for name in (self.sums, self.weighted):
            name[pl.ds(*rows)] = jnp.zeros((rows[1], name.shape[1]), jnp.float32)
        for j in range(self.tile // self.part):
            self.weigh(0, 0, j, rows, None)

    def turn(self, t, slot, rows, latest, before):
        parts = self.tile // self.part
        for j in range(parts):
            self.weigh(t, slot, j, rows, latest)
            for n, side in enumerate(before):
                if n * parts // len(before) == j:
                    self.add(t - 1, 1 - slot, side)

    def careful(self, t, rows, latest):
        up = jnp.maximum(self.peak(t, rows, latest), 0.0)
        factor = jnp.exp2(-up * self.scale)
        self.weighted[pl.ds(*rows)] *= factor
        self.sums[pl.ds(*rows)] *= factor
        self.shift[pl.ds(*rows)] += up
        for j in range(self.tile // self.part):
            self.weigh(t, 0, j, rows, latest)
        self.add(t, 0, rows)


def early_kernel(rows, scale, q_ref, *refs):
    pieces = refs[: len(EARLY)]
    shift, sums, weighted, queries, keys, values, even, odd, sems = refs[len(EARLY) :]
    count, half, _ = q_ref.shape
    tile = pieces[0].shape[1] - rows
    copies = [
        prefix_copies(n, piece, rows, keys, values, sems) for n, piece in enumerate(pieces)
    ]

    @pl.when(pl.program_id(0) == 0)
    def _():
        for pair in copies:
            for copy in pair:
                copy.start()

    for n in range(count):
        queries[n * half : (n + 1) * half] = q_ref[n]

    @pl.when(pl.program_id(0) == 0)
    def _():
        for pair in copies:
            for copy in pair:
                copy.wait()

    tiles = Tiles(tile, scale, queries, keys, values, (even, odd), shift, sums, weighted)
    everything = (0, count * half)
    halves = [(n * half, half) for n in range(count)]
    tiles.first(everything)

    def pair(u, carry):
        tiles.turn(2 * u + 1, 1, everything, None, halves)
        tiles.turn(2 * u + 2, 0, everything, None, halves)
        return carry

    lax.fori_loop(0, 2, pair, 0)
    tiles.turn(5, 1, everything, None, halves)
    for side in halves:
        tiles.add(5, 1, side)


def early_attention(queries, pieces, rows):
    chunks, half, width = queries.shape
    held = pieces[0].shape[1]
    tile = held - rows
    step = 2
    state = jax.ShapeDtypeStruct((chunks * half, width), jnp.float32)
    size = step * half
    keys = len(EARLY) * tile
    return pl.pallas_call(
        functools.partial(early_kernel, rows, width ** (-0.5) * LOG2E),
        grid=(chunks // step,),
        out_shape=[state] * 3,
        in_specs=[pl.BlockSpec((step, half, width), lambda i: (i, 0, 0))] + hbm(len(EARLY)),
        out_specs=[pl.BlockSpec((size, width), lambda i: (i, 0))] * 3,
        scratch_shapes=[
            pltpu.VMEM((size, width), jnp.bfloat16),
            pltpu.VMEM((keys, width), jnp.bfloat16),
            pltpu.VMEM((keys, width), jnp.bfloat16),
            pltpu.VMEM((size, tile), jnp.bfloat16),
            pltpu.VMEM((size, tile), jnp.bfloat16),
            pltpu.SemaphoreType.DMA((len(EARLY), 2)),
        ],
        compiler_params=pltpu.CompilerParams(vmem_limit_bytes=24 * 1024 * 1024),
        cost_estimate=pl.CostEstimate(
            flops=2 * 2 * chunks * half * keys * width * 2,
            bytes_accessed=keys * width * 4 + 3 * chunks * half * width * 4,
            transcendentals=chunks * half * keys,
        ),
        name="early_attention",
    )(queries, *[pieces[p] for p in EARLY])


def attention_kernel(waits, chunk, chunk_rows, rows, group, scale, me, own, beside, *refs):
    states, pieces = refs[:3], refs[3:11]
    out_ref = refs[11 + waits]
    queries, keys, values, even, odd, shift, sums, weighted, sems, late_sems = refs[12 + waits :]
    half = own.shape[1]
    held, width = pieces[0].shape[1:]
    tile = held - rows
    y = me[0] >> 2
    own_rows = (pl.multiple_of(y * half, half), half)
    beside_rows = (pl.multiple_of((1 - y) * half, half), half)
    low, high, everything = (0, half), (half, half), (0, 2 * half)
    order = EARLY + LATE

    def fresh_copies(p):
        at = pl.multiple_of(8 * tile + (me[0] ^ p) * rows, rows)
        return [
            pltpu.make_async_copy(
                pieces[p].at[j, pl.ds(0, rows)], target.at[pl.ds(at, rows)], sems.at[p, 2 + j]
            )
            for j, target in enumerate((keys, values))
        ]

    query_copies = [
        pltpu.make_async_copy(source.at[chunk], queries.at[pl.ds(*place)], late_sems.at[n])
        for n, (source, place) in enumerate(((own, own_rows), (beside, beside_rows)))
    ]
    state_copies = [
        pltpu.make_async_copy(
            source.at[pl.ds(chunk * half, half)], target.at[pl.ds(*own_rows)], late_sems.at[2 + n]
        )
        for n, (source, target) in enumerate(zip(states, (shift, sums, weighted)))
    ]
    copies = [prefix_copies(n, pieces[p], rows, keys, values, sems) for n, p in enumerate(order)]
    for copy in query_copies + copies[0] + state_copies:
        copy.start()
    for pair in copies[1:]:
        for copy in pair:
            copy.start()
    for p in range(8):
        for copy in fresh_copies(p):
            copy.start()

    def wait_for(n):
        for copy in prefix_copies(n, pieces[0], rows, keys, values, sems):
            copy.wait()

    tiles = Tiles(tile, scale, queries, keys, values, (even, odd), shift, sums, weighted)
    for copy in query_copies + copies[0]:
        copy.wait()
    tiles.first(beside_rows)

    def pair(u, carry):
        wait_for(2 * u + 1)
        tiles.turn(2 * u + 1, 1, beside_rows, None, [beside_rows])
        wait_for(2 * u + 2)
        tiles.turn(2 * u + 2, 0, beside_rows, None, [beside_rows])
        return carry

    lax.fori_loop(0, 2, pair, 0)
    wait_for(5)
    tiles.turn(5, 1, beside_rows, None, [beside_rows])
    wait_for(6)
    wait_for(7)
    for copy in state_copies:
        copy.wait()
    tiles.turn(6, 0, everything, None, [beside_rows])
    tiles.turn(7, 1, everything, None, [low, high])
    for p in range(8):
        for copy in fresh_copies(p):
            copy.wait()

    def latest(count):
        row = lax.broadcasted_iota(jnp.int32, (count, width), 0)
        last = (me[0] & 3) * rows + chunk * chunk_rows + row % chunk_rows
        return last if count == half else jnp.where(row < half, last, tile)

    tiles.turn(8, 0, everything, latest(2 * half), [low, high])
    tiles.turn(9, 1, high, latest(half), [low, high])
    tiles.add(9, 1, high)

    @pl.when(jnp.logical_not(jnp.max(sums[...]) < LARGEST))
    def _():
        weighted[...] = jnp.zeros(weighted.shape, jnp.float32)
        sums[...] = jnp.zeros(sums.shape, jnp.float32)

        def prefix_tile(t, carry):
            tiles.careful(t, everything, None)
            return carry

        lax.fori_loop(0, 8, prefix_tile, 0)
        tiles.careful(8, everything, latest(2 * half))
        tiles.careful(9, high, latest(half))

    for h in range(2):
        block = slice(h * half, (h + 1) * half)
        total = jnp.sum(sums[block], axis=1, keepdims=True)
        result = (weighted[block] / total).astype(jnp.bfloat16)
        for g in range(group):
            out_ref[y ^ h, :, g * width : (g + 1) * width] = result[
                g * chunk_rows : (g + 1) * chunk_rows
            ]


def chunk_attention(chunk, me, queries, states, pieces, rows, group, so_far, after):
    _, half, width = queries[0].shape
    chunk_rows = half // group
    held = pieces[0].shape[1]
    tile = held - rows
    aliases = {}
    if so_far is not None:
        aliases = {14 + len(after): 0}
        after = after + [so_far]
    return pl.pallas_call(
        functools.partial(
            attention_kernel,
            len(after),
            chunk,
            chunk_rows,
            rows,
            group,
            width ** (-0.5) * LOG2E,
        ),
        grid=(1,),
        out_shape=jax.ShapeDtypeStruct((2, GROUP * chunk_rows, group * width), jnp.bfloat16),
        in_specs=smem() + hbm(13) + anywhere(len(after)),
        out_specs=pl.BlockSpec((2, chunk_rows, group * width), lambda i: (0, chunk % GROUP, 0)),
        input_output_aliases=aliases,
        scratch_shapes=[
            pltpu.VMEM((2 * half, width), jnp.bfloat16),
            pltpu.VMEM((8 * held, width), jnp.bfloat16),
            pltpu.VMEM((8 * held, width), jnp.bfloat16),
            pltpu.VMEM((2 * half, tile), jnp.bfloat16),
            pltpu.VMEM((2 * half, tile), jnp.bfloat16),
            pltpu.VMEM((2 * half, width), jnp.float32),
            pltpu.VMEM((2 * half, width), jnp.float32),
            pltpu.VMEM((2 * half, width), jnp.float32),
            pltpu.SemaphoreType.DMA((8, 4)),
            pltpu.SemaphoreType.DMA((5,)),
        ],
        compiler_params=pltpu.CompilerParams(vmem_limit_bytes=24 * 1024 * 1024),
        cost_estimate=pl.CostEstimate(
            flops=2 * 2 * 2 * half * 8 * held * width * 2 * 2 // 3,
            bytes_accessed=8 * held * width * 4,
            transcendentals=2 * half * 8 * held * 2 // 3,
        ),
        name="chunk_attention",
    )(me, *queries, *states, *pieces, *after)


def away_kernel(offset, here, across, beside, corner, *refs):
    send_ref = refs[-1]

    @pl.when(offset[0] % 2 == 0)
    def _():
        send_ref[0] = across[...]
        send_ref[1] = corner[...]

    @pl.when(offset[0] % 2 == 1)
    def _():
        send_ref[0] = here[...]
        send_ref[1] = beside[...]


def away(offset, parts, after):
    return pl.pallas_call(
        away_kernel,
        out_shape=jax.ShapeDtypeStruct((2, *parts[0].shape), jnp.bfloat16),
        in_specs=smem() + vmem(4) + anywhere(len(after)),
        out_specs=vmem()[0],
        name="away",
    )(offset, *parts, *after)


def merge_kernel(offset, here, across, beside, corner, came, *refs):
    keep_ref, send_ref = refs[-2:]
    sides = ((here, across), (beside, corner))
    for low in range(2):
        for high in range(2):

            @pl.when(offset[0] == low + 2 * high)
            def _():
                for r, target in ((high, keep_ref), (1 - high, send_ref)):
                    total = sides[r][low][...].astype(jnp.float32) + came[r].astype(jnp.float32)
                    target[...] = total.astype(target.dtype)


def merge(offset, parts, came, after):
    return pl.pallas_call(
        merge_kernel,
        out_shape=[
            jax.ShapeDtypeStruct(parts[0].shape, jnp.float32),
            jax.ShapeDtypeStruct(parts[0].shape, jnp.bfloat16),
        ],
        in_specs=smem() + vmem(5) + anywhere(len(after)),
        out_specs=vmem(2),
        name="merge",
    )(offset, *parts, came, *after)


def finish_kernel(me, keep, came, *refs):
    out_ref = refs[-1]
    columns = keep.shape[2]
    for half in range(2):
        at = pl.multiple_of(((me[0] & 1) ^ half) * columns, columns)
        total = keep[half] + came[half].astype(jnp.float32)
        out_ref[:, pl.ds(at, columns)] = total.astype(out_ref.dtype)


def finish(chunk, me, keep, came, so_far):
    _, rows, columns = keep.shape
    whole = pl.BlockSpec(keep.shape, lambda i: (0, 0, 0))
    operands = [me, keep, came]
    specs = smem() + [whole] * 2
    aliases = {}
    if so_far is not None:
        aliases = {len(operands): 0}
        operands.append(so_far)
        specs += anywhere()
    return pl.pallas_call(
        finish_kernel,
        grid=(1,),
        out_shape=jax.ShapeDtypeStruct((CHUNKS // GROUP * rows, 2 * columns), jnp.bfloat16),
        in_specs=specs,
        out_specs=pl.BlockSpec((rows, 2 * columns), lambda i: (chunk, 0)),
        input_output_aliases=aliases,
        name="finish",
    )(*operands)


def decode_kernel(scale, me, q_ref, last_ref, *refs):
    pieces, out_ref = refs[:8], refs[8]
    q = q_ref[...]
    width = q.shape[1]
    low = me[0] < 4
    last = [jnp.where(low, last_ref[j, 0:1, :], last_ref[j, 1:2, :]) for j in range(2)]
    last = [value.astype(jnp.float32) for value in last]
    running = jnp.sum(q.astype(jnp.float32) * last[0], axis=1, keepdims=True)
    total = jnp.ones_like(running)
    weighted = jnp.broadcast_to(last[1], (q.shape[0], width))
    for piece in pieces:
        scores = jnp.concatenate(
            [
                jnp.dot(q, piece[0, at : at + BLK], preferred_element_type=jnp.float32)
                for at in range(0, piece.shape[1], BLK)
            ],
            axis=1,
        )
        highest = jnp.maximum(running, jnp.max(scores, axis=1, keepdims=True))
        weights = jnp.exp2((scores - highest) * scale)
        factor = jnp.exp2((running - highest) * scale)
        total = total * factor + jnp.sum(weights, axis=1, keepdims=True)
        weighted = weighted * factor + jnp.dot(
            weights.astype(jnp.bfloat16), piece[1], preferred_element_type=jnp.float32
        )
        running = highest
    out_ref[...] = (weighted / total).astype(jnp.bfloat16)


def decode(me, query, last, pieces, after):
    width = query.shape[1]
    held = pieces[0].shape[1]

    def kernel(me, q_ref, last_ref, *refs):
        decode_kernel(width ** (-0.5) * LOG2E, me, q_ref, last_ref, *refs[:8], refs[-1])

    return pl.pallas_call(
        kernel,
        out_shape=jax.ShapeDtypeStruct(query.shape, jnp.bfloat16),
        in_specs=smem() + vmem(10) + anywhere(len(after)),
        out_specs=vmem()[0],
        compiler_params=pltpu.CompilerParams(vmem_limit_bytes=32 * 1024 * 1024),
        cost_estimate=pl.CostEstimate(
            flops=4 * query.shape[0] * width * 8 * held,
            bytes_accessed=8 * held * width * 4,
            transcendentals=query.shape[0] * 8 * held,
        ),
        name="decode",
    )(me, query, last, *pieces, *after)


def pick_kernel(rows, me, member, remaining, *refs):
    pieces, (*outs, held, sems) = refs[:8], refs[-4:]
    count = member.shape[0]
    copies = []
    for p in range(8):
        at = pl.multiple_of((me[0] ^ p) * rows, rows)
        copies.append(
            pltpu.make_async_copy(
                pieces[p].at[:, pl.ds(0, rows)], held.at[:, pl.ds(at, rows)], sems.at[p]
            )
        )
        copies[p].start()
    for out in outs:
        out[...] = jnp.zeros(out.shape, out.dtype)
    for copy in copies:
        copy.wait()
    for b in range(count):
        target = member[b, 0]
        owner = remaining[target]
        spot = jnp.int32(0)
        for before in range(b):
            spot += (member[before, 0] == target).astype(jnp.int32)
        at = pl.multiple_of(spot * BLK, BLK)
        for out, instance in zip(outs, (me[0], me[0] ^ 4)):

            @pl.when(owner == instance)
            def _():
                out[0, pl.ds(at, BLK), :] = held[0, b * BLK : (b + 1) * BLK, :].T
                out[1, pl.ds(at, BLK), :] = held[1, b * BLK : (b + 1) * BLK, :]


def pick_blocks(me, member, remaining, pieces, rows, after):
    width = pieces[0].shape[2]
    shape = jax.ShapeDtypeStruct((2, CAP * BLK, width), jnp.bfloat16)
    return pl.pallas_call(
        functools.partial(pick_kernel, rows),
        out_shape=[shape, shape],
        in_specs=smem(3) + hbm(8) + anywhere(len(after)),
        out_specs=vmem(2),
        scratch_shapes=[
            pltpu.VMEM((2, 8 * rows, width), jnp.bfloat16),
            pltpu.SemaphoreType.DMA((8,)),
        ],
        compiler_params=pltpu.CompilerParams(vmem_limit_bytes=32 * 1024 * 1024),
        name="pick_blocks",
    )(me, member, remaining, *pieces, *after)


def project_kernel(waits, slot, own, beside, across, corner, *refs):
    weights, outs = refs[:4], refs[4 + waits :]
    same = jnp.concatenate([own[0], own[1], across[0], across[1]], axis=0)
    other = jnp.concatenate([beside[1], beside[0], corner[1], corner[0]], axis=0)
    rows = own.shape[1]
    for half in range(2):
        total = jnp.dot(same, weights[2 * half][...], preferred_element_type=jnp.float32)
        total += jnp.dot(other, weights[2 * half + 1][...], preferred_element_type=jnp.float32)
        total = total.astype(jnp.bfloat16)
        for r in range(4):
            outs[r][half] = total[r * rows : (r + 1) * rows]


def project(slot, parts, own_weights, sibling_weights, after):
    _, rows, depth = parts[0].shape
    columns = own_weights.shape[1]
    tile = min(512, columns)
    whole = pl.BlockSpec((2, rows, depth), lambda j, slot: (0, 0, 0))
    same = pl.BlockSpec((depth, tile), lambda j, slot: (slot[0], j))
    other = pl.BlockSpec((depth, tile), lambda j, slot: (1 - slot[0], j))
    out = pl.BlockSpec((2, rows, tile), lambda j, slot: (0, 0, j))
    return pl.pallas_call(
        functools.partial(project_kernel, len(after)),
        grid_spec=pltpu.PrefetchScalarGridSpec(
            num_scalar_prefetch=1,
            grid=(columns // tile,),
            in_specs=[whole] * 4 + [same, other] * 2 + anywhere(len(after)),
            out_specs=[out] * 4,
        ),
        out_shape=[jax.ShapeDtypeStruct((2, rows, columns), jnp.bfloat16)] * 4,
        compiler_params=pltpu.CompilerParams(vmem_limit_bytes=26 * 1024 * 1024),
        cost_estimate=pl.CostEstimate(
            flops=2 * 4 * rows * 2 * depth * 2 * columns,
            bytes_accessed=2 * depth * 2 * columns * 2,
            transcendentals=0,
        ),
        name="project",
    )(slot, *parts, own_weights, own_weights, sibling_weights, sibling_weights, *after)


def on_device_planes(
    fresh_segment_probes,
    fresh_segment_pairs,
    earlier_stored_pairs,
    emitted_token_probe,
    emitted_token_pair,
    final_projection_weights,
    remaining_instance_ids,
    segment_destination_member,
):
    index = lax.axis_index("inst")
    slot = index // 4
    rows, heads, width = fresh_segment_probes.shape
    group = heads // 2
    me = jnp.reshape(index, (1,)).astype(jnp.int32)
    slot_array = jnp.reshape(slot, (1,)).astype(jnp.int32)
    offset = jnp.reshape(lax.axis_index("tp") ^ (index // 2), (1,)).astype(jnp.int32)

    piece = {}
    to_beside = split_pairs(1, me, fresh_segment_pairs, earlier_stored_pairs, [])
    piece[4] = swapped(to_beside, "inst", 4)
    piece[0] = split_pairs(0, me, fresh_segment_pairs, earlier_stored_pairs, [to_beside])
    piece[2] = swapped(piece[0], "inst", 2)
    queries_own, queries_send = split_queries(me, fresh_segment_probes, [piece[0]])
    queries = [queries_own, swapped(queries_send, "inst", 4)]
    piece[6] = swapped(piece[4], "inst", 2)
    for d in (0, 4, 2, 6):
        piece[d + 1] = swapped(piece[d], "inst", 1)
    pieces = [piece[d] for d in range(8)]
    sibling_weights = swapped(final_projection_weights, "inst", 1)

    states = early_attention(queries_own, pieces, rows)

    def attention(k, after):
        own = None
        for chunk in range(k * GROUP, (k + 1) * GROUP):
            own = chunk_attention(
                chunk, me, queries, states, pieces, rows, group, own, after if own is None else []
            )
        return [own] + [swapped(own, "inst", d) for d in (4, 2, 6)]

    def projected(parts, after):
        outs = project(slot_array, parts, final_projection_weights, sibling_weights, after)
        return [outs[0]] + [swapped(outs[i], "inst", d) for i, d in ((1, 4), (2, 2), (3, 6))]

    sums = {}

    def first_step(k, after):
        parts = [partial[k][0], partial[k][2], partial[k][1], partial[k][3]]
        send = away(offset, parts, after)
        sums[k] = (parts, swapped(send, "tp", 1))
        return send

    def second_step(k, after):
        keep, send = merge(offset, *sums[k], after)
        sums[k] = (keep, swapped(send, "tp", 2))
        return send

    gathered, partial = {}, {}
    picked_own, picked_send = pick_blocks(
        me, segment_destination_member, remaining_instance_ids, pieces, rows, []
    )
    picked_beside = swapped(picked_send, "inst", 4)
    token = picked_own
    groups = range(CHUNKS // GROUP)
    for k in groups:
        gathered[k] = attention(k, [token])
        token = gathered[k][0]
    for k in groups:
        partial[k] = projected(gathered[k], [token])
        token = partial[k][0]
        if k == 0:
            decoded = decode(me, emitted_token_probe, emitted_token_pair, pieces, [token])
            token = decoded
    for k in groups:
        token = first_step(k, [token])
    for k in groups:
        token = second_step(k, [token])
    span_hidden = None
    for k in groups:
        span_hidden = finish(k, me, *sums[k], span_hidden)

    first = jnp.where(slot == 0, picked_own, picked_beside)
    second = jnp.where(slot == 0, picked_beside, picked_own)
    cache = jnp.stack([first, second]).transpose(2, 1, 0, 3)

    decoded_beside = swapped(decoded, "inst", 4)
    mine = (jnp.arange(heads) // group == slot)[:, None]
    decode_attention = jnp.where(mine, decoded, decoded_beside)
    return (span_hidden, cache[None], decode_attention)


def solution(mesh):
    instances, groups = mesh.shape["inst"], mesh.shape["tp"]

    def on_device(*arguments):
        slots_local = arguments[1].shape[2]
        tile = arguments[2].shape[0]
        rows = arguments[1].shape[0]
        if instances == 8 and groups == 4 and slots_local == 2 and tile == 4 * rows:
            return on_device_planes(*arguments)
        return on_device_ring(*arguments)

    return jax.shard_map(
        on_device,
        mesh=mesh,
        in_specs=(
            P("inst", "tp", None),
            P("inst", None, "tp", None),
            P("inst", None, "tp", None),
            P("tp", None),
            P(None, "tp", None),
            P("tp", "inst"),
            P(),
            P(),
        ),
        out_specs=(P("inst", "tp"), P("inst", None, None, "tp", None), P("tp", None)),
        check_vma=False,
    )
```

```python
import functools

import jax
import jax.numpy as jnp
from jax import lax
from jax.experimental import pallas as pl
from jax.experimental.pallas import tpu as pltpu
from jax.sharding import PartitionSpec as P

BLK = 128
CAP = 8
NEG_FILL = -1e30
LOG2E = 1.4426950408889634
LARGEST = 2.0**100
CHUNKS = 4
GROUP = 2
BRIEF = pl.CostEstimate(flops=1024, bytes_accessed=1024, transcendentals=0)


def from_behind(block, axis, distance):
    devices = range(lax.axis_size(axis))
    route = [((i - distance) % len(devices), i) for i in devices]
    return lax.ppermute(block, axis, route)


def combined_all(value, axis, combine):
    everything = jax.tree.map(lambda part: lax.all_gather(part, axis), value)
    initial = jax.tree.map(lambda part: part[0], everything)

    def turn(k, so_far):
        return combine(so_far, jax.tree.map(lambda part: part[k], everything))

    return lax.fori_loop(1, lax.axis_size(axis), turn, initial)


def attend(state, queries, key_value, visible):
    width = queries.shape[-1]
    scores = jnp.einsum(
        "rkgd,nkd->rkgn", queries, key_value[:, 0], preferred_element_type=jnp.float32
    ) * width ** (-0.5)
    if visible is not None:
        scores = jnp.where(visible[:, None, None, :], scores, NEG_FILL)
    running, total, weighted = state
    highest = jnp.maximum(running, jnp.max(scores, axis=-1))
    factor = jnp.exp(running - highest)
    weights = jnp.exp(scores - highest[..., None])
    total = total * factor + jnp.sum(weights, axis=-1)
    update = jnp.einsum(
        "rkgn,nkd->rkgd",
        weights.astype(jnp.bfloat16),
        key_value[:, 1],
        preferred_element_type=jnp.float32,
    )
    weighted = weighted * factor[..., None] + update
    return (highest, total, weighted)


def empty_state(rows, slots_local, group, width):
    return (
        jnp.full((rows, slots_local, group), -jnp.inf, jnp.float32),
        jnp.zeros((rows, slots_local, group), jnp.float32),
        jnp.zeros((rows, slots_local, group, width), jnp.float32),
    )


def combine(first, second):
    highest = jnp.maximum(first[0], second[0])
    left = jnp.exp(first[0] - highest)
    right = jnp.exp(second[0] - highest)
    return (
        highest,
        first[1] * left + second[1] * right,
        first[2] * left[..., None] + second[2] * right[..., None],
    )


def place_blocks(cache, rows_in, destination_members, slots, own_index):
    count = rows_in.shape[0] // BLK

    def put(index, current):
        spot = slots[index] * BLK
        incoming = lax.dynamic_slice_in_dim(rows_in, index * BLK, BLK, 0)
        present = lax.dynamic_slice_in_dim(current, spot, BLK, 0)
        chosen = jnp.where(destination_members[index] == own_index, incoming, present)
        return lax.dynamic_update_slice_in_dim(current, chosen, spot, 0)

    return lax.fori_loop(0, count, put, cache)


def destinations(segment_destination_member, remaining_instance_ids):
    sequence = segment_destination_member[:, 0]
    agreement = (
        sequence[:, None]
        == jnp.arange(remaining_instance_ids.shape[0], dtype=jnp.int32)[None, :]
    ).astype(jnp.int32)
    slots = jnp.sum(jnp.cumsum(agreement, axis=0) * agreement, axis=1) - 1
    members = jnp.sum(agreement * remaining_instance_ids[None, :], axis=1)
    return slots, members


def on_device_ring(
    fresh_segment_probes,
    fresh_segment_pairs,
    earlier_stored_pairs,
    emitted_token_probe,
    emitted_token_pair,
    final_projection_weights,
    remaining_instance_ids,
    segment_destination_member,
):
    own_index = lax.axis_index("inst")
    instances = lax.axis_size("inst")
    rows, heads, width = fresh_segment_probes.shape
    slots_local = fresh_segment_pairs.shape[2]
    group = heads // slots_local
    queries = fresh_segment_probes.reshape(rows, slots_local, group, width)
    slots, destination_members = destinations(segment_destination_member, remaining_instance_ids)
    held_blocks = jnp.sum((destination_members == own_index).astype(jnp.int32))
    cache = jnp.zeros((CAP * BLK, 2, slots_local, width), jnp.bfloat16)
    causal = jnp.arange(rows)[:, None] >= jnp.arange(rows)[None, :]
    state = attend(
        empty_state(rows, slots_local, group, width), queries, earlier_stored_pairs, None
    )
    state = attend(state, queries, fresh_segment_pairs, causal)
    moving = jnp.concatenate([fresh_segment_pairs, earlier_stored_pairs], axis=0)

    def turn_both(step, carry):
        moving, state, current = carry
        moving = from_behind(moving, "inst", 1)
        source = (own_index - step) % instances
        state = attend(state, queries, moving[rows:], None)
        visible = jnp.broadcast_to(source < own_index, (rows, rows))
        state = attend(state, queries, moving[:rows], visible)
        return (moving, state, current)

    moving, state, cache = lax.fori_loop(1, instances, turn_both, (moving, state, cache))
    cache = place_blocks(
        cache,
        lax.all_gather(fresh_segment_pairs, "inst", axis=0, tiled=True),
        destination_members,
        slots,
        own_index,
    )
    attention = (state[2] / state[1][..., None]).astype(jnp.bfloat16).reshape(rows, heads * width)
    terms = jnp.dot(
        attention,
        lax.all_gather(final_projection_weights, "inst", axis=1, tiled=True),
        preferred_element_type=jnp.float32,
    )
    span_hidden = lax.psum_scatter(
        terms.astype(jnp.bfloat16), "tp", scatter_dimension=1, tiled=True
    )
    single = emitted_token_probe.reshape(1, slots_local, group, width)
    decode_state = attend(
        empty_state(1, slots_local, group, width), single, earlier_stored_pairs, None
    )
    live = (jnp.arange(CAP * BLK) < held_blocks * BLK)[None, :]
    decode_state = attend(decode_state, single, cache, live)
    merged = combined_all((decode_state[0], decode_state[1], decode_state[2]), "inst", combine)
    own_scores = jnp.einsum(
        "rkgd,kd->rkg", single, emitted_token_pair[0], preferred_element_type=jnp.float32
    ) * width ** (-0.5)
    highest = jnp.maximum(merged[0], own_scores)
    left = jnp.exp(merged[0] - highest)
    right = jnp.exp(own_scores - highest)
    total = merged[1] * left + right
    own_weight = lax.optimization_barrier(right.astype(jnp.bfloat16)).astype(jnp.float32)
    own_value = emitted_token_pair[1].astype(jnp.float32)
    weighted = merged[2] * left[..., None] + own_weight[..., None] * own_value[None, :, None, :]
    decode_attention = (weighted / total[..., None]).astype(jnp.bfloat16).reshape(heads, width)
    return (span_hidden, cache[None], decode_attention)


def swapped(value, axis, distance):
    size = lax.axis_size(axis)
    return lax.ppermute(value, axis, [(i, i ^ distance) for i in range(size)])


def vmem(count=1):
    return [pl.BlockSpec(memory_space=pltpu.VMEM)] * count


def smem(count=1):
    return [pl.BlockSpec(memory_space=pltpu.SMEM)] * count


def hbm(count=1):
    return [pl.BlockSpec(memory_space=pltpu.HBM)] * count


def anywhere(count=1):
    return [pl.BlockSpec(memory_space=pl.ANY)] * count


def split_pairs_kernel(away, me, fresh, prefix, out):
    rows = fresh.shape[0]
    for y in range(2):

        @pl.when(me[0] >> 2 == y)
        def _():
            s = y ^ away
            for part, start in ((fresh, 0), (prefix, rows)):
                size = part.shape[0]
                out[1, start : start + size] = part[:, 1, s, :]
                for at in range(0, size, BLK):
                    block = part[at : at + BLK, 0, s, :]
                    out[0, start + at : start + at + BLK] = block.T


def split_pairs(away, me, fresh, prefix, after):
    def kernel(me, fresh, prefix, *refs):
        split_pairs_kernel(away, me, fresh, prefix, refs[-1])

    held, width = fresh.shape[0] + prefix.shape[0], fresh.shape[3]
    return pl.pallas_call(
        kernel,
        out_shape=jax.ShapeDtypeStruct((2, held, width), jnp.bfloat16),
        in_specs=smem() + vmem(2) + anywhere(len(after)),
        out_specs=vmem()[0],
        compiler_params=pltpu.CompilerParams(vmem_limit_bytes=24 * 1024 * 1024),
        cost_estimate=BRIEF,
        name="split_pairs",
    )(me, fresh, prefix, *after)


def split_queries_kernel(group, me, queries, own_ref, send_ref):
    chunk_rows = queries.shape[0] // CHUNKS

    def place(out, s):
        for k in range(CHUNKS):
            for g in range(group):
                out[k, g * chunk_rows : (g + 1) * chunk_rows] = queries[
                    k * chunk_rows : (k + 1) * chunk_rows, s * group + g, :
                ]

    for y in range(2):

        @pl.when(me[0] >> 2 == y)
        def _():
            place(own_ref, y)
            place(send_ref, 1 - y)


def split_queries(me, queries, after):
    rows, heads, width = queries.shape
    group = heads // 2
    probes = jax.ShapeDtypeStruct((CHUNKS, group * rows // CHUNKS, width), jnp.bfloat16)

    def kernel(me, queries, *refs):
        split_queries_kernel(group, me, queries, *refs[-2:])

    return pl.pallas_call(
        kernel,
        out_shape=[probes, probes],
        in_specs=smem() + vmem() + anywhere(len(after)),
        out_specs=vmem(2),
        compiler_params=pltpu.CompilerParams(vmem_limit_bytes=24 * 1024 * 1024),
        cost_estimate=BRIEF,
        name="split_queries",
    )(me, queries, *after)


EARLY = (0, 1, 4, 5, 2, 3)
LATE = (6, 7)


def prefix_copies(n, piece, rows, keys, values, sems):
    tile = piece.shape[1] - rows
    at = pl.multiple_of(n * tile, tile)
    return [
        pltpu.make_async_copy(
            piece.at[j, pl.ds(rows, tile)], target.at[pl.ds(at, tile)], sems.at[n, j]
        )
        for j, target in enumerate((keys, values))
    ]


class Tiles:
    def __init__(self, tile, scale, queries, keys, values, weights, shift, sums, weighted):
        self.tile, self.part, self.scale = tile, 2 * BLK, scale
        self.queries, self.keys, self.values = queries, keys, values
        self.weights, self.shift, self.sums, self.weighted = weights, shift, sums, weighted

    def scores(self, t, j, rows):
        at = pl.multiple_of(t * self.tile + j * self.part, self.part)
        block = jnp.concatenate(
            [self.keys[pl.ds(at + l, BLK), :] for l in range(0, self.part, BLK)], axis=1
        )
        return jnp.dot(self.queries[pl.ds(*rows)], block, preferred_element_type=jnp.float32)

    def above(self, t, j, rows, latest):
        width = self.shift.shape[1]
        value, shift = self.scores(t, j, rows), self.shift[pl.ds(*rows)]
        blocks = [value[:, l : l + width] - shift for l in range(0, self.part, width)]
        if latest is None:
            return blocks
        column = lax.broadcasted_iota(jnp.int32, blocks[0].shape, 1)
        return [
            jnp.where(column <= latest - (j * self.part + l * width), block, NEG_FILL)
            for l, block in enumerate(blocks)
        ]

    def weigh(self, t, slot, j, rows, latest):
        width = self.shift.shape[1]
        total = self.sums[pl.ds(*rows)]
        for l, block in enumerate(self.above(t, j, rows, latest)):
            weight = jnp.exp2(block * self.scale)
            total += weight
            at = j * self.part + l * width
            self.weights[slot][pl.ds(*rows), at : at + width] = weight.astype(jnp.bfloat16)
        self.sums[pl.ds(*rows)] = total

    def add(self, t, slot, rows):
        at = pl.multiple_of(t * self.tile, self.tile)
        self.weighted[pl.ds(*rows)] += jnp.dot(
            self.weights[slot][pl.ds(*rows)],
            self.values[pl.ds(at, self.tile), :],
            preferred_element_type=jnp.float32,
        )

    def peak(self, t, rows, latest=None, shifted=True):
        width = self.shift.shape[1]
        peak = None
        for j in range(self.tile // self.part):
            if shifted:
                blocks = self.above(t, j, rows, latest)
            else:
                value = self.scores(t, j, rows)
                blocks = [value[:, l : l + width] for l in range(0, self.part, width)]
            for block in blocks:
                peak = block if peak is None else jnp.maximum(peak, block)
        return jnp.max(peak, axis=1, keepdims=True)

    def first(self, rows):
        top = self.peak(0, rows, shifted=False)
        self.shift[pl.ds(*rows)] = jnp.broadcast_to(top, (rows[1], self.shift.shape[1]))
        for name in (self.sums, self.weighted):
            name[pl.ds(*rows)] = jnp.zeros((rows[1], name.shape[1]), jnp.float32)
        for j in range(self.tile // self.part):
            self.weigh(0, 0, j, rows, None)

    def turn(self, t, slot, rows, latest, before):
        parts = self.tile // self.part
        for j in range(parts):
            self.weigh(t, slot, j, rows, latest)
            for n, side in enumerate(before):
                if n * parts // len(before) == j:
                    self.add(t - 1, 1 - slot, side)

    def careful(self, t, rows, latest):
        up = jnp.maximum(self.peak(t, rows, latest), 0.0)
        factor = jnp.exp2(-up * self.scale)
        self.weighted[pl.ds(*rows)] *= factor
        self.sums[pl.ds(*rows)] *= factor
        self.shift[pl.ds(*rows)] += up
        for j in range(self.tile // self.part):
            self.weigh(t, 0, j, rows, latest)
        self.add(t, 0, rows)


def early_kernel(rows, scale, q_ref, *refs):
    pieces = refs[: len(EARLY)]
    shift, sums, weighted, queries, keys, values, even, odd, sems = refs[len(EARLY) :]
    count, half, _ = q_ref.shape
    tile = pieces[0].shape[1] - rows
    copies = [
        prefix_copies(n, piece, rows, keys, values, sems) for n, piece in enumerate(pieces)
    ]

    @pl.when(pl.program_id(0) == 0)
    def _():
        for pair in copies:
            for copy in pair:
                copy.start()

    for n in range(count):
        queries[n * half : (n + 1) * half] = q_ref[n]

    @pl.when(pl.program_id(0) == 0)
    def _():
        for pair in copies:
            for copy in pair:
                copy.wait()

    tiles = Tiles(tile, scale, queries, keys, values, (even, odd), shift, sums, weighted)
    everything = (0, count * half)
    halves = [(n * half, half) for n in range(count)]
    tiles.first(everything)

    def pair(u, carry):
        tiles.turn(2 * u + 1, 1, everything, None, halves)
        tiles.turn(2 * u + 2, 0, everything, None, halves)
        return carry

    lax.fori_loop(0, 2, pair, 0)
    tiles.turn(5, 1, everything, None, halves)
    for side in halves:
        tiles.add(5, 1, side)


def early_attention(queries, pieces, rows):
    chunks, half, width = queries.shape
    held = pieces[0].shape[1]
    tile = held - rows
    step = 2
    state = jax.ShapeDtypeStruct((chunks * half, width), jnp.float32)
    size = step * half
    keys = len(EARLY) * tile
    return pl.pallas_call(
        functools.partial(early_kernel, rows, width ** (-0.5) * LOG2E),
        grid=(chunks // step,),
        out_shape=[state] * 3,
        in_specs=[pl.BlockSpec((step, half, width), lambda i: (i, 0, 0))] + hbm(len(EARLY)),
        out_specs=[pl.BlockSpec((size, width), lambda i: (i, 0))] * 3,
        scratch_shapes=[
            pltpu.VMEM((size, width), jnp.bfloat16),
            pltpu.VMEM((keys, width), jnp.bfloat16),
            pltpu.VMEM((keys, width), jnp.bfloat16),
            pltpu.VMEM((size, tile), jnp.bfloat16),
            pltpu.VMEM((size, tile), jnp.bfloat16),
            pltpu.SemaphoreType.DMA((len(EARLY), 2)),
        ],
        compiler_params=pltpu.CompilerParams(vmem_limit_bytes=24 * 1024 * 1024),
        cost_estimate=BRIEF,
        name="early_attention",
    )(queries, *[pieces[p] for p in EARLY])


def attention_kernel(waits, chunk, chunk_rows, rows, group, scale, me, own, beside, *refs):
    states, pieces = refs[:3], refs[3:11]
    out_ref = refs[11 + waits]
    queries, keys, values, even, odd, shift, sums, weighted, sems, late_sems = refs[12 + waits :]
    half = own.shape[1]
    held, width = pieces[0].shape[1:]
    tile = held - rows
    y = me[0] >> 2
    own_rows = (pl.multiple_of(y * half, half), half)
    beside_rows = (pl.multiple_of((1 - y) * half, half), half)
    low, high, everything = (0, half), (half, half), (0, 2 * half)
    order = EARLY + LATE

    def fresh_copies(p):
        at = pl.multiple_of(8 * tile + (me[0] ^ p) * rows, rows)
        return [
            pltpu.make_async_copy(
                pieces[p].at[j, pl.ds(0, rows)], target.at[pl.ds(at, rows)], sems.at[p, 2 + j]
            )
            for j, target in enumerate((keys, values))
        ]

    query_copies = [
        pltpu.make_async_copy(source.at[chunk], queries.at[pl.ds(*place)], late_sems.at[n])
        for n, (source, place) in enumerate(((own, own_rows), (beside, beside_rows)))
    ]
    state_copies = [
        pltpu.make_async_copy(
            source.at[pl.ds(chunk * half, half)], target.at[pl.ds(*own_rows)], late_sems.at[2 + n]
        )
        for n, (source, target) in enumerate(zip(states, (shift, sums, weighted)))
    ]
    copies = [prefix_copies(n, pieces[p], rows, keys, values, sems) for n, p in enumerate(order)]
    for copy in query_copies + copies[0] + state_copies:
        copy.start()
    for pair in copies[1:]:
        for copy in pair:
            copy.start()
    for p in range(8):
        for copy in fresh_copies(p):
            copy.start()

    def wait_for(n):
        for copy in prefix_copies(n, pieces[0], rows, keys, values, sems):
            copy.wait()

    tiles = Tiles(tile, scale, queries, keys, values, (even, odd), shift, sums, weighted)
    for copy in query_copies + copies[0]:
        copy.wait()
    tiles.first(beside_rows)

    def pair(u, carry):
        wait_for(2 * u + 1)
        tiles.turn(2 * u + 1, 1, beside_rows, None, [beside_rows])
        wait_for(2 * u + 2)
        tiles.turn(2 * u + 2, 0, beside_rows, None, [beside_rows])
        return carry

    lax.fori_loop(0, 2, pair, 0)
    wait_for(5)
    tiles.turn(5, 1, beside_rows, None, [beside_rows])
    wait_for(6)
    wait_for(7)
    for copy in state_copies:
        copy.wait()
    tiles.turn(6, 0, everything, None, [beside_rows])
    tiles.turn(7, 1, everything, None, [low, high])
    for p in range(8):
        for copy in fresh_copies(p):
            copy.wait()

    def latest(count):
        row = lax.broadcasted_iota(jnp.int32, (count, width), 0)
        last = (me[0] & 3) * rows + chunk * chunk_rows + row % chunk_rows
        return last if count == half else jnp.where(row < half, last, tile)

    tiles.turn(8, 0, everything, latest(2 * half), [low, high])
    tiles.turn(9, 1, high, latest(half), [low, high])
    tiles.add(9, 1, high)

    @pl.when(jnp.logical_not(jnp.max(sums[...]) < LARGEST))
    def _():
        weighted[...] = jnp.zeros(weighted.shape, jnp.float32)
        sums[...] = jnp.zeros(sums.shape, jnp.float32)

        def prefix_tile(t, carry):
            tiles.careful(t, everything, None)
            return carry

        lax.fori_loop(0, 8, prefix_tile, 0)
        tiles.careful(8, everything, latest(2 * half))
        tiles.careful(9, high, latest(half))

    for h in range(2):
        block = slice(h * half, (h + 1) * half)
        total = jnp.sum(sums[block], axis=1, keepdims=True)
        result = (weighted[block] / total).astype(jnp.bfloat16)
        for g in range(group):
            out_ref[y ^ h, :, g * width : (g + 1) * width] = result[
                g * chunk_rows : (g + 1) * chunk_rows
            ]


def chunk_attention(chunk, me, queries, states, pieces, rows, group, so_far, after):
    _, half, width = queries[0].shape
    chunk_rows = half // group
    held = pieces[0].shape[1]
    tile = held - rows
    aliases = {}
    if so_far is not None:
        aliases = {14 + len(after): 0}
        after = after + [so_far]
    return pl.pallas_call(
        functools.partial(
            attention_kernel,
            len(after),
            chunk,
            chunk_rows,
            rows,
            group,
            width ** (-0.5) * LOG2E,
        ),
        grid=(1,),
        out_shape=jax.ShapeDtypeStruct((2, GROUP * chunk_rows, group * width), jnp.bfloat16),
        in_specs=smem() + hbm(13) + anywhere(len(after)),
        out_specs=pl.BlockSpec((2, chunk_rows, group * width), lambda i: (0, chunk % GROUP, 0)),
        input_output_aliases=aliases,
        scratch_shapes=[
            pltpu.VMEM((2 * half, width), jnp.bfloat16),
            pltpu.VMEM((8 * held, width), jnp.bfloat16),
            pltpu.VMEM((8 * held, width), jnp.bfloat16),
            pltpu.VMEM((2 * half, tile), jnp.bfloat16),
            pltpu.VMEM((2 * half, tile), jnp.bfloat16),
            pltpu.VMEM((2 * half, width), jnp.float32),
            pltpu.VMEM((2 * half, width), jnp.float32),
            pltpu.VMEM((2 * half, width), jnp.float32),
            pltpu.SemaphoreType.DMA((8, 4)),
            pltpu.SemaphoreType.DMA((5,)),
        ],
        compiler_params=pltpu.CompilerParams(vmem_limit_bytes=24 * 1024 * 1024),
        cost_estimate=BRIEF,
        name="chunk_attention",
    )(me, *queries, *states, *pieces, *after)


def away_kernel(offset, here, across, beside, corner, *refs):
    send_ref = refs[-1]

    @pl.when(offset[0] % 2 == 0)
    def _():
        send_ref[0] = across[...]
        send_ref[1] = corner[...]

    @pl.when(offset[0] % 2 == 1)
    def _():
        send_ref[0] = here[...]
        send_ref[1] = beside[...]


def away(offset, parts, after):
    return pl.pallas_call(
        away_kernel,
        out_shape=jax.ShapeDtypeStruct((2, *parts[0].shape), jnp.bfloat16),
        in_specs=smem() + vmem(4) + anywhere(len(after)),
        out_specs=vmem()[0],
        cost_estimate=BRIEF,
        name="away",
    )(offset, *parts, *after)


def merge_kernel(offset, here, across, beside, corner, came, *refs):
    keep_ref, send_ref = refs[-2:]
    sides = ((here, across), (beside, corner))
    for low in range(2):
        for high in range(2):

            @pl.when(offset[0] == low + 2 * high)
            def _():
                for r, target in ((high, keep_ref), (1 - high, send_ref)):
                    total = sides[r][low][...].astype(jnp.float32) + came[r].astype(jnp.float32)
                    target[...] = total.astype(target.dtype)


def merge(offset, parts, came, after):
    return pl.pallas_call(
        merge_kernel,
        out_shape=[
            jax.ShapeDtypeStruct(parts[0].shape, jnp.float32),
            jax.ShapeDtypeStruct(parts[0].shape, jnp.bfloat16),
        ],
        in_specs=smem() + vmem(5) + anywhere(len(after)),
        out_specs=vmem(2),
        cost_estimate=BRIEF,
        name="merge",
    )(offset, *parts, came, *after)


def finish_kernel(me, keep, came, *refs):
    out_ref = refs[-1]
    columns = keep.shape[2]
    for half in range(2):
        at = pl.multiple_of(((me[0] & 1) ^ half) * columns, columns)
        total = keep[half] + came[half].astype(jnp.float32)
        out_ref[:, pl.ds(at, columns)] = total.astype(out_ref.dtype)


def finish(chunk, me, keep, came, so_far):
    _, rows, columns = keep.shape
    whole = pl.BlockSpec(keep.shape, lambda i: (0, 0, 0))
    operands = [me, keep, came]
    specs = smem() + [whole] * 2
    aliases = {}
    if so_far is not None:
        aliases = {len(operands): 0}
        operands.append(so_far)
        specs += anywhere()
    return pl.pallas_call(
        finish_kernel,
        grid=(1,),
        out_shape=jax.ShapeDtypeStruct((CHUNKS // GROUP * rows, 2 * columns), jnp.bfloat16),
        in_specs=specs,
        out_specs=pl.BlockSpec((rows, 2 * columns), lambda i: (chunk, 0)),
        input_output_aliases=aliases,
        cost_estimate=BRIEF,
        name="finish",
    )(*operands)


def decode_kernel(scale, me, q_ref, last_ref, *refs):
    pieces, out_ref = refs[:8], refs[8]
    q = q_ref[...]
    width = q.shape[1]
    low = me[0] < 4
    last = [jnp.where(low, last_ref[j, 0:1, :], last_ref[j, 1:2, :]) for j in range(2)]
    last = [value.astype(jnp.float32) for value in last]
    running = jnp.sum(q.astype(jnp.float32) * last[0], axis=1, keepdims=True)
    total = jnp.ones_like(running)
    weighted = jnp.broadcast_to(last[1], (q.shape[0], width))
    for piece in pieces:
        scores = jnp.concatenate(
            [
                jnp.dot(q, piece[0, at : at + BLK], preferred_element_type=jnp.float32)
                for at in range(0, piece.shape[1], BLK)
            ],
            axis=1,
        )
        highest = jnp.maximum(running, jnp.max(scores, axis=1, keepdims=True))
        weights = jnp.exp2((scores - highest) * scale)
        factor = jnp.exp2((running - highest) * scale)
        total = total * factor + jnp.sum(weights, axis=1, keepdims=True)
        weighted = weighted * factor + jnp.dot(
            weights.astype(jnp.bfloat16), piece[1], preferred_element_type=jnp.float32
        )
        running = highest
    out_ref[...] = (weighted / total).astype(jnp.bfloat16)


def decode(me, query, last, pieces, after):
    width = query.shape[1]
    held = pieces[0].shape[1]

    def kernel(me, q_ref, last_ref, *refs):
        decode_kernel(width ** (-0.5) * LOG2E, me, q_ref, last_ref, *refs[:8], refs[-1])

    return pl.pallas_call(
        kernel,
        out_shape=jax.ShapeDtypeStruct(query.shape, jnp.bfloat16),
        in_specs=smem() + vmem(10) + anywhere(len(after)),
        out_specs=vmem()[0],
        compiler_params=pltpu.CompilerParams(vmem_limit_bytes=32 * 1024 * 1024),
        cost_estimate=BRIEF,
        name="decode",
    )(me, query, last, *pieces, *after)


def pick_kernel(rows, me, member, remaining, *refs):
    pieces, (*outs, held, sems) = refs[:8], refs[-4:]
    count = member.shape[0]
    copies = []
    for p in range(8):
        at = pl.multiple_of((me[0] ^ p) * rows, rows)
        copies.append(
            pltpu.make_async_copy(
                pieces[p].at[:, pl.ds(0, rows)], held.at[:, pl.ds(at, rows)], sems.at[p]
            )
        )
        copies[p].start()
    for out in outs:
        out[...] = jnp.zeros(out.shape, out.dtype)
    for copy in copies:
        copy.wait()
    for b in range(count):
        target = member[b, 0]
        owner = remaining[target]
        spot = jnp.int32(0)
        for before in range(b):
            spot += (member[before, 0] == target).astype(jnp.int32)
        at = pl.multiple_of(spot * BLK, BLK)
        for out, instance in zip(outs, (me[0], me[0] ^ 4)):

            @pl.when(owner == instance)
            def _():
                out[0, pl.ds(at, BLK), :] = held[0, b * BLK : (b + 1) * BLK, :].T
                out[1, pl.ds(at, BLK), :] = held[1, b * BLK : (b + 1) * BLK, :]


def pick_blocks(me, member, remaining, pieces, rows, after):
    width = pieces[0].shape[2]
    shape = jax.ShapeDtypeStruct((2, CAP * BLK, width), jnp.bfloat16)
    return pl.pallas_call(
        functools.partial(pick_kernel, rows),
        out_shape=[shape, shape],
        in_specs=smem(3) + hbm(8) + anywhere(len(after)),
        out_specs=vmem(2),
        scratch_shapes=[
            pltpu.VMEM((2, 8 * rows, width), jnp.bfloat16),
            pltpu.SemaphoreType.DMA((8,)),
        ],
        compiler_params=pltpu.CompilerParams(vmem_limit_bytes=32 * 1024 * 1024),
        cost_estimate=BRIEF,
        name="pick_blocks",
    )(me, member, remaining, *pieces, *after)


def project_kernel(waits, slot, own, beside, across, corner, *refs):
    weights, outs = refs[:4], refs[4 + waits :]
    same = jnp.concatenate([own[0], own[1], across[0], across[1]], axis=0)
    other = jnp.concatenate([beside[1], beside[0], corner[1], corner[0]], axis=0)
    rows = own.shape[1]
    for half in range(2):
        total = jnp.dot(same, weights[2 * half][...], preferred_element_type=jnp.float32)
        total += jnp.dot(other, weights[2 * half + 1][...], preferred_element_type=jnp.float32)
        total = total.astype(jnp.bfloat16)
        for r in range(4):
            outs[r][half] = total[r * rows : (r + 1) * rows]


def project(slot, parts, own_weights, sibling_weights, after):
    _, rows, depth = parts[0].shape
    columns = own_weights.shape[1]
    tile = min(512, columns)
    whole = pl.BlockSpec((2, rows, depth), lambda j, slot: (0, 0, 0))
    same = pl.BlockSpec((depth, tile), lambda j, slot: (slot[0], j))
    other = pl.BlockSpec((depth, tile), lambda j, slot: (1 - slot[0], j))
    out = pl.BlockSpec((2, rows, tile), lambda j, slot: (0, 0, j))
    return pl.pallas_call(
        functools.partial(project_kernel, len(after)),
        grid_spec=pltpu.PrefetchScalarGridSpec(
            num_scalar_prefetch=1,
            grid=(columns // tile,),
            in_specs=[whole] * 4 + [same, other] * 2 + anywhere(len(after)),
            out_specs=[out] * 4,
        ),
        out_shape=[jax.ShapeDtypeStruct((2, rows, columns), jnp.bfloat16)] * 4,
        compiler_params=pltpu.CompilerParams(vmem_limit_bytes=26 * 1024 * 1024),
        cost_estimate=BRIEF,
        name="project",
    )(slot, *parts, own_weights, own_weights, sibling_weights, sibling_weights, *after)


def on_device_planes(
    fresh_segment_probes,
    fresh_segment_pairs,
    earlier_stored_pairs,
    emitted_token_probe,
    emitted_token_pair,
    final_projection_weights,
    remaining_instance_ids,
    segment_destination_member,
):
    index = lax.axis_index("inst")
    slot = index // 4
    rows, heads, width = fresh_segment_probes.shape
    group = heads // 2
    me = jnp.reshape(index, (1,)).astype(jnp.int32)
    slot_array = jnp.reshape(slot, (1,)).astype(jnp.int32)
    offset = jnp.reshape(lax.axis_index("tp") ^ (index // 2), (1,)).astype(jnp.int32)

    piece = {}
    to_beside = split_pairs(1, me, fresh_segment_pairs, earlier_stored_pairs, [])
    piece[4] = swapped(to_beside, "inst", 4)
    piece[0] = split_pairs(0, me, fresh_segment_pairs, earlier_stored_pairs, [to_beside])
    piece[2] = swapped(piece[0], "inst", 2)
    queries_own, queries_send = split_queries(me, fresh_segment_probes, [piece[0]])
    queries = [queries_own, swapped(queries_send, "inst", 4)]
    piece[6] = swapped(piece[4], "inst", 2)
    for d in (0, 4, 2, 6):
        piece[d + 1] = swapped(piece[d], "inst", 1)
    pieces = [piece[d] for d in range(8)]
    sibling_weights = swapped(final_projection_weights, "inst", 1)

    states = early_attention(queries_own, pieces, rows)

    def attention(k, after, between):
        own = None
        for chunk in range(k * GROUP, (k + 1) * GROUP):
            if between and chunk == (k + 1) * GROUP - 1:
                after = between(own)
            own = chunk_attention(
                chunk, me, queries, states, pieces, rows, group, own, after
            )
            after = []
        return [own] + [swapped(own, "inst", d) for d in (4, 2, 6)]

    def projected(parts, after):
        outs = project(slot_array, parts, final_projection_weights, sibling_weights, after)
        return [outs[0]] + [swapped(outs[i], "inst", d) for i, d in ((1, 4), (2, 2), (3, 6))]

    sums = {}

    def first_step(k, after):
        parts = [partial[k][0], partial[k][2], partial[k][1], partial[k][3]]
        send = away(offset, parts, after)
        sums[k] = (parts, swapped(send, "tp", 1))
        return send

    def second_step(k, after):
        keep, send = merge(offset, *sums[k], after)
        sums[k] = (keep, swapped(send, "tp", 2))
        return send

    gathered, partial = {}, {}
    groups = range(CHUNKS // GROUP)
    gathered[0] = attention(0, [], [])
    for k in groups[1:]:
        def between(own, k=k):
            partial[k - 1] = projected(gathered[k - 1], [own])
            return [partial[k - 1][0]]

        gathered[k] = attention(k, [gathered[k - 1][0]], between)
        if k >= 2:
            first_step(k - 2, [gathered[k][0]])
            second_step(k - 2, [partial[k - 1][0]])
    last = len(groups) - 1
    token = first_step(last - 1, [gathered[last][0]])
    partial[last] = projected(gathered[last], [token])
    token = second_step(last - 1, [partial[last][0]])
    token = first_step(last, [token])
    picked_own, picked_send = pick_blocks(
        me, segment_destination_member, remaining_instance_ids, pieces, rows, [token]
    )
    picked_beside = swapped(picked_send, "inst", 4)
    decoded = decode(me, emitted_token_probe, emitted_token_pair, pieces, [picked_own])
    second_step(last, [decoded])
    span_hidden = None
    for k in groups:
        span_hidden = finish(k, me, *sums[k], span_hidden)

    first = jnp.where(slot == 0, picked_own, picked_beside)
    second = jnp.where(slot == 0, picked_beside, picked_own)
    cache = jnp.stack([first, second]).transpose(2, 1, 0, 3)

    decoded_beside = swapped(decoded, "inst", 4)
    mine = (jnp.arange(heads) // group == slot)[:, None]
    decode_attention = jnp.where(mine, decoded, decoded_beside)
    return (span_hidden, cache[None], decode_attention)


def solution(mesh):
    instances, groups = mesh.shape["inst"], mesh.shape["tp"]

    def on_device(*arguments):
        slots_local = arguments[1].shape[2]
        tile = arguments[2].shape[0]
        rows = arguments[1].shape[0]
        if instances == 8 and groups == 4 and slots_local == 2 and tile == 4 * rows:
            return on_device_planes(*arguments)
        return on_device_ring(*arguments)

    return jax.shard_map(
        on_device,
        mesh=mesh,
        in_specs=(
            P("inst", "tp", None),
            P("inst", None, "tp", None),
            P("inst", None, "tp", None),
            P("tp", None),
            P(None, "tp", None),
            P("tp", "inst"),
            P(),
            P(),
        ),
        out_specs=(P("inst", "tp"), P("inst", None, None, "tp", None), P("tp", None)),
        check_vma=False,
    )
```

```python
import functools

import jax
import jax.numpy as jnp
from jax import lax
from jax.experimental import pallas as pl
from jax.experimental.pallas import tpu as pltpu
from jax.sharding import PartitionSpec as P

BLK = 128
CAP = 8
NEG_FILL = -1e30
LOG2E = 1.4426950408889634
LARGEST = 2.0**100
CHUNKS = 4
GROUP = 2


def from_behind(block, axis, distance):
    devices = range(lax.axis_size(axis))
    route = [((i - distance) % len(devices), i) for i in devices]
    return lax.ppermute(block, axis, route)


def combined_all(value, axis, combine):
    everything = jax.tree.map(lambda part: lax.all_gather(part, axis), value)
    initial = jax.tree.map(lambda part: part[0], everything)

    def turn(k, so_far):
        return combine(so_far, jax.tree.map(lambda part: part[k], everything))

    return lax.fori_loop(1, lax.axis_size(axis), turn, initial)


def attend(state, queries, key_value, visible):
    width = queries.shape[-1]
    scores = jnp.einsum(
        "rkgd,nkd->rkgn", queries, key_value[:, 0], preferred_element_type=jnp.float32
    ) * width ** (-0.5)
    if visible is not None:
        scores = jnp.where(visible[:, None, None, :], scores, NEG_FILL)
    running, total, weighted = state
    highest = jnp.maximum(running, jnp.max(scores, axis=-1))
    factor = jnp.exp(running - highest)
    weights = jnp.exp(scores - highest[..., None])
    total = total * factor + jnp.sum(weights, axis=-1)
    update = jnp.einsum(
        "rkgn,nkd->rkgd",
        weights.astype(jnp.bfloat16),
        key_value[:, 1],
        preferred_element_type=jnp.float32,
    )
    weighted = weighted * factor[..., None] + update
    return (highest, total, weighted)


def empty_state(rows, slots_local, group, width):
    return (
        jnp.full((rows, slots_local, group), -jnp.inf, jnp.float32),
        jnp.zeros((rows, slots_local, group), jnp.float32),
        jnp.zeros((rows, slots_local, group, width), jnp.float32),
    )


def combine(first, second):
    highest = jnp.maximum(first[0], second[0])
    left = jnp.exp(first[0] - highest)
    right = jnp.exp(second[0] - highest)
    return (
        highest,
        first[1] * left + second[1] * right,
        first[2] * left[..., None] + second[2] * right[..., None],
    )


def place_blocks(cache, rows_in, destination_members, slots, own_index):
    count = rows_in.shape[0] // BLK

    def put(index, current):
        spot = slots[index] * BLK
        incoming = lax.dynamic_slice_in_dim(rows_in, index * BLK, BLK, 0)
        present = lax.dynamic_slice_in_dim(current, spot, BLK, 0)
        chosen = jnp.where(destination_members[index] == own_index, incoming, present)
        return lax.dynamic_update_slice_in_dim(current, chosen, spot, 0)

    return lax.fori_loop(0, count, put, cache)


def destinations(segment_destination_member, remaining_instance_ids):
    sequence = segment_destination_member[:, 0]
    agreement = (
        sequence[:, None]
        == jnp.arange(remaining_instance_ids.shape[0], dtype=jnp.int32)[None, :]
    ).astype(jnp.int32)
    slots = jnp.sum(jnp.cumsum(agreement, axis=0) * agreement, axis=1) - 1
    members = jnp.sum(agreement * remaining_instance_ids[None, :], axis=1)
    return slots, members


def on_device_ring(
    fresh_segment_probes,
    fresh_segment_pairs,
    earlier_stored_pairs,
    emitted_token_probe,
    emitted_token_pair,
    final_projection_weights,
    remaining_instance_ids,
    segment_destination_member,
):
    own_index = lax.axis_index("inst")
    instances = lax.axis_size("inst")
    rows, heads, width = fresh_segment_probes.shape
    slots_local = fresh_segment_pairs.shape[2]
    group = heads // slots_local
    queries = fresh_segment_probes.reshape(rows, slots_local, group, width)
    slots, destination_members = destinations(segment_destination_member, remaining_instance_ids)
    held_blocks = jnp.sum((destination_members == own_index).astype(jnp.int32))
    cache = jnp.zeros((CAP * BLK, 2, slots_local, width), jnp.bfloat16)
    causal = jnp.arange(rows)[:, None] >= jnp.arange(rows)[None, :]
    state = attend(
        empty_state(rows, slots_local, group, width), queries, earlier_stored_pairs, None
    )
    state = attend(state, queries, fresh_segment_pairs, causal)
    moving = jnp.concatenate([fresh_segment_pairs, earlier_stored_pairs], axis=0)

    def turn_both(step, carry):
        moving, state, current = carry
        moving = from_behind(moving, "inst", 1)
        source = (own_index - step) % instances
        state = attend(state, queries, moving[rows:], None)
        visible = jnp.broadcast_to(source < own_index, (rows, rows))
        state = attend(state, queries, moving[:rows], visible)
        return (moving, state, current)

    moving, state, cache = lax.fori_loop(1, instances, turn_both, (moving, state, cache))
    cache = place_blocks(
        cache,
        lax.all_gather(fresh_segment_pairs, "inst", axis=0, tiled=True),
        destination_members,
        slots,
        own_index,
    )
    attention = (state[2] / state[1][..., None]).astype(jnp.bfloat16).reshape(rows, heads * width)
    terms = jnp.dot(
        attention,
        lax.all_gather(final_projection_weights, "inst", axis=1, tiled=True),
        preferred_element_type=jnp.float32,
    )
    span_hidden = lax.psum_scatter(
        terms.astype(jnp.bfloat16), "tp", scatter_dimension=1, tiled=True
    )
    single = emitted_token_probe.reshape(1, slots_local, group, width)
    decode_state = attend(
        empty_state(1, slots_local, group, width), single, earlier_stored_pairs, None
    )
    live = (jnp.arange(CAP * BLK) < held_blocks * BLK)[None, :]
    decode_state = attend(decode_state, single, cache, live)
    merged = combined_all((decode_state[0], decode_state[1], decode_state[2]), "inst", combine)
    own_scores = jnp.einsum(
        "rkgd,kd->rkg", single, emitted_token_pair[0], preferred_element_type=jnp.float32
    ) * width ** (-0.5)
    highest = jnp.maximum(merged[0], own_scores)
    left = jnp.exp(merged[0] - highest)
    right = jnp.exp(own_scores - highest)
    total = merged[1] * left + right
    own_weight = lax.optimization_barrier(right.astype(jnp.bfloat16)).astype(jnp.float32)
    own_value = emitted_token_pair[1].astype(jnp.float32)
    weighted = merged[2] * left[..., None] + own_weight[..., None] * own_value[None, :, None, :]
    decode_attention = (weighted / total[..., None]).astype(jnp.bfloat16).reshape(heads, width)
    return (span_hidden, cache[None], decode_attention)


def swapped(value, axis, distance):
    size = lax.axis_size(axis)
    return lax.ppermute(value, axis, [(i, i ^ distance) for i in range(size)])


def vmem(count=1):
    return [pl.BlockSpec(memory_space=pltpu.VMEM)] * count


def smem(count=1):
    return [pl.BlockSpec(memory_space=pltpu.SMEM)] * count


def hbm(count=1):
    return [pl.BlockSpec(memory_space=pltpu.HBM)] * count


def anywhere(count=1):
    return [pl.BlockSpec(memory_space=pl.ANY)] * count


def split_pairs_kernel(away, me, fresh, prefix, out):
    rows = fresh.shape[0]
    for y in range(2):

        @pl.when(me[0] >> 2 == y)
        def _():
            s = y ^ away
            for part, start in ((fresh, 0), (prefix, rows)):
                size = part.shape[0]
                out[1, start : start + size] = part[:, 1, s, :]
                for at in range(0, size, BLK):
                    block = part[at : at + BLK, 0, s, :]
                    out[0, start + at : start + at + BLK] = block.T


def split_pairs(away, me, fresh, prefix, after):
    def kernel(me, fresh, prefix, *refs):
        split_pairs_kernel(away, me, fresh, prefix, refs[-1])

    held, width = fresh.shape[0] + prefix.shape[0], fresh.shape[3]
    return pl.pallas_call(
        kernel,
        out_shape=jax.ShapeDtypeStruct((2, held, width), jnp.bfloat16),
        in_specs=smem() + vmem(2) + anywhere(len(after)),
        out_specs=vmem()[0],
        compiler_params=pltpu.CompilerParams(vmem_limit_bytes=24 * 1024 * 1024),
        name="split_pairs",
    )(me, fresh, prefix, *after)


def split_queries_kernel(group, me, queries, own_ref, send_ref):
    chunk_rows = queries.shape[0] // CHUNKS

    def place(out, s):
        for k in range(CHUNKS):
            for g in range(group):
                out[k, g * chunk_rows : (g + 1) * chunk_rows] = queries[
                    k * chunk_rows : (k + 1) * chunk_rows, s * group + g, :
                ]

    for y in range(2):

        @pl.when(me[0] >> 2 == y)
        def _():
            place(own_ref, y)
            place(send_ref, 1 - y)


def split_queries(me, queries, after):
    rows, heads, width = queries.shape
    group = heads // 2
    probes = jax.ShapeDtypeStruct((CHUNKS, group * rows // CHUNKS, width), jnp.bfloat16)

    def kernel(me, queries, *refs):
        split_queries_kernel(group, me, queries, *refs[-2:])

    return pl.pallas_call(
        kernel,
        out_shape=[probes, probes],
        in_specs=smem() + vmem() + anywhere(len(after)),
        out_specs=vmem(2),
        compiler_params=pltpu.CompilerParams(vmem_limit_bytes=24 * 1024 * 1024),
        name="split_queries",
    )(me, queries, *after)


EARLY = (0, 1, 4, 5, 2, 3)
LATE = (6, 7)


def prefix_copies(n, piece, rows, keys, values, sems):
    tile = piece.shape[1] - rows
    at = pl.multiple_of(n * tile, tile)
    return [
        pltpu.make_async_copy(
            piece.at[j, pl.ds(rows, tile)], target.at[pl.ds(at, tile)], sems.at[n, j]
        )
        for j, target in enumerate((keys, values))
    ]


class Tiles:
    def __init__(self, tile, scale, queries, keys, values, weights, shift, sums, weighted):
        self.tile, self.part, self.scale = tile, 2 * BLK, scale
        self.queries, self.keys, self.values = queries, keys, values
        self.weights, self.shift, self.sums, self.weighted = weights, shift, sums, weighted

    def scores(self, t, j, rows):
        at = pl.multiple_of(t * self.tile + j * self.part, self.part)
        block = jnp.concatenate(
            [self.keys[pl.ds(at + l, BLK), :] for l in range(0, self.part, BLK)], axis=1
        )
        return jnp.dot(self.queries[pl.ds(*rows)], block, preferred_element_type=jnp.float32)

    def above(self, t, j, rows, latest):
        width = self.shift.shape[1]
        value, shift = self.scores(t, j, rows), self.shift[pl.ds(*rows)]
        blocks = [value[:, l : l + width] - shift for l in range(0, self.part, width)]
        if latest is None:
            return blocks
        column = lax.broadcasted_iota(jnp.int32, blocks[0].shape, 1)
        return [
            jnp.where(column <= latest - (j * self.part + l * width), block, NEG_FILL)
            for l, block in enumerate(blocks)
        ]

    def weigh(self, t, slot, j, rows, latest):
        width = self.shift.shape[1]
        total = self.sums[pl.ds(*rows)]
        for l, block in enumerate(self.above(t, j, rows, latest)):
            weight = jnp.exp2(block * self.scale)
            total += weight
            at = j * self.part + l * width
            self.weights[slot][pl.ds(*rows), at : at + width] = weight.astype(jnp.bfloat16)
        self.sums[pl.ds(*rows)] = total

    def add(self, t, slot, rows):
        at = pl.multiple_of(t * self.tile, self.tile)
        self.weighted[pl.ds(*rows)] += jnp.dot(
            self.weights[slot][pl.ds(*rows)],
            self.values[pl.ds(at, self.tile), :],
            preferred_element_type=jnp.float32,
        )

    def peak(self, t, rows, latest=None, shifted=True):
        width = self.shift.shape[1]
        peak = None
        for j in range(self.tile // self.part):
            if shifted:
                blocks = self.above(t, j, rows, latest)
            else:
                value = self.scores(t, j, rows)
                blocks = [value[:, l : l + width] for l in range(0, self.part, width)]
            for block in blocks:
                peak = block if peak is None else jnp.maximum(peak, block)
        return jnp.max(peak, axis=1, keepdims=True)

    def first(self, rows):
        top = self.peak(0, rows, shifted=False)
        self.shift[pl.ds(*rows)] = jnp.broadcast_to(top, (rows[1], self.shift.shape[1]))
        for name in (self.sums, self.weighted):
            name[pl.ds(*rows)] = jnp.zeros((rows[1], name.shape[1]), jnp.float32)
        for j in range(self.tile // self.part):
            self.weigh(0, 0, j, rows, None)

    def turn(self, t, slot, rows, latest, before):
        parts = self.tile // self.part
        for j in range(parts):
            self.weigh(t, slot, j, rows, latest)
            for n, side in enumerate(before):
                if n * parts // len(before) == j:
                    self.add(t - 1, 1 - slot, side)

    def careful(self, t, rows, latest):
        up = jnp.maximum(self.peak(t, rows, latest), 0.0)
        factor = jnp.exp2(-up * self.scale)
        self.weighted[pl.ds(*rows)] *= factor
        self.sums[pl.ds(*rows)] *= factor
        self.shift[pl.ds(*rows)] += up
        for j in range(self.tile // self.part):
            self.weigh(t, 0, j, rows, latest)
        self.add(t, 0, rows)


def early_kernel(rows, scale, q_ref, *refs):
    pieces = refs[: len(EARLY)]
    shift, sums, weighted, queries, keys, values, even, odd, sems = refs[len(EARLY) :]
    count, half, _ = q_ref.shape
    tile = pieces[0].shape[1] - rows
    copies = [
        prefix_copies(n, piece, rows, keys, values, sems) for n, piece in enumerate(pieces)
    ]

    @pl.when(pl.program_id(0) == 0)
    def _():
        for pair in copies:
            for copy in pair:
                copy.start()

    for n in range(count):
        queries[n * half : (n + 1) * half] = q_ref[n]

    @pl.when(pl.program_id(0) == 0)
    def _():
        for pair in copies:
            for copy in pair:
                copy.wait()

    tiles = Tiles(tile, scale, queries, keys, values, (even, odd), shift, sums, weighted)
    everything = (0, count * half)
    halves = [(n * half, half) for n in range(count)]
    tiles.first(everything)

    def pair(u, carry):
        tiles.turn(2 * u + 1, 1, everything, None, halves)
        tiles.turn(2 * u + 2, 0, everything, None, halves)
        return carry

    lax.fori_loop(0, 2, pair, 0)
    tiles.turn(5, 1, everything, None, halves)
    for side in halves:
        tiles.add(5, 1, side)


def early_attention(queries, pieces, rows):
    chunks, half, width = queries.shape
    held = pieces[0].shape[1]
    tile = held - rows
    step = 2
    state = jax.ShapeDtypeStruct((chunks * half, width), jnp.float32)
    size = step * half
    keys = len(EARLY) * tile
    return pl.pallas_call(
        functools.partial(early_kernel, rows, width ** (-0.5) * LOG2E),
        grid=(chunks // step,),
        out_shape=[state] * 3,
        in_specs=[pl.BlockSpec((step, half, width), lambda i: (i, 0, 0))] + hbm(len(EARLY)),
        out_specs=[pl.BlockSpec((size, width), lambda i: (i, 0))] * 3,
        scratch_shapes=[
            pltpu.VMEM((size, width), jnp.bfloat16),
            pltpu.VMEM((keys, width), jnp.bfloat16),
            pltpu.VMEM((keys, width), jnp.bfloat16),
            pltpu.VMEM((size, tile), jnp.bfloat16),
            pltpu.VMEM((size, tile), jnp.bfloat16),
            pltpu.SemaphoreType.DMA((len(EARLY), 2)),
        ],
        compiler_params=pltpu.CompilerParams(vmem_limit_bytes=24 * 1024 * 1024),
        cost_estimate=pl.CostEstimate(
            flops=2 * 2 * chunks * half * keys * width * 2,
            bytes_accessed=keys * width * 4 + 3 * chunks * half * width * 4,
            transcendentals=chunks * half * keys,
        ),
        name="early_attention",
    )(queries, *[pieces[p] for p in EARLY])


def attention_kernel(waits, chunk, chunk_rows, rows, group, scale, me, own, beside, *refs):
    states, pieces = refs[:3], refs[3:11]
    out_ref = refs[11 + waits]
    queries, keys, values, even, odd, shift, sums, weighted, sems, late_sems = refs[12 + waits :]
    half = own.shape[1]
    held, width = pieces[0].shape[1:]
    tile = held - rows
    y = me[0] >> 2
    own_rows = (pl.multiple_of(y * half, half), half)
    beside_rows = (pl.multiple_of((1 - y) * half, half), half)
    low, high, everything = (0, half), (half, half), (0, 2 * half)
    order = EARLY + LATE

    def fresh_copies(p):
        at = pl.multiple_of(8 * tile + (me[0] ^ p) * rows, rows)
        return [
            pltpu.make_async_copy(
                pieces[p].at[j, pl.ds(0, rows)], target.at[pl.ds(at, rows)], sems.at[p, 2 + j]
            )
            for j, target in enumerate((keys, values))
        ]

    query_copies = [
        pltpu.make_async_copy(source.at[chunk], queries.at[pl.ds(*place)], late_sems.at[n])
        for n, (source, place) in enumerate(((own, own_rows), (beside, beside_rows)))
    ]
    state_copies = [
        pltpu.make_async_copy(
            source.at[pl.ds(chunk * half, half)], target.at[pl.ds(*own_rows)], late_sems.at[2 + n]
        )
        for n, (source, target) in enumerate(zip(states, (shift, sums, weighted)))
    ]
    copies = [prefix_copies(n, pieces[p], rows, keys, values, sems) for n, p in enumerate(order)]
    for copy in query_copies + copies[0] + state_copies:
        copy.start()
    for pair in copies[1:]:
        for copy in pair:
            copy.start()
    for p in range(8):
        for copy in fresh_copies(p):
            copy.start()

    def wait_for(n):
        for copy in prefix_copies(n, pieces[0], rows, keys, values, sems):
            copy.wait()

    tiles = Tiles(tile, scale, queries, keys, values, (even, odd), shift, sums, weighted)
    for copy in query_copies + copies[0]:
        copy.wait()
    tiles.first(beside_rows)

    def pair(u, carry):
        wait_for(2 * u + 1)
        tiles.turn(2 * u + 1, 1, beside_rows, None, [beside_rows])
        wait_for(2 * u + 2)
        tiles.turn(2 * u + 2, 0, beside_rows, None, [beside_rows])
        return carry

    lax.fori_loop(0, 2, pair, 0)
    wait_for(5)
    tiles.turn(5, 1, beside_rows, None, [beside_rows])
    wait_for(6)
    wait_for(7)
    for copy in state_copies:
        copy.wait()
    tiles.turn(6, 0, everything, None, [beside_rows])
    tiles.turn(7, 1, everything, None, [low, high])
    for p in range(8):
        for copy in fresh_copies(p):
            copy.wait()

    def latest(count):
        row = lax.broadcasted_iota(jnp.int32, (count, width), 0)
        last = (me[0] & 3) * rows + chunk * chunk_rows + row % chunk_rows
        return last if count == half else jnp.where(row < half, last, tile)

    tiles.turn(8, 0, everything, latest(2 * half), [low, high])
    tiles.turn(9, 1, high, latest(half), [low, high])
    tiles.add(9, 1, high)

    @pl.when(jnp.logical_not(jnp.max(sums[...]) < LARGEST))
    def _():
        weighted[...] = jnp.zeros(weighted.shape, jnp.float32)
        sums[...] = jnp.zeros(sums.shape, jnp.float32)

        def prefix_tile(t, carry):
            tiles.careful(t, everything, None)
            return carry

        lax.fori_loop(0, 8, prefix_tile, 0)
        tiles.careful(8, everything, latest(2 * half))
        tiles.careful(9, high, latest(half))

    for h in range(2):
        block = slice(h * half, (h + 1) * half)
        total = jnp.sum(sums[block], axis=1, keepdims=True)
        result = (weighted[block] / total).astype(jnp.bfloat16)
        for g in range(group):
            out_ref[y ^ h, :, g * width : (g + 1) * width] = result[
                g * chunk_rows : (g + 1) * chunk_rows
            ]


def chunk_attention(chunk, me, queries, states, pieces, rows, group, so_far, after):
    _, half, width = queries[0].shape
    chunk_rows = half // group
    held = pieces[0].shape[1]
    tile = held - rows
    aliases = {}
    if so_far is not None:
        aliases = {14 + len(after): 0}
        after = after + [so_far]
    return pl.pallas_call(
        functools.partial(
            attention_kernel,
            len(after),
            chunk,
            chunk_rows,
            rows,
            group,
            width ** (-0.5) * LOG2E,
        ),
        grid=(1,),
        out_shape=jax.ShapeDtypeStruct((2, GROUP * chunk_rows, group * width), jnp.bfloat16),
        in_specs=smem() + hbm(13) + anywhere(len(after)),
        out_specs=pl.BlockSpec((2, chunk_rows, group * width), lambda i: (0, chunk % GROUP, 0)),
        input_output_aliases=aliases,
        scratch_shapes=[
            pltpu.VMEM((2 * half, width), jnp.bfloat16),
            pltpu.VMEM((8 * held, width), jnp.bfloat16),
            pltpu.VMEM((8 * held, width), jnp.bfloat16),
            pltpu.VMEM((2 * half, tile), jnp.bfloat16),
            pltpu.VMEM((2 * half, tile), jnp.bfloat16),
            pltpu.VMEM((2 * half, width), jnp.float32),
            pltpu.VMEM((2 * half, width), jnp.float32),
            pltpu.VMEM((2 * half, width), jnp.float32),
            pltpu.SemaphoreType.DMA((8, 4)),
            pltpu.SemaphoreType.DMA((5,)),
        ],
        compiler_params=pltpu.CompilerParams(vmem_limit_bytes=24 * 1024 * 1024),
        cost_estimate=pl.CostEstimate(
            flops=2 * 2 * 2 * half * 8 * held * width * 2 * 2 // 3,
            bytes_accessed=8 * held * width * 4,
            transcendentals=2 * half * 8 * held * 2 // 3,
        ),
        name="chunk_attention",
    )(me, *queries, *states, *pieces, *after)


def stack_kernel(*refs):
    for r in range(4):
        refs[-1][r] = refs[r][...]


def stack(parts, after):
    return pl.pallas_call(
        stack_kernel,
        out_shape=jax.ShapeDtypeStruct((4, *parts[0].shape), jnp.bfloat16),
        in_specs=vmem(4) + anywhere(len(after)),
        out_specs=vmem()[0],
        compiler_params=pltpu.CompilerParams(vmem_limit_bytes=16 * 1024 * 1024),
        name="stack",
    )(*parts, *after)


def decode_kernel(scale, me, q_ref, last_ref, *refs):
    pieces, out_ref = refs[:8], refs[8]
    q = q_ref[...]
    width = q.shape[1]
    low = me[0] < 4
    last = [jnp.where(low, last_ref[j, 0:1, :], last_ref[j, 1:2, :]) for j in range(2)]
    last = [value.astype(jnp.float32) for value in last]
    running = jnp.sum(q.astype(jnp.float32) * last[0], axis=1, keepdims=True)
    total = jnp.ones_like(running)
    weighted = jnp.broadcast_to(last[1], (q.shape[0], width))
    for piece in pieces:
        scores = jnp.concatenate(
            [
                jnp.dot(q, piece[0, at : at + BLK], preferred_element_type=jnp.float32)
                for at in range(0, piece.shape[1], BLK)
            ],
            axis=1,
        )
        highest = jnp.maximum(running, jnp.max(scores, axis=1, keepdims=True))
        weights = jnp.exp2((scores - highest) * scale)
        factor = jnp.exp2((running - highest) * scale)
        total = total * factor + jnp.sum(weights, axis=1, keepdims=True)
        weighted = weighted * factor + jnp.dot(
            weights.astype(jnp.bfloat16), piece[1], preferred_element_type=jnp.float32
        )
        running = highest
    out_ref[...] = (weighted / total).astype(jnp.bfloat16)


def decode(me, query, last, pieces, after):
    width = query.shape[1]
    held = pieces[0].shape[1]

    def kernel(me, q_ref, last_ref, *refs):
        decode_kernel(width ** (-0.5) * LOG2E, me, q_ref, last_ref, *refs[:8], refs[-1])

    return pl.pallas_call(
        kernel,
        out_shape=jax.ShapeDtypeStruct(query.shape, jnp.bfloat16),
        in_specs=smem() + vmem(10) + anywhere(len(after)),
        out_specs=vmem()[0],
        compiler_params=pltpu.CompilerParams(vmem_limit_bytes=32 * 1024 * 1024),
        cost_estimate=pl.CostEstimate(
            flops=4 * query.shape[0] * width * 8 * held,
            bytes_accessed=8 * held * width * 4,
            transcendentals=query.shape[0] * 8 * held,
        ),
        name="decode",
    )(me, query, last, *pieces, *after)


def pick_kernel(rows, me, member, remaining, *refs):
    pieces, (*outs, held, sems) = refs[:8], refs[-4:]
    count = member.shape[0]
    copies = []
    for p in range(8):
        at = pl.multiple_of((me[0] ^ p) * rows, rows)
        copies.append(
            pltpu.make_async_copy(
                pieces[p].at[:, pl.ds(0, rows)], held.at[:, pl.ds(at, rows)], sems.at[p]
            )
        )
        copies[p].start()
    for out in outs:
        out[...] = jnp.zeros(out.shape, out.dtype)
    for copy in copies:
        copy.wait()
    for b in range(count):
        target = member[b, 0]
        owner = remaining[target]
        spot = jnp.int32(0)
        for before in range(b):
            spot += (member[before, 0] == target).astype(jnp.int32)
        at = pl.multiple_of(spot * BLK, BLK)
        for out, instance in zip(outs, (me[0], me[0] ^ 4)):

            @pl.when(owner == instance)
            def _():
                out[0, pl.ds(at, BLK), :] = held[0, b * BLK : (b + 1) * BLK, :].T
                out[1, pl.ds(at, BLK), :] = held[1, b * BLK : (b + 1) * BLK, :]


def pick_blocks(me, member, remaining, pieces, rows, after):
    width = pieces[0].shape[2]
    shape = jax.ShapeDtypeStruct((2, CAP * BLK, width), jnp.bfloat16)
    return pl.pallas_call(
        functools.partial(pick_kernel, rows),
        out_shape=[shape, shape],
        in_specs=smem(3) + hbm(8) + anywhere(len(after)),
        out_specs=vmem(2),
        scratch_shapes=[
            pltpu.VMEM((2, 8 * rows, width), jnp.bfloat16),
            pltpu.SemaphoreType.DMA((8,)),
        ],
        compiler_params=pltpu.CompilerParams(vmem_limit_bytes=32 * 1024 * 1024),
        name="pick_blocks",
    )(me, member, remaining, *pieces, *after)


def project_kernel(waits, slot, own, beside, across, corner, *refs):
    weights, outs = refs[:4], refs[4 + waits :]
    same = jnp.concatenate([own[0], own[1], across[0], across[1]], axis=0)
    other = jnp.concatenate([beside[1], beside[0], corner[1], corner[0]], axis=0)
    rows = own.shape[1]
    for half in range(2):
        total = jnp.dot(same, weights[2 * half][...], preferred_element_type=jnp.float32)
        total += jnp.dot(other, weights[2 * half + 1][...], preferred_element_type=jnp.float32)
        total = total.astype(jnp.bfloat16)
        for r in range(4):
            outs[r][half] = total[r * rows : (r + 1) * rows]


def project(slot, parts, own_weights, sibling_weights, after):
    _, rows, depth = parts[0].shape
    columns = own_weights.shape[1]
    tile = min(512, columns)
    whole = pl.BlockSpec((2, rows, depth), lambda j, slot: (0, 0, 0))
    same = pl.BlockSpec((depth, tile), lambda j, slot: (slot[0], j))
    other = pl.BlockSpec((depth, tile), lambda j, slot: (1 - slot[0], j))
    out = pl.BlockSpec((2, rows, tile), lambda j, slot: (0, 0, j))
    return pl.pallas_call(
        functools.partial(project_kernel, len(after)),
        grid_spec=pltpu.PrefetchScalarGridSpec(
            num_scalar_prefetch=1,
            grid=(columns // tile,),
            in_specs=[whole] * 4 + [same, other] * 2 + anywhere(len(after)),
            out_specs=[out] * 4,
        ),
        out_shape=[jax.ShapeDtypeStruct((2, rows, columns), jnp.bfloat16)] * 4,
        compiler_params=pltpu.CompilerParams(vmem_limit_bytes=26 * 1024 * 1024),
        cost_estimate=pl.CostEstimate(
            flops=2 * 4 * rows * 2 * depth * 2 * columns,
            bytes_accessed=2 * depth * 2 * columns * 2,
            transcendentals=0,
        ),
        name="project",
    )(slot, *parts, own_weights, own_weights, sibling_weights, sibling_weights, *after)


def on_device_planes(
    fresh_segment_probes,
    fresh_segment_pairs,
    earlier_stored_pairs,
    emitted_token_probe,
    emitted_token_pair,
    final_projection_weights,
    remaining_instance_ids,
    segment_destination_member,
):
    index = lax.axis_index("inst")
    slot = index // 4
    rows, heads, width = fresh_segment_probes.shape
    group = heads // 2
    me = jnp.reshape(index, (1,)).astype(jnp.int32)
    slot_array = jnp.reshape(slot, (1,)).astype(jnp.int32)
    core = index % 2

    piece = {}
    to_beside = split_pairs(1, me, fresh_segment_pairs, earlier_stored_pairs, [])
    piece[4] = swapped(to_beside, "inst", 4)
    piece[0] = split_pairs(0, me, fresh_segment_pairs, earlier_stored_pairs, [to_beside])
    piece[2] = swapped(piece[0], "inst", 2)
    queries_own, queries_send = split_queries(me, fresh_segment_probes, [piece[0]])
    queries = [queries_own, swapped(queries_send, "inst", 4)]
    piece[6] = swapped(piece[4], "inst", 2)
    for d in (0, 4, 2, 6):
        piece[d + 1] = swapped(piece[d], "inst", 1)
    pieces = [piece[d] for d in range(8)]
    sibling_weights = swapped(final_projection_weights, "inst", 1)

    states = early_attention(queries_own, pieces, rows)

    def attention(k, after, between):
        own = None
        for chunk in range(k * GROUP, (k + 1) * GROUP):
            if between and chunk == (k + 1) * GROUP - 1:
                after = between(own)
            own = chunk_attention(
                chunk, me, queries, states, pieces, rows, group, own, after
            )
            after = []
        return [own] + [swapped(own, "inst", d) for d in (4, 2, 6)]

    def projected(parts, after):
        outs = project(slot_array, parts, final_projection_weights, sibling_weights, after)
        return [outs[0]] + [swapped(outs[i], "inst", d) for i, d in ((1, 4), (2, 2), (3, 6))]

    planes = lax.axis_size("tp")
    lines = [
        [i * planes + (r ^ (i // 2)) for r in range(planes)] for i in range(lax.axis_size("inst"))
    ]
    reduced = {}

    def reduce_group(k, after):
        here, beside, across, corner = partial[k]
        ordered = stack([here, across, beside, corner], after)
        total = lax.psum_scatter(ordered, ("inst", "tp"), axis_index_groups=lines)
        left = jnp.where(core == 0, total[0], total[1])
        right = jnp.where(core == 0, total[1], total[0])
        reduced[k] = jnp.concatenate([left, right], axis=1)
        return ordered

    gathered, partial = {}, {}
    groups = range(CHUNKS // GROUP)
    gathered[0] = attention(0, [], [])
    for k in groups[1:]:
        def between(own, k=k):
            partial[k - 1] = projected(gathered[k - 1], [own])
            return [partial[k - 1][0]]

        gathered[k] = attention(k, [gathered[k - 1][0]], between)
        if k >= 2:
            reduce_group(k - 2, [gathered[k][0]])
    last = len(groups) - 1
    token = reduce_group(last - 1, [gathered[last][0]])
    partial[last] = projected(gathered[last], [token])
    token = reduce_group(last, [])
    picked_own, picked_send = pick_blocks(
        me, segment_destination_member, remaining_instance_ids, pieces, rows, [token]
    )
    picked_beside = swapped(picked_send, "inst", 4)
    decoded = decode(me, emitted_token_probe, emitted_token_pair, pieces, [picked_own])
    span_hidden = jnp.concatenate([reduced[k] for k in groups], axis=0)

    first = jnp.where(slot == 0, picked_own, picked_beside)
    second = jnp.where(slot == 0, picked_beside, picked_own)
    cache = jnp.stack([first, second]).transpose(2, 1, 0, 3)

    decoded_beside = swapped(decoded, "inst", 4)
    mine = (jnp.arange(heads) // group == slot)[:, None]
    decode_attention = jnp.where(mine, decoded, decoded_beside)
    return (span_hidden, cache[None], decode_attention)


def solution(mesh):
    instances, groups = mesh.shape["inst"], mesh.shape["tp"]

    def on_device(*arguments):
        slots_local = arguments[1].shape[2]
        tile = arguments[2].shape[0]
        rows = arguments[1].shape[0]
        if instances == 8 and groups == 4 and slots_local == 2 and tile == 4 * rows:
            return on_device_planes(*arguments)
        return on_device_ring(*arguments)

    return jax.shard_map(
        on_device,
        mesh=mesh,
        in_specs=(
            P("inst", "tp", None),
            P("inst", None, "tp", None),
            P("inst", None, "tp", None),
            P("tp", None),
            P(None, "tp", None),
            P("tp", "inst"),
            P(),
            P(),
        ),
        out_specs=(P("inst", "tp"), P("inst", None, None, "tp", None), P("tp", None)),
        check_vma=False,
    )
```
